32 devices in a mesh: scale: 2 (over y), dp: 16 (over z, x, core).
Axes of the slice: x: 2, y: 2, z: 4, core: 2. Of those that a mesh axis runs over, the one named last changes fastest.
Arguments:
- tokens: bfloat16 [147456, 128], P(('scale', 'dp')), may hold values from -6 to 6
- cotangent: bfloat16 [147456, 128], P(('scale', 'dp')), may hold values from -6 to 6
- item_mask: int32 [2, 384], P('scale'), may hold values 0 or 1
- ln_gain: float32 [2, 128], replicated, may hold values from 0.5 to 1.5
- ln_bias: float32 [2, 128], replicated, may hold values from -3 to 3
- season_in: bfloat16 [2, 84, 96], replicated, may hold values from -0.875 to 0.875
- season_out: bfloat16 [2, 84, 48], replicated, may hold values from -1.25 to 1.25
- trend_in: bfloat16 [2, 168, 48], replicated, may hold values from -1.25 to 1.25
- trend_out: bfloat16 [2, 168, 96], replicated, may hold values from -0.875 to 0.875
- ffn_in: bfloat16 [2, 128, 256], replicated, may hold values from -0.5 to 0.5
- ffn_bias: float32 [2, 256], replicated, may hold values from -3 to 3
- ffn_out: bfloat16 [2, 256, 128], replicated, may hold values from -0.5 to 0.5
Outputs:
- mixed_out: bfloat16 [147456, 128], P(('scale', 'dp'))
- input_grad: bfloat16 [147456, 128], P(('scale', 'dp'))
- gain_grad: float32 [2, 128], replicated
- bias_grad: float32 [2, 128], replicated
- season_in_grad: float32 [2, 84, 96], replicated
- season_out_grad: float32 [2, 84, 48], replicated
- trend_in_grad: float32 [2, 168, 48], replicated
- trend_out_grad: float32 [2, 168, 96], replicated
- ffn_in_grad: float32 [2, 128, 256], replicated
- ffn_bias_grad: float32 [2, 256], replicated
- ffn_out_grad: float32 [2, 256, 128], replicated
The draws below stay inside these ranges and needn't reach their ends.
All inputs are finite; a program needn't handle non-finite values. No bound on the sum of `item_mask` on one device may be relied on, other than what follows from the above.
Results may differ from the reference program's by a relative error of at most 0.017.
Values may be sent and summed in bfloat16 or wider, within the bound.
A program may use at most 192 MiB of HBM per device.

```python
import jax
import jax.numpy as jnp
from jax import lax

D = 128
FF = 256
L0 = 96
KERNEL = 25
NL = 2
ITEM_DEV = 48
TOK_DEV = 4608
ITEMS_ROW = 384
ROWS = 147456
SEASON_ROWS = 84
TREND_ROWS = 168
HALF_L = 48
N_SCALE = 2
N_DP = 16


def set_ends(drawn, stream_key, low, largest):
    place = [jax.random.randint(jax.random.fold_in(stream_key, axis), (), 0, length) for axis, length in enumerate(drawn.shape)]
    longest = drawn.shape.index(max(drawn.shape))
    next_to = place[:longest] + [(place[longest] + 1) % drawn.shape[longest]] + place[longest + 1:]
    return drawn.at[tuple(place)].set(low).at[tuple(next_to)].set(largest)


def shard_levels(stream_key, shape, cuts, least, high):
    def one(position, parts):
        heights = jax.random.uniform(jax.random.fold_in(jax.random.fold_in(stream_key, 6), position), (parts,), jnp.float32, least / len(cuts), high / len(cuts))
        return jnp.repeat(jnp.exp(heights), shape[position] // parts).reshape((-1,) + (1,) * (len(shape) - position - 1))

    factor_of = one(*cuts[0])
    for cut in cuts[1:]:
        factor_of = factor_of * one(*cut)
    return factor_of


def normal_values(key, dims, width, limit, cuts=(), kind=jnp.bfloat16):
    array = jax.random.normal(key, dims, jnp.float32) * width
    if len(cuts) > 0:
        array = shard_levels(key, dims, cuts, -0.22, 0.18) * array
    return jnp.clip(array, min=-limit, max=limit).astype(kind)


def setup_inputs(seed: int = 0) -> dict:
    seeds = jax.random.split(jax.random.key(seed), 13)
    tokens = normal_values(seeds[0], (ROWS, D), 1.0, 6.0, ((0, 32),))
    cotangent = normal_values(seeds[1], (ROWS, D), 1.0, 6.0, ((0, 32),))
    item_mask = set_ends((jax.random.randint(seeds[2], (N_SCALE, ITEMS_ROW), 0, 4) < 3).astype(jnp.int32), jax.random.fold_in(seeds[2], 1), 0, 1)
    ln_gain = jnp.clip(1.0 + 0.1 * jax.random.normal(seeds[3], (NL, D), jnp.float32), 0.5, 1.5)
    ln_bias = normal_values(seeds[4], (NL, D), 0.5, 3.0, (), jnp.float32)
    season_in = normal_values(seeds[5], (NL, SEASON_ROWS, L0), (L0 // 2) ** -0.5, 0.875)
    season_out = normal_values(seeds[6], (NL, SEASON_ROWS, HALF_L), (L0 // 4) ** -0.5, 1.25)
    trend_in = normal_values(seeds[7], (NL, TREND_ROWS, HALF_L), (L0 // 4) ** -0.5, 1.25)
    trend_out = normal_values(seeds[8], (NL, TREND_ROWS, L0), (L0 // 2) ** -0.5, 0.875)
    ffn_in = normal_values(seeds[9], (NL, D, FF), D ** -0.5, 0.5)
    ffn_bias = normal_values(seeds[10], (NL, FF), 0.5, 3.0, (), jnp.float32)
    ffn_out = normal_values(seeds[11], (NL, FF, D), (FF // 2) ** -0.5, 0.5)
    return {"tokens": tokens, "cotangent": cotangent, "item_mask": item_mask, "ln_gain": ln_gain, "ln_bias": ln_bias, "season_in": season_in, "season_out": season_out, "trend_in": trend_in, "trend_out": trend_out, "ffn_in": ffn_in, "ffn_bias": ffn_bias, "ffn_out": ffn_out}


EPS = 1e-05
HIGHEST = lax.Precision.HIGHEST

@jax.custom_vjp
def low(v):
    return lax.optimization_barrier(v.astype(jnp.bfloat16)).astype(jnp.float32)

@jax.custom_vjp
def low_back(v):
    return v

def low_keep(v):
    return (low(v), None)

def low_pass(kept, grad):
    return (grad,)

def back_keep(v):
    return (v, None)

def back_low(kept, grad):
    return (low(grad),)
low.defvjp(low_keep, low_pass)
low_back.defvjp(back_keep, back_low)

def moving_matrix(length):
    half_width = (KERNEL - 1) // 2
    shifts = jnp.arange(-half_width, half_width + 1, dtype=jnp.int32)[:, None, None]
    row_place = jnp.arange(length, dtype=jnp.int32)[None, :, None]
    column_place = jnp.arange(length, dtype=jnp.int32)[None, None, :]
    matches = (jnp.clip(row_place + shifts, 0, length - 1) == column_place).astype(jnp.float32)
    return lax.optimization_barrier(jnp.sum(matches, 0)) / KERNEL

def norm_forward(rows_in, gain_row, offset_row):
    mean_row = lax.optimization_barrier(jnp.mean(rows_in, -1, keepdims=True))
    centered = rows_in - mean_row
    inverse = lax.rsqrt(lax.optimization_barrier(jnp.mean(centered * centered, -1, keepdims=True)) + EPS)
    return centered * inverse * gain_row + offset_row

def mix(first_weight, second_weight, source):
    rounded = low(low_back(source))
    inner_act = low_back(jnp.einsum('ts,bsd->btd', first_weight, rounded, precision=HIGHEST))
    hidden = low(jax.nn.gelu(inner_act, approximate=False))
    return low(low_back(jnp.einsum('ts,bsd->btd', second_weight, hidden, precision=HIGHEST)))

def layer_forward(params, levels, live_items):
    gain_row, offset_row, season_first, season_second, trend_first, trend_second, weight_in, bias_in, weight_out = params
    seasons = []
    trends = []
    for level_index in range(4):
        length = L0 >> level_index
        normed = norm_forward(levels[level_index], gain_row, offset_row)
        trend_rows = jnp.einsum('tu,bud->btd', moving_matrix(length), normed, precision=HIGHEST)
        seasons.append(normed - trend_rows)
        trends.append(trend_rows)
    for coarse in (1, 2, 3):
        length_out = L0 >> coarse
        length_in = L0 >> coarse - 1
        row_start = L0 - length_in
        seasons[coarse] = seasons[coarse] + mix(season_first[row_start:row_start + length_out, :length_in], season_second[row_start:row_start + length_out, :length_out], seasons[coarse - 1])
    for coarse in (3, 2, 1):
        length_out = L0 >> coarse - 1
        length_in = L0 >> coarse
        row_start = 2 * L0 - 2 * length_out
        trends[coarse - 1] = trends[coarse - 1] + mix(trend_first[row_start:row_start + length_out, :length_in], trend_second[row_start:row_start + length_out, :length_out], trends[coarse])
    outputs = []
    for level_index in range(4):
        mixed_in = low(seasons[level_index] + trends[level_index])
        inner_act = low_back(jnp.einsum('bld,df->blf', mixed_in, weight_in, precision=HIGHEST) + bias_in)
        hidden = low(jax.nn.gelu(inner_act, approximate=False))
        branch = low_back(jnp.einsum('blf,fd->bld', hidden, weight_out, precision=HIGHEST))
        outputs.append(levels[level_index] + live_items[:, None, None] * branch)
    return tuple(outputs)

def split_rows(buffer):
    groups = N_DP
    level_zero = buffer[:groups // 2].reshape(groups // 2 * ITEM_DEV, L0, D)
    level_one = buffer[groups // 2:3 * groups // 4].reshape(groups // 4, 2, ITEM_DEV, L0 // 2, D)
    level_one = jnp.transpose(level_one, (1, 0, 2, 3, 4)).reshape(groups // 2 * ITEM_DEV, L0 // 2, D)
    parts_two = buffer[3 * groups // 4:7 * groups // 8].reshape(groups // 8, 4, ITEM_DEV, L0 // 4, D)
    level_two = jnp.stack([parts_two[:, 0], parts_two[:, 2], parts_two[:, 1], parts_two[:, 3]], 0)
    level_two = level_two.reshape(groups // 2 * ITEM_DEV, L0 // 4, D)
    parts_three = buffer[7 * groups // 8:, :TOK_DEV // 2].reshape(groups // 8, 4, ITEM_DEV, L0 // 8, D)
    level_three = jnp.stack([parts_three[:, 0], parts_three[:, 2], parts_three[:, 1], parts_three[:, 3]], 0)
    level_three = level_three.reshape(groups // 2 * ITEM_DEV, L0 // 8, D)
    return (level_zero, level_one, level_two, level_three)

def merge_rows(levels, padding):
    groups = N_DP
    level_zero = levels[0].reshape(groups // 2, TOK_DEV, D)
    level_one = jnp.transpose(levels[1].reshape(2, groups // 4, ITEM_DEV, L0 // 2, D), (1, 0, 2, 3, 4))
    level_one = level_one.reshape(groups // 4, TOK_DEV, D)
    parts_two = levels[2].reshape(4, groups // 8, ITEM_DEV, L0 // 4, D)
    level_two = jnp.stack([parts_two[0], parts_two[2], parts_two[1], parts_two[3]], 1).reshape(groups // 8, TOK_DEV, D)
    parts_three = levels[3].reshape(4, groups // 8, ITEM_DEV, L0 // 8, D)
    level_three = jnp.stack([parts_three[0], parts_three[2], parts_three[1], parts_three[3]], 1)
    level_three = level_three.reshape(groups // 8, TOK_DEV // 2, D)
    level_three = jnp.concatenate([level_three, padding[7 * groups // 8:, TOK_DEV // 2:]], 1)
    return jnp.concatenate([level_zero, level_one, level_two, level_three], 0)

def reference(tokens, cotangent, item_mask, ln_gain, ln_bias, season_in, season_out, trend_in, trend_out, ffn_in, ffn_bias, ffn_out):
    weights = tuple((member.astype(jnp.float32) for member in (ln_gain, ln_bias, season_in, season_out, trend_in, trend_out, ffn_in, ffn_bias, ffn_out)))

    def per_block(totals, inputs):
        level_inputs, level_cotangents, live_items = inputs

        def full_forward(params, levels):
            for layer_index in range(NL):
                levels = layer_forward(tuple((member[layer_index] for member in params)), levels, live_items)
            return levels
        outputs, pullback = jax.vjp(full_forward, weights, tuple(level_inputs))
        grad_params, grad_levels = pullback(tuple(level_cotangents))
        totals = tuple((total + grad for total, grad in zip(totals, grad_params)))
        return (totals, (outputs, grad_levels))

    def per_row(totals, inputs):
        row_tokens, row_cotangent, row_mask = inputs
        level_inputs = split_rows(row_tokens.astype(jnp.float32))
        level_cotangents = split_rows(row_cotangent.astype(jnp.float32))
        blocks_in = tuple((member.reshape(N_DP // 2, ITEM_DEV, L0 >> level_index, D) for level_index, member in enumerate(level_inputs)))
        blocks_cot = tuple((member.reshape(N_DP // 2, ITEM_DEV, L0 >> level_index, D) for level_index, member in enumerate(level_cotangents)))
        live_items = row_mask.astype(jnp.float32).reshape(N_DP // 2, ITEM_DEV)
        totals, (outputs, grads) = lax.scan(per_block, totals, (blocks_in, blocks_cot, live_items))
        outputs = tuple((member.reshape(-1, L0 >> level_index, D) for level_index, member in enumerate(outputs)))
        grads = tuple((member.reshape(-1, L0 >> level_index, D) for level_index, member in enumerate(grads)))
        merged_out = merge_rows(outputs, row_tokens.astype(jnp.float32)).astype(jnp.bfloat16)
        merged_grad = merge_rows(grads, row_cotangent.astype(jnp.float32)).astype(jnp.bfloat16)
        return (totals, (merged_out, merged_grad))
    zeros = tuple((jnp.zeros_like(member) for member in weights))
    totals, (outs_all, grads_all) = lax.scan(per_row, zeros, (tokens.reshape(N_SCALE, N_DP, TOK_DEV, D), cotangent.reshape(N_SCALE, N_DP, TOK_DEV, D), item_mask))
    return (outs_all.reshape(ROWS, D), grads_all.reshape(ROWS, D), totals[0], totals[1], totals[2], totals[3], totals[4], totals[5], totals[6], totals[7], totals[8])
```

```python
import functools

import jax
import jax.numpy as jnp
from jax import lax
from jax.experimental import pallas as pl
from jax.experimental.pallas import tpu as pltpu
from jax.sharding import PartitionSpec as P

L0 = 96
KERNEL = 25
NL = 2
SEASON_ROWS = 84
TREND_ROWS = 168
EPS = 1e-05
LANES = 128
ITEMS = 8
PAIR = 4
MESH = pl.DeviceIdType.MESH
F32 = jnp.float32
BF16 = jnp.bfloat16

LENGTHS = [L0 >> i for i in range(4)]
SIZES = [ITEMS * n for n in LENGTHS]
STARTS = [sum(SIZES[:i]) for i in range(4)]
CHUNK = sum(SIZES)
SLOTS = [1, 2, 4, 4]
SELF = [(0, 0), (0, 1), (1, 1), (3, 1)]
TILE = 480

AT_SMALL, AT_SEASON_IN, AT_TREND_IN, AT_TREND_OUT = 0, 8, 96, 264
AT_FFN_IN, AT_FFN_OUT, LAYER_ROWS = 432, 688, 944
SEASON_OUT_LANE = 48


def dot(a, b):
    return jnp.dot(a, b, preferred_element_type=F32)


def dot_nt(a, b):
    return lax.dot_general(a, b, (((1,), (1,)), ((), ())), preferred_element_type=F32)


def dot_tn(a, b):
    return lax.dot_general(a, b, (((0,), (0,)), ((), ())), preferred_element_type=F32)


def dot_exact(a, b):
    return jnp.dot(a, b, preferred_element_type=F32, precision=lax.Precision.HIGHEST)


def gelu_parts(v):
    cumulative = 0.5 * (1.0 + lax.erf(v * 0.7071067811865476))
    density = jnp.exp(-0.5 * (v * v)) * 0.3989422804014327
    return v * cumulative, cumulative + v * density


def iota(shape, dim):
    return lax.broadcasted_iota(jnp.int32, shape, dim)


def selection(rows, columns, count, length, base, turned=False):
    shape = (columns, rows) if turned else (rows, columns)
    r = iota(shape, 1 if turned else 0)
    c = iota(shape, 0 if turned else 1)
    found = jnp.zeros(shape, jnp.bool_)
    for k in range(count):
        found = found | ((c == r - (k * length - base)) & (r >= k * length) & (r < (k + 1) * length))
    return found.astype(F32)


def block_mask(count, height, width, turned=False):
    shape = (count * width, count * height) if turned else (count * height, count * width)
    r = iota(shape, 1 if turned else 0)
    c = iota(shape, 0 if turned else 1)
    found = jnp.zeros(shape, jnp.bool_)
    for k in range(count):
        found = found | (
            (r >= k * height) & (r < (k + 1) * height) & (c >= k * width) & (c < (k + 1) * width)
        )
    return found.astype(F32)


def moving_counts(count, length, turned):
    size = count * length
    t = iota((size, size), 1 if turned else 0)
    u = iota((size, size), 0 if turned else 1)
    total = jnp.zeros((size, size), F32)
    half = (KERNEL - 1) // 2
    for k in range(count):
        low, high = k * length, (k + 1) * length - 1
        inside = (t >= low) & (t <= high) & (u >= low) & (u <= high)
        near = (jnp.abs(t - u) <= half).astype(F32)
        first = jnp.where(u == low, jnp.maximum(half - (t - low), 0), 0).astype(F32)
        last = jnp.where(u == high, jnp.maximum(half - (high - t), 0), 0).astype(F32)
        total = total + jnp.where(inside, near + first + last, 0.0)
    return total


def pair_of(ref, start, half, height):
    return jnp.concatenate(
        [ref[start : start + height, :], ref[start + half : start + half + height, :]], 1
    )


def fold_rows(value):
    return jnp.sum(value.reshape(-1, 8, value.shape[-1]), 0)


class Names:
    pass


def group_of(groups, scale, slot, position):
    bounds = [0, groups // 2, 3 * groups // 4, 7 * groups // 8]
    offsets = [0, groups // 4, groups // 8, 3 * groups // 8]
    return position - bounds[scale] + offsets[slot]


def home_of(groups, scale, group):
    if scale == 0:
        return group, 0
    if scale == 1:
        return groups // 2 + lax.rem(group, groups // 4), lax.div(group, groups // 4)
    part = lax.div(group, groups // 8)
    slot = jnp.where(part == 1, 2, jnp.where(part == 2, 1, part))
    first = 3 * groups // 4 if scale == 2 else 7 * groups // 8
    return first + lax.rem(group, groups // 8), slot


def kernel_body(
    groups,
    n_scale,
    per_device,
    pack_rows,
    tokens,
    cotangent,
    item_mask,
    ln_gain,
    ln_bias,
    season_in,
    season_out,
    trend_in,
    trend_out,
    ffn_in,
    ffn_bias,
    ffn_out,
    mixed_out,
    input_grad,
    packed_out,
    tok_buf,
    cot_buf,
    out_buf,
    grad_buf,
    live,
    field,
    grad,
    dz,
    unit,
    inverse,
    z_keep,
    hidden,
    slope,
    season_src,
    trend_src,
    season_hid,
    season_slope,
    trend_hid,
    trend_slope,
    sa,
    sb,
    ta,
    tb,
    sa_t,
    sb_t,
    ta_t,
    tb_t,
    moving,
    moving_t,
    moving3,
    moving3_t,
    win_t,
    wout_t,
    d_sa,
    d_sb,
    d_ta,
    d_tb,
    d_win,
    d_wout,
    d_bias,
    d_gain,
    d_off,
    pack,
    half_in,
    half_bf,
    plane_in,
    plane_bf,
    depth_in,
    in_send,
    in_recv,
    out_send,
    out_recv,
    pad_sem,
    ar_send,
    ar_recv,
):
    scale_index = lax.axis_index("scale")
    position = lax.axis_index("dp")
    worker_group = lax.rem(position, groups // 2)
    worker_half = lax.div(position, groups // 2)
    half_items = per_device // 2
    chunks = half_items // ITEMS
    bounds = [0, groups // 2, 3 * groups // 4, 7 * groups // 8, groups]

    barrier = pltpu.get_barrier_semaphore()

    def greet(k, carry):
        other = lax.rem(scale_index * groups + position + k, n_scale * groups)
        pl.semaphore_signal(
            barrier,
            inc=1,
            device_id=(lax.div(other, groups), lax.rem(other, groups)),
            device_id_type=MESH,
        )
        return carry

    lax.fori_loop(1, n_scale * groups, greet, 0)
    pl.semaphore_wait(barrier, n_scale * groups - 1)

    def inbound(kind, scale, slot, half, chunk):
        source = (tokens, cotangent)[kind]
        target = (tok_buf, cot_buf)[kind]
        length, size = LENGTHS[scale], SIZES[scale]
        first = (slot * per_device + half * half_items + chunk * ITEMS) * length
        src = source.at[pl.ds(pl.multiple_of(first, 16), size)]
        dst = target.at[chunk, pl.ds(STARTS[scale], size)]
        recv = in_recv.at[kind, chunk, scale]
        if (slot, half) == SELF[scale]:
            return pltpu.make_async_copy(src, dst, recv), False
        owner = half * (groups // 2) + group_of(groups, scale, slot, position)
        return (
            pltpu.make_async_remote_copy(
                src_ref=src,
                dst_ref=dst,
                send_sem=in_send.at[kind, chunk, slot * 2 + half],
                recv_sem=recv,
                device_id=(scale_index, owner),
                device_id_type=MESH,
            ),
            True,
        )

    def each_inbound(act):
        for scale in range(4):

            @pl.when((position >= bounds[scale]) & (position < bounds[scale + 1]))
            def _():
                def one_chunk(chunk, carry):
                    for kind in range(2):
                        for slot in range(SLOTS[scale]):
                            for half in (1, 0):
                                act(*inbound(kind, scale, slot, half, chunk))
                    return carry

                lax.fori_loop(0, chunks, one_chunk, 0)

    each_inbound(lambda copy, remote: copy.start())

    def inbound_wait(kind, chunk):
        target = (tok_buf, cot_buf)[kind]
        for scale in range(4):
            ref = target.at[chunk, pl.ds(STARTS[scale], SIZES[scale])]
            pltpu.make_async_copy(ref, ref, in_recv.at[kind, chunk, scale]).wait()

    pad_rows = SLOTS[3] * per_device * LENGTHS[3]

    def pad_copies():
        return [
            pltpu.make_async_copy(
                source.at[pl.ds(pad_rows, pad_rows)], target.at[pl.ds(pad_rows, pad_rows)], pad_sem.at[k]
            )
            for k, (source, target) in enumerate(((tokens, mixed_out), (cotangent, input_grad)))
        ]

    @pl.when(position >= bounds[3])
    def _():
        for copy in pad_copies():
            copy.start()

    def outbound(kind, scale, chunk):
        source = (out_buf, grad_buf)[kind]
        target = (mixed_out, input_grad)[kind]
        home, slot = home_of(groups, scale, worker_group)
        length, size = LENGTHS[scale], SIZES[scale]
        first = (slot * per_device + worker_half * half_items + chunk * ITEMS) * length
        src = source.at[chunk, pl.ds(STARTS[scale], size)]
        dst = target.at[pl.ds(pl.multiple_of(first, 16), size)]
        recv = out_recv.at[kind, chunk, slot * 2 + worker_half]
        local = pltpu.make_async_copy(src, dst, recv)
        remote = pltpu.make_async_remote_copy(
            src_ref=src,
            dst_ref=dst,
            send_sem=out_send.at[kind, chunk, scale],
            recv_sem=recv,
            device_id=(scale_index, home),
            device_id_type=MESH,
        )
        return home, local, remote

    def outbound_start(kind, chunk):
        for scale in range(4):
            home, local, remote = outbound(kind, scale, chunk)

            @pl.when(home == position)
            def _():
                local.start()

            @pl.when(home != position)
            def _():
                remote.start()

    for layer in range(NL):
        for c in (1, 2, 3):
            count = 1 << (c - 1)
            fine, coarse = LENGTHS[c - 1], LENGTHS[c]
            at_season = L0 - fine
            at_trend = 2 * L0 - 2 * fine
            for source, normal, turned, height, width, base in (
                (season_in, sa, sa_t, coarse, fine, at_season),
                (season_out, sb, sb_t, coarse, coarse, at_season),
                (trend_in, ta, ta_t, fine, coarse, at_trend),
                (trend_out, tb, tb_t, fine, fine, at_trend),
            ):
                whole = source[layer]
                rows = selection(count * height, whole.shape[0], count, height, base).astype(BF16)
                columns = selection(count * width, whole.shape[1], count, width, 0).astype(BF16)
                tall = dot(rows, whole).astype(BF16)
                normal[layer, c - 1] = (
                    dot_nt(tall, columns) * block_mask(count, height, width)
                ).astype(BF16)
                turned[layer, c - 1] = (
                    dot_nt(columns, tall) * block_mask(count, height, width, True)
                ).astype(BF16)
        eye_in = selection(ffn_in.shape[2], ffn_in.shape[2], 1, ffn_in.shape[2], 0).astype(BF16)
        eye_out = selection(LANES, LANES, 1, LANES, 0).astype(BF16)
        win_t[layer] = dot_nt(eye_in, ffn_in[layer]).astype(BF16)
        wout_t[layer] = dot_nt(eye_out, ffn_out[layer]).astype(BF16)
    for i in range(3):
        moving[i] = moving_counts(1 << i, LENGTHS[i], False).astype(BF16)
        moving_t[i] = moving_counts(1 << i, LENGTHS[i], True).astype(BF16)
    moving3[...] = moving_counts(PAIR, LENGTHS[3], False).astype(BF16)
    moving3_t[...] = moving_counts(PAIR, LENGTHS[3], True).astype(BF16)

    mask_rows = jnp.broadcast_to(item_mask[...].astype(F32), (LANES, item_mask.shape[1])).astype(BF16)
    first_item = worker_group * per_device + worker_half * half_items
    chosen = iota((32, item_mask.shape[1]), 1) == iota((32, item_mask.shape[1]), 0) + first_item
    item_live = dot_nt(chosen.astype(F32).astype(BF16), mask_rows).astype(BF16)
    for chunk in range(chunks):
        for i in range(4):
            place = (iota((SIZES[i], 32), 0).astype(F32) + 0.5) * (1.0 / LENGTHS[i])
            column = iota((SIZES[i], 32), 1).astype(F32) - float(chunk * ITEMS)
            one = ((place >= column) & (place < column + 1.0)).astype(F32).astype(BF16)
            live[chunk, STARTS[i] : STARTS[i] + SIZES[i], :] = dot(one, item_live)

    for total in (d_sa, d_sb, d_ta, d_tb, d_win, d_wout, d_bias, d_gain, d_off, pack):
        total[...] = jnp.zeros(total.shape, F32)

    taps = 1.0 / KERNEL
    slabs = [(0, 96, 4), (1, 96, 2), (2, 96, 1), (3, 48, 1)]

    def count_matrix(scale, turned):
        if scale == 3:
            return (moving3_t if turned else moving3)[...]
        return (moving_t if turned else moving)[scale]

    def forward(layer, carry):
        gain = ln_gain[pl.ds(layer, 1), :]
        offset = ln_bias[pl.ds(layer, 1), :]
        offset_pair = jnp.concatenate([offset, offset], 1)
        scaled = [[], [], [], []]
        season_part = [[], [], [], []]
        trend_part = [[], [], [], []]
        for scale, height, number in slabs:
            half = SIZES[scale] // 2
            for j in range(number):
                parts = []
                for side in range(2):
                    start = STARTS[scale] + side * half + j * height
                    x = field[start : start + height, :]
                    mean = jnp.mean(x, -1, keepdims=True)
                    centered = x - mean
                    inv = lax.rsqrt(jnp.mean(centered * centered, -1, keepdims=True) + EPS)
                    n = centered * inv
                    unit[layer, start : start + height, :] = n
                    inverse[layer, start : start + height, :] = jnp.broadcast_to(inv, n.shape)
                    parts.append(n * gain)
                both = jnp.concatenate(parts, 1)
                average = dot(count_matrix(scale, False), both.astype(BF16)) * taps
                scaled[scale].append(both + offset_pair)
                season_part[scale].append(both - average)
                trend_part[scale].append(average + offset_pair)

        season_mixed = [None, [], [], []]
        unit_number = 0
        sources = season_part[0]
        for c in (1, 2, 3):
            halves = []
            for j in range(PAIR >> (c - 1)):
                a = sources[j].astype(BF16)
                season_src[layer, unit_number] = a
                h, s = gelu_parts(dot(sa[layer, c - 1], a))
                h = h.astype(BF16)
                season_hid[layer, unit_number] = h
                season_slope[layer, unit_number] = s.astype(BF16)
                halves.append(dot(sb[layer, c - 1], h))
                unit_number += 1
            if c < 3:
                season_mixed[c] = [
                    jnp.concatenate(halves[2 * j : 2 * j + 2], 0) for j in range(len(halves) // 2)
                ]
            else:
                season_mixed[c] = halves
            sources = [e + m for e, m in zip(season_part[c], season_mixed[c])]

        trend_mixed = [[], [], [], None]
        sources = trend_part[3]
        for c in (3, 2, 1):
            base = {1: 0, 2: 4, 3: 6}[c]
            for j in range(PAIR >> (c - 1)):
                a = sources[j].astype(BF16)
                trend_src[layer, base + j] = a
                h, s = gelu_parts(dot(ta[layer, c - 1], a))
                h = h.astype(BF16)
                trend_hid[layer, base + j] = h
                trend_slope[layer, base + j] = s.astype(BF16)
                trend_mixed[c - 1].append(dot(tb[layer, c - 1], h))
            if c > 1:
                wide = [r + m for r, m in zip(trend_part[c - 1], trend_mixed[c - 1])]
                sources = []
                for value in wide:
                    sources.append(value[:48])
                    sources.append(value[48:])

        for scale, height, number in slabs:
            half = SIZES[scale] // 2
            for j in range(number):
                value = scaled[scale][j]
                if season_mixed[scale] is not None:
                    value = value + season_mixed[scale][j]
                if trend_mixed[scale] is not None:
                    value = value + trend_mixed[scale][j]
                value = value.astype(BF16)
                for side in range(2):
                    start = STARTS[scale] + side * half + j * height
                    z_keep[layer, start : start + height, :] = value[:, side * LANES : (side + 1) * LANES]
        return carry

    def ffn_forward(layer, live_chunk):
        bias = ffn_bias[pl.ds(layer, 1), :]
        for t in range(0, CHUNK, TILE):
            a = dot(z_keep[layer, t : t + TILE, :], ffn_in[layer]) + bias
            h, s = gelu_parts(a)
            h = h.astype(BF16)
            hidden[layer, t : t + TILE, :] = h
            slope[layer, t : t + TILE, :] = s.astype(BF16)
            f = dot(h, ffn_out[layer])
            field[t : t + TILE, :] = field[t : t + TILE, :] + live_chunk[t : t + TILE, :] * f

    def backward(layer, live_chunk):
        for t in range(0, CHUNK, TILE):
            df = (live_chunk[t : t + TILE, :] * grad[t : t + TILE, :]).astype(BF16)
            da = (dot(df, wout_t[layer]) * slope[layer, t : t + TILE, :].astype(F32)).astype(BF16)
            dz[t : t + TILE, :] = dot(da, win_t[layer])
            d_win[layer] += dot_tn(z_keep[layer, t : t + TILE, :], da)
            d_wout[layer] += dot_tn(df, hidden[layer, t : t + TILE, :])
            d_bias[layer] += fold_rows(da.astype(F32))

        def slab_of(scale, height, j):
            return pair_of(dz, STARTS[scale] + j * height, SIZES[scale] // 2, height)

        gathered = [[slab_of(scale, height, j) for j in range(number)] for scale, height, number in slabs]

        trend_grad = [None, [], [], []]
        incoming = gathered[0]
        for c in (1, 2, 3):
            base = {1: 0, 2: 4, 3: 6}[c]
            sum_b = sum_a = None
            for j in range(PAIR >> (c - 1)):
                g = incoming[j].astype(BF16)
                part_b = dot_nt(g, trend_hid[layer, base + j])
                dp = (dot(tb_t[layer, c - 1], g) * trend_slope[layer, base + j].astype(F32)).astype(BF16)
                part_a = dot_nt(dp, trend_src[layer, base + j])
                sum_b = part_b if sum_b is None else sum_b + part_b
                sum_a = part_a if sum_a is None else sum_a + part_a
                trend_grad[c].append(dot(ta_t[layer, c - 1], dp))
            d_tb[layer, c - 1] += sum_b
            d_ta[layer, c - 1] += sum_a
            if c < 3:
                trend_grad[c] = [
                    jnp.concatenate(trend_grad[c][2 * j : 2 * j + 2], 0)
                    for j in range(len(trend_grad[c]) // 2)
                ]
                incoming = [z + g for z, g in zip(gathered[c], trend_grad[c])]

        season_grad = [[], [], [], None]
        incoming = gathered[3]
        for c in (3, 2, 1):
            base = {1: 0, 2: 4, 3: 6}[c]
            sum_b = sum_a = None
            for j in range(PAIR >> (c - 1)):
                g = incoming[j].astype(BF16)
                part_b = dot_nt(g, season_hid[layer, base + j])
                dp = (dot(sb_t[layer, c - 1], g) * season_slope[layer, base + j].astype(F32)).astype(BF16)
                part_a = dot_nt(dp, season_src[layer, base + j])
                sum_b = part_b if sum_b is None else sum_b + part_b
                sum_a = part_a if sum_a is None else sum_a + part_a
                season_grad[c - 1].append(dot(sa_t[layer, c - 1], dp))
            d_sb[layer, c - 1] += sum_b
            d_sa[layer, c - 1] += sum_a
            if c > 1:
                wide = [z + g for z, g in zip(gathered[c - 1], season_grad[c - 1])]
                incoming = []
                for value in wide:
                    incoming.append(value[:48])
                    incoming.append(value[48:])

        gain = ln_gain[pl.ds(layer, 1), :]
        sum_gain = jnp.zeros((8, LANES), F32)
        sum_off = jnp.zeros((8, LANES), F32)
        for scale, height, number in slabs:
            half = SIZES[scale] // 2
            for j in range(number):
                value = gathered[scale][j]
                if scale == 0:
                    moved = -season_grad[0][j]
                    value = value + season_grad[0][j]
                elif scale == 3:
                    moved = trend_grad[3][j]
                else:
                    moved = trend_grad[scale][j] - season_grad[scale][j]
                    value = value + season_grad[scale][j]
                value = value + dot(count_matrix(scale, True), moved.astype(BF16)) * taps
                for side in range(2):
                    start = STARTS[scale] + side * half + j * height
                    d = value[:, side * LANES : (side + 1) * LANES]
                    n = unit[layer, start : start + height, :]
                    sum_gain = sum_gain + fold_rows(d * n)
                    sum_off = sum_off + fold_rows(d)
                    q = d * gain
                    mean_q = jnp.mean(q, -1, keepdims=True)
                    mean_qn = jnp.mean(q * n, -1, keepdims=True)
                    grad[start : start + height, :] = grad[start : start + height, :] + inverse[
                        layer, start : start + height, :
                    ] * (q - mean_q - n * mean_qn)
        d_gain[layer] += sum_gain
        d_off[layer] += sum_off

    def one_chunk(chunk, carry):
        inbound_wait(0, chunk)
        field[...] = tok_buf[chunk].astype(F32)

        def one_forward(layer, inner):
            forward(layer, 0)
            ffn_forward(layer, live.at[chunk])
            return inner

        lax.fori_loop(0, NL, one_forward, 0)
        out_buf[chunk] = field[...].astype(BF16)
        outbound_start(0, chunk)
        inbound_wait(1, chunk)
        grad[...] = cot_buf[chunk].astype(F32)

        def one_backward(step, inner):
            backward(NL - 1 - step, live.at[chunk])
            return inner

        lax.fori_loop(0, NL, one_backward, 0)
        grad_buf[chunk] = grad[...].astype(BF16)
        outbound_start(1, chunk)
        return carry

    lax.fori_loop(0, chunks, one_chunk, 0)

    for layer in range(NL):
        at = layer * LAYER_ROWS
        season_in_sum = season_out_sum = trend_in_sum = trend_out_sum = None
        for c in (1, 2, 3):
            count = 1 << (c - 1)
            fine, coarse = LENGTHS[c - 1], LENGTHS[c]
            at_season = L0 - fine
            at_trend = 2 * L0 - 2 * fine
            found = []
            for value, rows, height, width, base, lane in (
                (d_sa, 88, coarse, fine, at_season, 0),
                (d_sb, 88, coarse, coarse, at_season, SEASON_OUT_LANE),
                (d_ta, TREND_ROWS, fine, coarse, at_trend, 0),
                (d_tb, TREND_ROWS, fine, fine, at_trend, 0),
            ):
                masked = value[layer, c - 1] * block_mask(count, height, width)
                tall = dot_exact(selection(count * height, rows, count, height, base, True), masked)
                found.append(dot_exact(tall, selection(count * width, LANES, count, width, lane)))
            if season_in_sum is None:
                season_in_sum, season_out_sum, trend_in_sum, trend_out_sum = found
            else:
                season_in_sum += found[0]
                season_out_sum += found[1]
                trend_in_sum += found[2]
                trend_out_sum += found[3]
        pack[at : at + 1, :] = jnp.sum(d_gain[layer], 0, keepdims=True)
        pack[at + 1 : at + 2, :] = jnp.sum(d_off[layer], 0, keepdims=True)
        bias_sum = jnp.sum(d_bias[layer], 0, keepdims=True)
        pack[at + 2 : at + 3, :] = bias_sum[:, :LANES]
        pack[at + 3 : at + 4, :] = bias_sum[:, LANES:]
        pack[at + AT_SEASON_IN : at + AT_SEASON_IN + 88, :] = season_in_sum
        pack[at + AT_TREND_IN : at + AT_TREND_IN + 88, :] = trend_in_sum[:88] + season_out_sum
        pack[at + AT_TREND_IN + 88 : at + AT_TREND_IN + TREND_ROWS, :] = trend_in_sum[88:]
        pack[at + AT_TREND_OUT : at + AT_TREND_OUT + TREND_ROWS, :] = trend_out_sum
        for side in range(2):
            lanes = slice(side * LANES, (side + 1) * LANES)
            row = at + AT_FFN_IN + side * LANES
            pack[row : row + LANES, :] = d_win[layer, :, lanes]
            row = at + AT_FFN_OUT + side * LANES
            pack[row : row + LANES, :] = d_wout[layer, :, lanes]

    plane_dp = groups // 8
    plane_size = plane_dp * n_scale
    core = lax.rem(position, 2)
    place_dp = lax.rem(lax.div(position, 2), plane_dp)
    depth_index = lax.div(position, 2 * plane_dp)
    plane_index = scale_index * plane_dp + place_dp
    half_rows = pack_rows // 2
    plane_rows = half_rows // plane_size
    depth_rows = plane_rows // 4

    def core_id():
        return (scale_index, position + 1 - 2 * core)

    def plane_id(index):
        return (
            lax.div(index, plane_dp),
            depth_index * (2 * plane_dp) + lax.rem(index, plane_dp) * 2 + core,
        )

    def depth_id(index):
        return (scale_index, index * (2 * plane_dp) + place_dp * 2 + core)

    def remote(src, dst, stage, slot_out, slot_in, device):
        return pltpu.make_async_remote_copy(
            src_ref=src,
            dst_ref=dst,
            send_sem=ar_send.at[stage, slot_out],
            recv_sem=ar_recv.at[stage, slot_in],
            device_id=device,
            device_id_type=MESH,
        )

    def arrived(ref, stage, slot):
        pltpu.make_async_copy(ref, ref, ar_recv.at[stage, slot]).wait()

    mine = pl.multiple_of(core * half_rows, 16)
    theirs = pl.multiple_of((1 - core) * half_rows, 16)
    first_copy = remote(pack.at[pl.ds(theirs, half_rows)], half_in, 0, 0, 0, core_id())
    first_copy.start()
    first_copy.wait_send()
    arrived(half_in, 0, 0)
    half_bf[pl.ds(mine, half_rows)] = (pack[pl.ds(mine, half_rows)] + half_in[...]).astype(BF16)

    def plane_piece(index):
        return pl.ds(pl.multiple_of(mine + index * plane_rows, 16), plane_rows)

    def plane_round(stage, source_of, target_of, act):
        def one(k, carry):
            other = lax.rem(plane_index + k, plane_size)
            back = lax.rem(plane_index + plane_size - k, plane_size)
            act(other, back, k)
            return carry

        lax.fori_loop(1, plane_size, one, 0)

    def plane_scatter(other, back, k):
        remote(half_bf.at[plane_piece(other)], plane_in.at[k], 1, k, k, plane_id(other)).start()

    plane_round(1, None, None, plane_scatter)
    plane_sum = pack[plane_piece(plane_index)] + half_in[
        pl.ds(pl.multiple_of(plane_index * plane_rows, 16), plane_rows)
    ]

    def plane_wait(k, carry):
        remote(half_bf.at[plane_piece(0)], plane_in.at[k], 1, k, k, core_id()).wait_send()
        arrived(plane_in.at[k], 1, k)
        return carry

    lax.fori_loop(1, plane_size, plane_wait, 0)
    for k in range(1, plane_size):
        plane_sum = plane_sum + plane_in[k].astype(F32)
    plane_bf[...] = plane_sum.astype(BF16)

    def depth_piece(index):
        return pl.ds(pl.multiple_of(index * depth_rows, 16), depth_rows)

    for k in range(1, 4):
        other = lax.rem(depth_index + k, 4)
        remote(plane_bf.at[depth_piece(other)], depth_in.at[k], 2, k, k, depth_id(other)).start()
    for k in range(1, 4):
        remote(plane_bf.at[depth_piece(0)], depth_in.at[k], 2, k, k, core_id()).wait_send()
        arrived(depth_in.at[k], 2, k)
    total = plane_bf[depth_piece(depth_index)].astype(F32)
    for k in range(1, 4):
        total = total + depth_in[k].astype(F32)

    def final_piece(plane, depth):
        return pl.ds(pl.multiple_of(mine + plane * plane_rows + depth * depth_rows, 16), depth_rows)

    own = final_piece(plane_index, depth_index)
    packed_out[own] = total.astype(BF16)
    for k in range(1, 4):
        other = lax.rem(depth_index + k, 4)
        remote(packed_out.at[own], packed_out.at[own], 3, k, k, depth_id(other)).start()
    for k in range(1, 4):
        back = lax.rem(depth_index + 4 - k, 4)
        remote(packed_out.at[own], packed_out.at[own], 3, k, k, core_id()).wait_send()
        arrived(packed_out.at[final_piece(plane_index, back)], 3, k)
    own_plane = plane_piece(plane_index)

    def plane_gather(other, back, k):
        remote(packed_out.at[own_plane], packed_out.at[own_plane], 4, k, k, plane_id(other)).start()

    plane_round(4, None, None, plane_gather)

    def plane_gathered(other, back, k):
        remote(packed_out.at[own_plane], packed_out.at[own_plane], 4, k, k, core_id()).wait_send()
        arrived(packed_out.at[plane_piece(back)], 4, k)

    plane_round(4, None, None, plane_gathered)
    own_half = pl.ds(mine, half_rows)
    last_copy = remote(packed_out.at[own_half], packed_out.at[own_half], 5, 0, 0, core_id())
    last_copy.start()
    last_copy.wait_send()
    arrived(packed_out.at[pl.ds(theirs, half_rows)], 5, 0)

    def sent(copy, remote_copy):
        if remote_copy:
            copy.wait_send()

    each_inbound(sent)

    def finish(chunk, carry):
        for kind in range(2):
            for scale in range(4):
                home, local, remote_copy = outbound(kind, scale, chunk)

                @pl.when(home != position)
                def _():
                    remote_copy.wait_send()

            for scale in range(4):

                @pl.when((position >= bounds[scale]) & (position < bounds[scale + 1]))
                def _():
                    for slot in range(SLOTS[scale]):
                        for half in range(2):
                            first = (slot * per_device + half * half_items + chunk * ITEMS) * LENGTHS[scale]
                            ref = (mixed_out, input_grad)[kind].at[
                                pl.ds(pl.multiple_of(first, 16), SIZES[scale])
                            ]
                            pltpu.make_async_copy(ref, ref, out_recv.at[kind, chunk, slot * 2 + half]).wait()

        return carry

    lax.fori_loop(0, chunks, finish, 0)

    @pl.when(position >= bounds[3])
    def _():
        for copy in pad_copies():
            copy.wait()


def body(groups, n_scale, *args):
    tokens = args[0]
    hidden = args[9].shape[2]
    per_device = tokens.shape[0] // L0
    chunks = per_device // 2 // ITEMS
    devices = groups * n_scale
    unit_rows = 16 * devices
    pack_rows = -(-NL * LAYER_ROWS // unit_rows) * unit_rows
    plane_size = groups // 8 * n_scale
    plane_rows = pack_rows // 2 // plane_size
    anywhere = pl.BlockSpec(memory_space=pl.ANY)
    vmem = pl.BlockSpec(memory_space=pltpu.VMEM)
    dma = pltpu.SemaphoreType.DMA
    scratch = [
        pltpu.VMEM((chunks, CHUNK, LANES), BF16),
        pltpu.VMEM((chunks, CHUNK, LANES), BF16),
        pltpu.VMEM((chunks, CHUNK, LANES), BF16),
        pltpu.VMEM((chunks, CHUNK, LANES), BF16),
        pltpu.VMEM((chunks, CHUNK, LANES), F32),
        pltpu.VMEM((CHUNK, LANES), F32),
        pltpu.VMEM((CHUNK, LANES), F32),
        pltpu.VMEM((CHUNK, LANES), F32),
        pltpu.VMEM((NL, CHUNK, LANES), F32),
        pltpu.VMEM((NL, CHUNK, LANES), F32),
        pltpu.VMEM((NL, CHUNK, LANES), BF16),
        pltpu.VMEM((NL, CHUNK, hidden), BF16),
        pltpu.VMEM((NL, CHUNK, hidden), BF16),
        pltpu.VMEM((NL, 7, 96, 2 * LANES), BF16),
        pltpu.VMEM((NL, 7, 48, 2 * LANES), BF16),
        pltpu.VMEM((NL, 7, 48, 2 * LANES), BF16),
        pltpu.VMEM((NL, 7, 48, 2 * LANES), BF16),
        pltpu.VMEM((NL, 7, 96, 2 * LANES), BF16),
        pltpu.VMEM((NL, 7, 96, 2 * LANES), BF16),
        pltpu.VMEM((NL, 3, 48, 96), BF16),
        pltpu.VMEM((NL, 3, 48, 48), BF16),
        pltpu.VMEM((NL, 3, 96, 48), BF16),
        pltpu.VMEM((NL, 3, 96, 96), BF16),
        pltpu.VMEM((NL, 3, 96, 48), BF16),
        pltpu.VMEM((NL, 3, 48, 48), BF16),
        pltpu.VMEM((NL, 3, 48, 96), BF16),
        pltpu.VMEM((NL, 3, 96, 96), BF16),
        pltpu.VMEM((3, 96, 96), BF16),
        pltpu.VMEM((3, 96, 96), BF16),
        pltpu.VMEM((48, 48), BF16),
        pltpu.VMEM((48, 48), BF16),
        pltpu.VMEM((NL, hidden, LANES), BF16),
        pltpu.VMEM((NL, LANES, hidden), BF16),
        pltpu.VMEM((NL, 3, 48, 96), F32),
        pltpu.VMEM((NL, 3, 48, 48), F32),
        pltpu.VMEM((NL, 3, 96, 48), F32),
        pltpu.VMEM((NL, 3, 96, 96), F32),
        pltpu.VMEM((NL, LANES, hidden), F32),
        pltpu.VMEM((NL, LANES, hidden), F32),
        pltpu.VMEM((NL, 8, hidden), F32),
        pltpu.VMEM((NL, 8, LANES), F32),
        pltpu.VMEM((NL, 8, LANES), F32),
        pltpu.VMEM((pack_rows, LANES), F32),
        pltpu.VMEM((pack_rows // 2, LANES), F32),
        pltpu.VMEM((pack_rows, LANES), BF16),
        pltpu.VMEM((plane_size, plane_rows, LANES), BF16),
        pltpu.VMEM((plane_rows, LANES), BF16),
        pltpu.VMEM((4, plane_rows // 4, LANES), BF16),
        dma((2, chunks, 8)),
        dma((2, chunks, 4)),
        dma((2, chunks, 4)),
        dma((2, chunks, 8)),
        dma((2,)),
        dma((6, max(plane_size, 4))),
        dma((6, max(plane_size, 4))),
    ]
    mixed_out, input_grad, packed = pl.pallas_call(
        functools.partial(kernel_body, groups, n_scale, per_device, pack_rows),
        out_shape=[
            jax.ShapeDtypeStruct(tokens.shape, BF16),
            jax.ShapeDtypeStruct(tokens.shape, BF16),
            jax.ShapeDtypeStruct((pack_rows, LANES), BF16),
        ],
        in_specs=[anywhere, anywhere] + [vmem] * 10,
        out_specs=[anywhere, anywhere, vmem],
        scratch_shapes=scratch,
        compiler_params=pltpu.CompilerParams(
            collective_id=0, has_side_effects=True, vmem_limit_bytes=56 << 20
        ),
    )(*args)
    layers = packed[: NL * LAYER_ROWS].reshape(NL, LAYER_ROWS, LANES).astype(F32)
    ffn_in_grad = jnp.concatenate(
        [layers[:, AT_FFN_IN : AT_FFN_IN + LANES], layers[:, AT_FFN_IN + LANES : AT_FFN_OUT]], 2
    )
    ffn_out_grad = jnp.swapaxes(
        jnp.concatenate(
            [layers[:, AT_FFN_OUT : AT_FFN_OUT + LANES], layers[:, AT_FFN_OUT + LANES : LAYER_ROWS]], 2
        ),
        1,
        2,
    )
    return (
        mixed_out,
        input_grad,
        layers[:, 0],
        layers[:, 1],
        layers[:, AT_SEASON_IN : AT_SEASON_IN + SEASON_ROWS, :L0],
        layers[:, AT_TREND_IN : AT_TREND_IN + SEASON_ROWS, SEASON_OUT_LANE : SEASON_OUT_LANE + L0 // 2],
        layers[:, AT_TREND_IN : AT_TREND_IN + TREND_ROWS, : L0 // 2],
        layers[:, AT_TREND_OUT : AT_TREND_OUT + TREND_ROWS, :L0],
        ffn_in_grad,
        layers[:, 2:4].reshape(NL, hidden),
        ffn_out_grad,
    )


def solution(mesh):
    rows = P(("scale", "dp"), None)
    return jax.shard_map(
        functools.partial(body, mesh.shape["dp"], mesh.shape["scale"]),
        mesh=mesh,
        in_specs=(rows, rows, P("scale", None)) + (P(),) * 9,
        out_specs=(rows, rows) + (P(),) * 9,
        check_vma=False,
    )
```

```python
import functools

import jax
import jax.numpy as jnp
from jax import lax
from jax.experimental import pallas as pl
from jax.experimental.pallas import tpu as pltpu
from jax.sharding import PartitionSpec as P

L0 = 96
KERNEL = 25
NL = 2
SEASON_ROWS = 84
TREND_ROWS = 168
EPS = 1e-05
LANES = 128
ITEMS = 8
PAIR = 4
MESH = pl.DeviceIdType.MESH
F32 = jnp.float32
BF16 = jnp.bfloat16

LENGTHS = [L0 >> i for i in range(4)]
SIZES = [ITEMS * n for n in LENGTHS]
STARTS = [sum(SIZES[:i]) for i in range(4)]
CHUNK = sum(SIZES)
SLOTS = [1, 2, 4, 4]
SELF = [(0, 0), (0, 1), (1, 1), (3, 1)]
TILE = 480
SLABS = [(0, 192, 2), (1, 192, 1), (2, 96, 1), (3, 48, 1)]
UNITS = {1: (0, 1), 2: (2,), 3: (3,)}
WEIGHT_COUNT = {1: 2, 2: 4, 3: 4}
GRAD_COUNT = {1: 1, 2: 2, 3: 4}
DUE_FAR = {
    ("forward", 2): [(0, 0), (1, 0), (0, 1), (1, 1)],
    ("scattered", 0): [(0, 2)],
    ("gathered", 0): [(1, 2)],
}
DUE_NEAR = {
    ("forward", 0): [(0, 0)],
    ("backward", 0): [(1, 0)],
    ("forward", 1): [(0, 1)],
    ("backward", 1): [(1, 1)],
    ("scattered", 0): [(0, 2)],
    ("gathered", 0): [(1, 2)],
}

AT_SEASON_IN = 8
AT_TREND_IN = AT_SEASON_IN + NL * SEASON_ROWS
AT_SEASON_OUT = AT_TREND_IN + NL * L0
AT_TREND_OUT = AT_SEASON_OUT + NL * L0 // 2
AT_FFN_IN = AT_TREND_OUT + NL * TREND_ROWS
AT_FFN_OUT = AT_FFN_IN + NL * 2 * LANES
USED_ROWS = AT_FFN_OUT + NL * 2 * LANES
PIECES = 4


def dot(a, b):
    return jnp.dot(a, b, preferred_element_type=F32)


def dot_nt(a, b):
    return lax.dot_general(a, b, (((1,), (1,)), ((), ())), preferred_element_type=F32)


def dot_tn(a, b):
    return lax.dot_general(a, b, (((0,), (0,)), ((), ())), preferred_element_type=F32)


def gelu_parts(v):
    cumulative = 0.5 * (1.0 + lax.erf(v * 0.7071067811865476))
    density = jnp.exp(-0.5 * (v * v)) * 0.3989422804014327
    return v * cumulative, cumulative + v * density


def iota(shape, dim):
    return lax.broadcasted_iota(jnp.int32, shape, dim)


def selection(rows, columns, count, length, base, turned=False, stride=1):
    shape = (columns, rows) if turned else (rows, columns)
    r = iota(shape, 1 if turned else 0)
    c = iota(shape, 0 if turned else 1)
    found = jnp.zeros(shape, jnp.bool_)
    for k in range(count):
        near = c == (r - k * length) * stride + base
        found = found | (near & (r >= k * length) & (r < (k + 1) * length))
    return found.astype(F32)


def block_mask(count, height, width, turned=False):
    shape = (count * width, count * height) if turned else (count * height, count * width)
    r = iota(shape, 1 if turned else 0)
    c = iota(shape, 0 if turned else 1)
    found = jnp.zeros(shape, jnp.bool_)
    for k in range(count):
        found = found | (
            (r >= k * height) & (r < (k + 1) * height) & (c >= k * width) & (c < (k + 1) * width)
        )
    return found.astype(F32)


def moving_counts(count, length, turned):
    size = count * length
    t = iota((size, size), 1 if turned else 0)
    u = iota((size, size), 0 if turned else 1)
    total = jnp.zeros((size, size), F32)
    half = (KERNEL - 1) // 2
    for k in range(count):
        low, high = k * length, (k + 1) * length - 1
        inside = (t >= low) & (t <= high) & (u >= low) & (u <= high)
        near = (jnp.abs(t - u) <= half).astype(F32)
        first = jnp.where(u == low, jnp.maximum(half - (t - low), 0), 0).astype(F32)
        last = jnp.where(u == high, jnp.maximum(half - (high - t), 0), 0).astype(F32)
        total = total + jnp.where(inside, near + first + last, 0.0)
    return total


def beside(value, height):
    return jnp.concatenate([value[k : k + height] for k in range(0, value.shape[0], height)], 1)


def drive(threads):
    active = list(threads)
    while active:
        rest = []
        for thread in active:
            if next(thread, None) is not None:
                rest.append(thread)
        active = rest


def fold_rows(value):
    return jnp.sum(value.reshape(-1, 8, value.shape[-1]), 0)


def group_of(groups, scale, slot, position):
    bounds = [0, groups // 2, 3 * groups // 4, 7 * groups // 8]
    offsets = [0, groups // 4, groups // 8, 3 * groups // 8]
    return position - bounds[scale] + offsets[slot]


def home_of(groups, scale, group):
    if scale == 0:
        return group, 0
    if scale == 1:
        return groups // 2 + lax.rem(group, groups // 4), lax.div(group, groups // 4)
    part = lax.div(group, groups // 8)
    slot = jnp.where(part == 1, 2, jnp.where(part == 2, 1, part))
    first = 3 * groups // 4 if scale == 2 else 7 * groups // 8
    return first + lax.rem(group, groups // 8), slot


def kernel_body(
    groups,
    n_scale,
    per_device,
    pack_rows,
    tokens,
    cotangent,
    item_mask_hbm,
    ln_gain_hbm,
    ln_bias_hbm,
    season_in_hbm,
    season_out_hbm,
    trend_in_hbm,
    trend_out_hbm,
    ffn_in_hbm,
    ffn_bias_hbm,
    ffn_out_hbm,
    mixed_out,
    input_grad,
    packed_out,
    item_mask,
    ln_gain,
    ln_bias,
    season_in,
    season_out,
    trend_in,
    trend_out,
    ffn_in,
    ffn_bias,
    ffn_out,
    param_sem,
    tok_buf,
    cot_buf,
    out_buf,
    grad_buf,
    live,
    field,
    grad,
    df_keep,
    da_keep,
    unit,
    inverse,
    z_keep,
    hidden,
    slope,
    season_src,
    trend_src,
    season_hid,
    season_slope,
    trend_hid,
    trend_slope,
    sa,
    sb,
    ta,
    tb,
    sa_t,
    sb_t,
    ta_t,
    tb_t,
    moving,
    moving_t,
    win_t,
    wout_t,
    d_sa,
    d_sb,
    d_ta,
    d_tb,
    d_win,
    d_wout,
    d_bias,
    d_gain,
    d_off,
    pack,
    half_in,
    half_bf,
    plane_in,
    plane_bf,
    depth_in,
    relay_buf,
    relay_send,
    relay_recv,
    in_send,
    in_recv,
    out_send,
    out_recv,
    ar_send,
    ar_recv,
):
    scale_index = lax.axis_index("scale")
    position = lax.axis_index("dp")
    worker_group = lax.rem(position, groups // 2)
    worker_half = lax.div(position, groups // 2)
    half_items = per_device // 2
    chunks = half_items // ITEMS
    bounds = [0, groups // 2, 3 * groups // 4, 7 * groups // 8, groups]

    params = [
        pltpu.make_async_copy(source, target, param_sem.at[k])
        for k, (source, target) in enumerate(
            (
                (item_mask_hbm, item_mask),
                (ln_gain_hbm, ln_gain),
                (ln_bias_hbm, ln_bias),
                (season_in_hbm, season_in),
                (season_out_hbm, season_out),
                (trend_in_hbm, trend_in),
                (trend_out_hbm, trend_out),
                (ffn_in_hbm, ffn_in),
                (ffn_bias_hbm, ffn_bias),
                (ffn_out_hbm, ffn_out),
            )
        )
    ]

    barrier = pltpu.get_barrier_semaphore()

    plane_dp = groups // 8
    plane_size = plane_dp * n_scale
    core = lax.rem(position, 2)
    place_dp = lax.rem(lax.div(position, 2), plane_dp)
    depth_index = lax.div(position, 2 * plane_dp)

    def greet(device):
        pl.semaphore_signal(barrier, inc=1, device_id=device, device_id_type=MESH)

    def greet_row(k, carry):
        greet((scale_index, lax.rem(position + k, groups)))
        return carry

    def greet_plane(k, carry):
        other = lax.rem(scale_index + 1 + lax.div(k, plane_dp), n_scale)
        greet((other, (depth_index * plane_dp + lax.rem(k, plane_dp)) * 2 + core))
        return carry

    lax.fori_loop(1, groups, greet_row, 0)
    lax.fori_loop(0, (n_scale - 1) * plane_dp, greet_plane, 0)
    pl.semaphore_wait(barrier, groups - 1 + (n_scale - 1) * plane_dp)

    def relayed(scale, slot, half):
        return half == 0 and ((scale == 2 and slot >= 2) or (scale == 3 and slot < 2))

    def inbound(kind, scale, slot, half, chunk):
        source = (tokens, cotangent)[kind]
        target = (tok_buf, cot_buf)[kind]
        length, size = LENGTHS[scale], SIZES[scale]
        first = (slot * per_device + half * half_items + chunk * ITEMS) * length
        src = source.at[pl.ds(pl.multiple_of(first, 16), size)]
        dst = target.at[chunk, pl.ds(STARTS[scale], size)]
        recv = in_recv.at[kind, chunk, scale]
        if (slot, half) == SELF[scale]:
            return pltpu.make_async_copy(src, dst, recv), False
        owner = half * (groups // 2) + group_of(groups, scale, slot, position)
        if relayed(scale, slot, half):
            owner = position + (groups // 8 if scale == 2 else -(groups // 8))
            dst = relay_buf.at[kind, chunk, slot % 2, pl.ds(0, size)]
            recv = relay_recv.at[kind, chunk, slot % 2]
        return (
            pltpu.make_async_remote_copy(
                src_ref=src,
                dst_ref=dst,
                send_sem=in_send.at[kind, chunk, slot * 2 + half],
                recv_sem=recv,
                device_id=(scale_index, owner),
                device_id_type=MESH,
            ),
            True,
        )

    def relay(kind, scale, slot, chunk):
        length, size = LENGTHS[scale], SIZES[scale]
        src = relay_buf.at[kind, chunk, slot % 2, pl.ds(0, size)]
        target = (tok_buf, cot_buf)[kind]
        partner = position + (groups // 8 if scale == 3 else -(groups // 8))
        return pltpu.make_async_remote_copy(
            src_ref=src,
            dst_ref=target.at[chunk, pl.ds(STARTS[scale], size)],
            send_sem=relay_send.at[kind, chunk, slot % 2],
            recv_sem=in_recv.at[kind, chunk, scale],
            device_id=(scale_index, group_of(groups, scale, slot, partner)),
            device_id_type=MESH,
        )

    def order(scale):
        moves = [(kind, slot, half) for kind in range(2) for slot in range(SLOTS[scale]) for half in (1, 0)]
        return sorted(moves, key=lambda move: (move[0], not relayed(scale, move[1], move[2])))

    def each_inbound(act, act_relay, low, high):
        for scale in range(4):

            @pl.when((position >= bounds[scale]) & (position < bounds[scale + 1]))
            def _():
                def one_chunk(chunk, carry):
                    for kind, slot, half in order(scale):
                        act(*inbound(kind, scale, slot, half, chunk))
                    if scale >= 2:
                        other = 5 - scale
                        for kind in range(2):
                            for slot in range(4):
                                if relayed(other, slot, 0):
                                    act_relay(relay(kind, other, slot, chunk), kind, slot, chunk)
                    return carry

                lax.fori_loop(low, high, one_chunk, 0)

    def pass_on(copy, kind, slot, chunk):
        size = SIZES[2 if slot >= 2 else 3]
        ref = relay_buf.at[kind, chunk, slot % 2, pl.ds(0, size)]
        pltpu.make_async_copy(ref, ref, relay_recv.at[kind, chunk, slot % 2]).wait()
        copy.start()

    def inbound_start(low, high):
        each_inbound(lambda copy, remote: copy.start(), pass_on, low, high)

    far = (position < groups // 4) | (position >= bounds[2])
    inbound_start(0, jnp.where(far, 1, chunks))
    for copy in params:
        copy.start()
    for copy in params:
        copy.wait()

    def inbound_wait(kind, chunk):
        target = (tok_buf, cot_buf)[kind]
        for scale in range(4):
            ref = target.at[chunk, pl.ds(STARTS[scale], SIZES[scale])]
            pltpu.make_async_copy(ref, ref, in_recv.at[kind, chunk, scale]).wait()

    def outbound(kind, scale, chunk):
        source = (out_buf, grad_buf)[kind]
        target = (mixed_out, input_grad)[kind]
        home, slot = home_of(groups, scale, worker_group)
        length, size = LENGTHS[scale], SIZES[scale]
        first = (slot * per_device + worker_half * half_items + chunk * ITEMS) * length
        src = source.at[chunk, pl.ds(STARTS[scale], size)]
        dst = target.at[pl.ds(pl.multiple_of(first, 16), size)]
        recv = out_recv.at[kind, chunk, slot * 2 + worker_half]
        local = pltpu.make_async_copy(src, dst, recv)
        remote = pltpu.make_async_remote_copy(
            src_ref=src,
            dst_ref=dst,
            send_sem=out_send.at[kind, chunk, scale],
            recv_sem=recv,
            device_id=(scale_index, home),
            device_id_type=MESH,
        )
        return home, local, remote

    def outbound_start(kind, chunk):
        for scale in range(4):
            home, local, remote = outbound(kind, scale, chunk)

            @pl.when(home == position)
            def _():
                local.start()

            @pl.when(home != position)
            def _():
                remote.start()

    def results_out(event, chunk):
        for is_far, due in ((True, DUE_FAR), (False, DUE_NEAR)):
            for at, sends in due.items():
                if at[0] == event:

                    @pl.when((far if is_far else jnp.logical_not(far)) & (chunk == at[1]))
                    def _():
                        for kind, done in sends:
                            outbound_start(kind, done)

    for layer in range(NL):
        for c in (1, 2, 3):
            count = WEIGHT_COUNT[c]
            fine, coarse = LENGTHS[c - 1], LENGTHS[c]
            at_season = L0 - fine
            at_trend = 2 * L0 - 2 * fine
            for whole, normal, turned, height, width, row, column, stride in (
                (season_in[...], sa, sa_t, coarse, fine, NL * at_season + layer, 0, NL),
                (season_out[layer], sb_t, sb, coarse, coarse, 0, at_season, 1),
                (trend_in[layer], ta_t, ta, coarse, fine, 0, at_trend, 1),
                (trend_out[layer], tb, tb_t, fine, fine, at_trend, 0, 1),
            ):
                rows = selection(count * height, whole.shape[0], count, height, row, stride=stride)
                columns = selection(count * width, whole.shape[1], count, width, column).astype(BF16)
                tall = dot(rows.astype(BF16), whole).astype(BF16)
                normal[layer, c - 1, : count * height, : count * width] = (
                    dot_nt(tall, columns) * block_mask(count, height, width)
                ).astype(BF16)
                turned[layer, c - 1, : count * width, : count * height] = (
                    dot_nt(columns, tall) * block_mask(count, height, width, True)
                ).astype(BF16)
        eye_in = selection(ffn_in.shape[2], ffn_in.shape[2], 1, ffn_in.shape[2], 0).astype(BF16)
        eye_out = selection(LANES, LANES, 1, LANES, 0).astype(BF16)
        win_t[layer] = dot_nt(eye_in, ffn_in[layer]).astype(BF16)
        wout_t[layer] = dot_nt(eye_out, ffn_out[layer]).astype(BF16)
    for scale, height, number in SLABS:
        for ref, is_turned in ((moving, False), (moving_t, True)):
            counts = moving_counts(height // LENGTHS[scale], LENGTHS[scale], is_turned)
            ref[scale, :height, :height] = counts.astype(BF16)
    mean_lanes = jnp.full((LANES, LANES), 1.0 / LANES, BF16)

    mask_rows = jnp.broadcast_to(item_mask[...].astype(F32), (LANES, item_mask.shape[1])).astype(BF16)
    first_item = worker_group * per_device + worker_half * half_items
    chosen = iota((32, item_mask.shape[1]), 1) == iota((32, item_mask.shape[1]), 0) + first_item
    item_live = dot_nt(chosen.astype(F32).astype(BF16), mask_rows).astype(BF16)
    for chunk in range(chunks):
        for i in range(4):
            place = (iota((SIZES[i], 32), 0).astype(F32) + 0.5) * (1.0 / LENGTHS[i])
            column = iota((SIZES[i], 32), 1).astype(F32) - float(chunk * ITEMS)
            one = ((place >= column) & (place < column + 1.0)).astype(F32).astype(BF16)
            live[chunk, STARTS[i] : STARTS[i] + SIZES[i], :] = dot(one, item_live)

    for total in (d_sa, d_sb, d_ta, d_tb, d_win, d_wout, d_bias, d_gain, d_off, pack):
        total[...] = jnp.zeros(total.shape, F32)

    taps = 1.0 / KERNEL

    def matrix(ref, layer, c, rows, columns):
        return ref[layer, c - 1, :rows, :columns]

    def sides(scale, height, j):
        half = SIZES[scale] // 2
        return [STARTS[scale] + side * half + j * height for side in range(2)]

    def forward(layer, chunk, found):
        gain = ln_gain[layer : layer + 1, :]
        offset = ln_bias[layer : layer + 1, :]
        offset_pair = jnp.concatenate([offset, offset], 1)
        bias = ffn_bias[layer : layer + 1, :]

        def rows_of(start, height):
            if layer == 0:
                return tok_buf[chunk, start : start + height, :].astype(F32)
            return field[start : start + height, :]

        def norm(scale, height, j):
            while layer > 0 and ("y", layer - 1, scale, j) not in found:
                yield 1
            parts = []
            for start in sides(scale, height, j):
                x = rows_of(start, height)
                centered = x - jnp.mean(x, -1, keepdims=True)
                yield 1
                inv = lax.rsqrt(dot((centered * centered).astype(BF16), mean_lanes) + EPS)
                n = centered * inv
                unit[layer, start : start + height, :] = n
                inverse[layer, start : start + height, :] = inv
                parts.append(n * gain)
                yield 1
            both = jnp.concatenate(parts, 1)
            average = dot(moving[scale, :height, :height], both.astype(BF16)) * taps
            found["n", layer, scale, j] = both + offset_pair
            found["s", layer, scale, j] = both - average
            found["t", layer, scale, j] = average + offset_pair

        def mixed(source, first, second, kept, hid, slp, u, layer_at, c, fine_to_coarse):
            a = source.astype(BF16)
            rows_in = a.shape[0]
            rows_out = rows_in // 2 if fine_to_coarse else rows_in * 2
            kept[layer_at, u, :rows_in, :] = a
            p = dot(matrix(first, layer_at, c, rows_out, rows_in), a)
            yield None
            h, slope_value = gelu_parts(p)
            h = h.astype(BF16)
            hid[layer_at, u, :rows_out, :] = h
            slp[layer_at, u, :rows_out, :] = slope_value.astype(BF16)
            yield None
            yield dot(matrix(second, layer_at, c, rows_out, rows_out), h)

        def season(c):
            results = []
            for j, u in enumerate(UNITS[c]):
                while ("S", layer, c - 1, j) not in found and not (
                    c == 1 and ("s", layer, 0, j) in found
                ):
                    yield 1
                source = found["s", layer, 0, j] if c == 1 else found["S", layer, c - 1, j]
                for value in mixed(
                    source, sa, sb, season_src, season_hid, season_slope, u, layer, c, True
                ):
                    if value is None:
                        yield 1
                    else:
                        results.append(value)
            mix = results[0] if len(results) == 1 else jnp.concatenate(results, 0)
            found["sm", layer, c, 0] = mix
            while ("s", layer, c, 0) not in found:
                yield 1
            found["S", layer, c, 0] = found["s", layer, c, 0] + mix

        def trend(c):
            while ("t" if c == 3 else "T", layer, c, 0) not in found:
                yield 1
            source = found["t" if c == 3 else "T", layer, c, 0]
            for j, u in enumerate(UNITS[c]):
                part = source[96 * j : 96 * (j + 1)] if c == 1 else source
                for value in mixed(part, ta, tb, trend_src, trend_hid, trend_slope, u, layer, c, False):
                    if value is None:
                        yield 1
                    else:
                        found["tm", layer, c - 1, j] = value
            if c > 1:
                while ("t", layer, c - 1, 0) not in found:
                    yield 1
                found["T", layer, c - 1, 0] = found["t", layer, c - 1, 0] + found["tm", layer, c - 1, 0]

        def ffn(scale, height, j):
            needed = [("n", layer, scale, j)]
            if scale > 0:
                needed.append(("sm", layer, scale, j))
            if scale < 3:
                needed.append(("tm", layer, scale, j))
            while not all(key in found for key in needed):
                yield 1
            value = found[needed[0]]
            for key in needed[1:]:
                value = value + found[key]
            value = value.astype(BF16)
            starts = sides(scale, height, j)
            halves = [value[:, :LANES], value[:, LANES:]]
            for start, z in zip(starts, halves):
                z_keep[layer, start : start + height, :] = z
            a = dot(jnp.concatenate(halves, 0), ffn_in[layer]) + bias
            yield 1
            h, slope_value = gelu_parts(a)
            h = h.astype(BF16)
            slope_value = slope_value.astype(BF16)
            for k, start in enumerate(starts):
                hidden[layer, start : start + height, :] = h[k * height : (k + 1) * height]
                slope[layer, start : start + height, :] = slope_value[k * height : (k + 1) * height]
            yield 1
            f = dot(h, ffn_out[layer])
            yield 1
            for k, start in enumerate(starts):
                y = rows_of(start, height) + live[chunk, start : start + height, :] * f[
                    k * height : (k + 1) * height
                ]
                if layer == NL - 1:
                    out_buf[chunk, start : start + height, :] = y.astype(BF16)
                else:
                    field[start : start + height, :] = y
            found["y", layer, scale, j] = True

        for scale, height, number in reversed(SLABS):
            for j in range(number):
                yield norm(scale, height, j)
        for c in (3, 2, 1):
            yield trend(c)
        for c in (1, 2, 3):
            yield season(c)
        for scale, height, number in (SLABS[1], SLABS[2], SLABS[0], SLABS[3]):
            for j in range(number):
                yield ffn(scale, height, j)

    def backward(layer, chunk, found):
        gain = ln_gain[layer : layer + 1, :]

        def rows_of(start, height):
            if layer == NL - 1:
                return cot_buf[chunk, start : start + height, :].astype(F32)
            return grad[start : start + height, :]

        def ffn(scale, height, j):
            while layer < NL - 1 and ("x", layer + 1, scale, j) not in found:
                yield 1
            starts = sides(scale, height, j)
            parts = []
            for start in starts:
                df = (live[chunk, start : start + height, :] * rows_of(start, height)).astype(BF16)
                df_keep[start : start + height, :] = df
                parts.append(df)
            dh = dot(jnp.concatenate(parts, 0), wout_t[layer])
            yield 1
            parts = []
            for k, start in enumerate(starts):
                da = dh[k * height : (k + 1) * height] * slope[layer, start : start + height, :].astype(F32)
                d_bias[layer] += fold_rows(da)
                da = da.astype(BF16)
                da_keep[start : start + height, :] = da
                parts.append(da)
            yield 1
            dz = dot(jnp.concatenate(parts, 0), win_t[layer])
            found["dz", layer, scale, j] = jnp.concatenate([dz[:height], dz[height:]], 1)

        def weight_grads():
            while not all(("dz", layer, scale, j) in found for scale, _, number in SLABS for j in range(number)):
                yield 1
            for t in range(0, CHUNK, TILE):
                d_win[layer] += dot_tn(z_keep[layer, t : t + TILE, :], da_keep[t : t + TILE, :])
                yield 1
                d_wout[layer] += dot_tn(df_keep[t : t + TILE, :], hidden[layer, t : t + TILE, :])
                yield 1

        def mixed(g, first_t, second_t, slp, u, c, fine_to_coarse):
            rows = g.shape[0]
            rows_out = rows * 2 if fine_to_coarse else rows // 2
            dh = dot(matrix(second_t, layer, c, rows, rows), g)
            yield None
            dp = (dh * slp[layer, u, :rows, :].astype(F32)).astype(BF16)
            yield dp
            yield dot(matrix(first_t, layer, c, rows_out, rows), dp)

        def trend(c):
            results, gs, dps = [], [], []
            for j, u in enumerate(UNITS[c]):
                key = ("dz", layer, 0, j) if c == 1 else ("dT", layer, c - 1, 0)
                while key not in found:
                    yield 1
                g = found[key].astype(BF16)
                gs.append(beside(g, 96))
                steps = []
                for value in mixed(g, ta_t, tb_t, trend_slope, u, c, False):
                    if value is not None:
                        steps.append(value)
                    yield 1
                dps.append(beside(steps[0], 96))
                results.append(steps[1])
            total = results[0] if len(results) == 1 else jnp.concatenate(results, 0)
            found["gT", layer, c, 0] = total
            while ("dz", layer, c, 0) not in found:
                yield 1
            found["dT", layer, c, 0] = found["dz", layer, c, 0] + total
            rows = 48 if c == 3 else 96
            kept = [beside(trend_hid[layer, u, : 2 * rows, :], 96) for u in UNITS[c]]
            d_tb[layer, c - 1] += dot_nt(jnp.concatenate(gs, 1), jnp.concatenate(kept, 1))
            yield 1
            kept = [beside(trend_src[layer, u, :rows, :], 48) for u in UNITS[c]]
            d_ta[layer, c - 1] += dot_nt(jnp.concatenate(kept, 1), jnp.concatenate(dps, 1))

        def season(c):
            key = ("dz", layer, 3, 0) if c == 3 else ("dS", layer, c, 0)
            while key not in found:
                yield 1
            gs, dps = [], []
            for j, u in enumerate(UNITS[c]):
                g = found[key].astype(BF16)
                if c == 1:
                    g = g[96 * j : 96 * (j + 1)]
                gs.append(beside(g, 48))
                steps = []
                for value in mixed(g, sa_t, sb_t, season_slope, u, c, True):
                    if value is not None:
                        steps.append(value)
                    yield 1
                dps.append(beside(steps[0], 48))
                found["gS", layer, c - 1, j] = steps[1]
            if c > 1:
                while ("dz", layer, c - 1, 0) not in found:
                    yield 1
                found["dS", layer, c - 1, 0] = found["dz", layer, c - 1, 0] + found["gS", layer, c - 1, 0]
            rows = 48 if c == 3 else 96
            kept = [beside(season_hid[layer, u, :rows, :], 48) for u in UNITS[c]]
            d_sb[layer, c - 1] += dot_nt(jnp.concatenate(kept, 1), jnp.concatenate(gs, 1))
            yield 1
            kept = [beside(season_src[layer, u, : 2 * rows, :], 96) for u in UNITS[c]]
            d_sa[layer, c - 1] += dot_nt(jnp.concatenate(dps, 1), jnp.concatenate(kept, 1))

        def norm(scale, height, j):
            needed = [("dz", layer, scale, j)]
            if scale < 3:
                needed.append(("gS", layer, scale, j))
            if scale > 0:
                needed.append(("gT", layer, scale, j))
            while not all(key in found for key in needed):
                yield 1
            value = found[needed[0]]
            if scale == 0:
                moved = -found[needed[1]]
                value = value + found[needed[1]]
            elif scale == 3:
                moved = found[needed[1]]
            else:
                moved = found[needed[2]] - found[needed[1]]
                value = value + found[needed[1]]
            value = value + dot(moving_t[scale, :height, :height], moved.astype(BF16)) * taps
            yield 1
            for side, start in enumerate(sides(scale, height, j)):
                d = value[:, side * LANES : (side + 1) * LANES]
                n = unit[layer, start : start + height, :]
                dn = d * n
                d_gain[layer] += fold_rows(dn)
                d_off[layer] += fold_rows(d)
                q = d * gain
                qn = dn * gain
                mean_q = dot(q.astype(BF16), mean_lanes)
                mean_qn = dot(qn.astype(BF16), mean_lanes)
                yield 1
                x = rows_of(start, height) + inverse[layer, start : start + height, :] * (
                    q - mean_q - n * mean_qn
                )
                if layer == 0:
                    grad_buf[chunk, start : start + height, :] = x.astype(BF16)
                else:
                    grad[start : start + height, :] = x
                yield 1
            found["x", layer, scale, j] = True

        for scale, height, number in (SLABS[0], SLABS[3], SLABS[1], SLABS[2]):
            for j in range(number):
                yield ffn(scale, height, j)
        for c in (1, 2, 3):
            yield trend(c)
        for c in (3, 2, 1):
            yield season(c)
        for scale, height, number in reversed(SLABS):
            for j in range(number):
                yield norm(scale, height, j)
        yield weight_grads()

    def one_chunk(chunk, carry):
        inbound_wait(0, chunk)
        found = {}
        drive([thread for layer in range(NL) for thread in forward(layer, chunk, found)])
        inbound_start(chunk + 1, jnp.where(far & (chunk < chunks - 1), chunk + 2, chunk + 1))

        results_out("forward", chunk)
        inbound_wait(1, chunk)
        found = {}
        drive([thread for layer in reversed(range(NL)) for thread in backward(layer, chunk, found)])
        results_out("backward", chunk)
        return carry

    lax.fori_loop(0, chunks, one_chunk, 0)

    for layer in range(NL):
        parts = [None] * 4
        for c in (1, 2, 3):
            count = GRAD_COUNT[c]
            fine, coarse = LENGTHS[c - 1], LENGTHS[c]
            at_season = L0 - fine
            at_trend = 2 * L0 - 2 * fine
            for k, (value, height, width, rows, row, lanes, lane, stride) in enumerate(
                (
                    (d_sa, coarse, fine, NL * SEASON_ROWS, NL * at_season + layer, LANES, 0, NL),
                    (d_sb, coarse, coarse, L0 // 2, 0, LANES, at_season, 1),
                    (d_ta, coarse, fine, L0 // 2, 0, 2 * LANES, at_trend, 1),
                    (d_tb, fine, fine, TREND_ROWS, at_trend, LANES, 0, 1),
                )
            ):
                masked = (value[layer, c - 1] * block_mask(count, height, width)).astype(BF16)
                place = selection(count * height, rows, count, height, row, True, stride).astype(BF16)
                lay = selection(count * width, lanes, count, width, lane).astype(BF16)
                found = dot(dot(place, masked).astype(BF16), lay)
                parts[k] = found if parts[k] is None else parts[k] + found
        pack[layer : layer + 1, :] = jnp.sum(d_gain[layer], 0, keepdims=True)
        pack[NL + layer : NL + layer + 1, :] = jnp.sum(d_off[layer], 0, keepdims=True)
        bias_sum = jnp.sum(d_bias[layer], 0, keepdims=True)
        pack[AT_SEASON_IN : AT_SEASON_IN + NL * SEASON_ROWS, :] += parts[0]
        row = AT_SEASON_OUT + layer * L0 // 2
        pack[row : row + L0 // 2, :] = parts[1]
        row = AT_TREND_OUT + layer * TREND_ROWS
        pack[row : row + TREND_ROWS, :] = parts[3]
        for side in range(2):
            lanes = slice(side * LANES, (side + 1) * LANES)
            row = 2 * NL + 2 * layer + side
            pack[row : row + 1, :] = bias_sum[:, lanes]
            row = AT_TREND_IN + layer * L0 + side * L0 // 2
            pack[row : row + L0 // 2, :] = parts[2][:, lanes]
            row = AT_FFN_IN + (2 * layer + side) * LANES
            pack[row : row + LANES, :] = d_win[layer, :, lanes]
            row = AT_FFN_OUT + (2 * layer + side) * LANES
            pack[row : row + LANES, :] = d_wout[layer, :, lanes].T

    plane_index = scale_index * plane_dp + place_dp
    half_rows = pack_rows // 2
    plane_rows = half_rows // plane_size
    depth_rows = plane_rows // 4

    def core_id():
        return (scale_index, position + 1 - 2 * core)

    def plane_id(index):
        return (
            lax.div(index, plane_dp),
            depth_index * (2 * plane_dp) + lax.rem(index, plane_dp) * 2 + core,
        )

    def depth_id(index):
        return (scale_index, index * (2 * plane_dp) + place_dp * 2 + core)

    def remote(src, dst, stage, slot_out, slot_in, device):
        return pltpu.make_async_remote_copy(
            src_ref=src,
            dst_ref=dst,
            send_sem=ar_send.at[stage, slot_out],
            recv_sem=ar_recv.at[stage, slot_in],
            device_id=device,
            device_id_type=MESH,
        )

    def arrived(ref, stage, slot):
        pltpu.make_async_copy(ref, ref, ar_recv.at[stage, slot]).wait()

    mine = pl.multiple_of(core * half_rows, 16)
    theirs = pl.multiple_of((1 - core) * half_rows, 16)
    first_copy = remote(pack.at[pl.ds(theirs, half_rows)], half_in, 0, 0, 0, core_id())
    first_copy.start()
    first_copy.wait_send()
    arrived(half_in, 0, 0)
    half_bf[pl.ds(mine, half_rows)] = (pack[pl.ds(mine, half_rows)] + half_in[...]).astype(BF16)

    def plane_piece(index):
        return pl.ds(pl.multiple_of(mine + index * plane_rows, 16), plane_rows)

    def plane_round(stage, source_of, target_of, act):
        def one(k, carry):
            other = lax.rem(plane_index + k, plane_size)
            back = lax.rem(plane_index + plane_size - k, plane_size)
            act(other, back, k)
            return carry

        lax.fori_loop(1, plane_size, one, 0)

    def plane_scatter(other, back, k):
        remote(half_bf.at[plane_piece(other)], plane_in.at[k], 1, k, k, plane_id(other)).start()

    plane_round(1, None, None, plane_scatter)
    plane_sum = pack[plane_piece(plane_index)] + half_in[
        pl.ds(pl.multiple_of(plane_index * plane_rows, 16), plane_rows)
    ]

    def plane_wait(k, carry):
        remote(half_bf.at[plane_piece(0)], plane_in.at[k], 1, k, k, core_id()).wait_send()
        arrived(plane_in.at[k], 1, k)
        return carry

    lax.fori_loop(1, plane_size, plane_wait, 0)
    for k in range(1, plane_size):
        plane_sum = plane_sum + plane_in[k].astype(F32)
    plane_bf[...] = plane_sum.astype(BF16)

    def depth_piece(index):
        return pl.ds(pl.multiple_of(index * depth_rows, 16), depth_rows)

    for k in range(1, 4):
        other = lax.rem(depth_index + k, 4)
        remote(plane_bf.at[depth_piece(other)], depth_in.at[k], 2, k, k, depth_id(other)).start()
    results_out("scattered", 0)
    for k in range(1, 4):
        remote(plane_bf.at[depth_piece(0)], depth_in.at[k], 2, k, k, core_id()).wait_send()
        arrived(depth_in.at[k], 2, k)
    total = plane_bf[depth_piece(depth_index)].astype(F32)
    for k in range(1, 4):
        total = total + depth_in[k].astype(F32)

    def final_piece(plane, depth):
        return pl.ds(pl.multiple_of(mine + plane * plane_rows + depth * depth_rows, 16), depth_rows)

    own = final_piece(plane_index, depth_index)
    packed_out[own] = total.astype(BF16)
    for k in range(1, 4):
        other = lax.rem(depth_index + k, 4)
        remote(packed_out.at[own], packed_out.at[own], 3, k, k, depth_id(other)).start()
    results_out("gathered", 0)
    for k in range(1, 4):
        back = lax.rem(depth_index + 4 - k, 4)
        remote(packed_out.at[own], packed_out.at[own], 3, k, k, core_id()).wait_send()
        arrived(packed_out.at[final_piece(plane_index, back)], 3, k)
    own_plane = plane_piece(plane_index)

    def plane_gather(other, back, k):
        remote(packed_out.at[own_plane], packed_out.at[own_plane], 4, k, k, plane_id(other)).start()

    plane_round(4, None, None, plane_gather)

    def plane_gathered(other, back, k):
        remote(packed_out.at[own_plane], packed_out.at[own_plane], 4, k, k, core_id()).wait_send()
        arrived(packed_out.at[plane_piece(back)], 4, k)

    plane_round(4, None, None, plane_gathered)
    own_half = pl.ds(mine, half_rows)
    last_copy = remote(packed_out.at[own_half], packed_out.at[own_half], 5, 0, 0, core_id())
    last_copy.start()
    last_copy.wait_send()
    arrived(packed_out.at[pl.ds(theirs, half_rows)], 5, 0)

    def sent(copy, remote_copy):
        if remote_copy:
            copy.wait_send()

    each_inbound(sent, lambda copy, kind, slot, chunk: copy.wait_send(), 0, chunks)

    def finish(chunk, carry):
        for kind in range(2):
            for scale in range(4):
                home, local, remote_copy = outbound(kind, scale, chunk)

                @pl.when(home != position)
                def _():
                    remote_copy.wait_send()

            for scale in range(4):

                @pl.when((position >= bounds[scale]) & (position < bounds[scale + 1]))
                def _():
                    for slot in range(SLOTS[scale]):
                        for half in range(2):
                            first = (slot * per_device + half * half_items + chunk * ITEMS) * LENGTHS[scale]
                            ref = (mixed_out, input_grad)[kind].at[
                                pl.ds(pl.multiple_of(first, 16), SIZES[scale])
                            ]
                            pltpu.make_async_copy(ref, ref, out_recv.at[kind, chunk, slot * 2 + half]).wait()

        return carry

    lax.fori_loop(0, chunks, finish, 0)


def unpack_body(
    groups,
    tokens,
    cotangent,
    mixed,
    grad,
    packed_hbm,
    mixed_out,
    input_grad,
    *refs,
):
    finals, (packed, staged, in_sem, out_sem, small_sem) = refs[:9], refs[18:]
    (
        gain_grad,
        bias_grad,
        season_in_grad,
        season_out_grad,
        trend_in_grad,
        trend_out_grad,
        ffn_in_grad,
        ffn_bias_grad,
        ffn_out_grad,
    ) = refs[9:18]
    packed_copy = pltpu.make_async_copy(packed_hbm, packed, small_sem.at[9])
    packed_copy.start()
    padded = lax.axis_index("dp") >= 7 * groups // 8
    size = tokens.shape[0] // PIECES
    for kind, (own, other) in enumerate(((mixed, tokens), (grad, cotangent))):
        for k in range(PIECES):
            rows = pl.ds(k * size, size)
            usual = pltpu.make_async_copy(own.at[rows], staged.at[kind, rows], in_sem.at[kind, k])
            if k < PIECES // 2:
                usual.start()
            else:
                rest = pltpu.make_async_copy(other.at[rows], staged.at[kind, rows], in_sem.at[kind, k])

                @pl.when(padded)
                def _():
                    rest.start()

                @pl.when(jnp.logical_not(padded))
                def _():
                    usual.start()

    def piece_out(kind, k):
        rows = pl.ds(k * size, size)
        target = (mixed_out, input_grad)[kind]
        return pltpu.make_async_copy(staged.at[kind, rows], target.at[rows], out_sem.at[kind, k])

    packed_copy.wait()
    top = packed[0:16, :].astype(F32)
    gain_grad[...] = top[0:NL]
    bias_grad[...] = top[NL : 2 * NL]
    for layer in range(NL):
        for side in range(2):
            lanes = slice(side * LANES, (side + 1) * LANES)
            row = 2 * NL + 2 * layer + side
            ffn_bias_grad[layer : layer + 1, lanes] = top[row : row + 1]
            row = AT_FFN_IN + (2 * layer + side) * LANES
            ffn_in_grad[layer, :, lanes] = packed[row : row + LANES, :].astype(F32)
            row = AT_FFN_OUT + (2 * layer + side) * LANES
            ffn_out_grad[layer, side * LANES : (side + 1) * LANES, :] = packed[row : row + LANES, :].astype(F32)
        row = AT_SEASON_OUT + layer * L0 // 2
        season_out_grad[layer] = packed[row : row + L0 // 2, :SEASON_ROWS].astype(F32)
        row = AT_TREND_IN + layer * L0
        trend_in_grad[layer, :, :LANES] = packed[row : row + L0 // 2, :].astype(F32)
        trend_in_grad[layer, :, LANES:] = packed[
            row + L0 // 2 : row + L0, : TREND_ROWS - LANES
        ].astype(F32)
        row = AT_TREND_OUT + layer * TREND_ROWS
        trend_out_grad[layer] = packed[row : row + TREND_ROWS, :L0].astype(F32)
    season_in_grad[...] = packed[AT_SEASON_IN : AT_SEASON_IN + NL * SEASON_ROWS, :L0].astype(F32)
    small = [
        pltpu.make_async_copy(source, target, small_sem.at[k])
        for k, (source, target) in enumerate(zip(refs[9:18], finals))
    ]
    for copy in small:
        copy.start()
    for kind in range(2):
        for k in range(PIECES):
            rows = pl.ds(k * size, size)
            pltpu.make_async_copy(mixed.at[rows], staged.at[kind, rows], in_sem.at[kind, k]).wait()
            piece_out(kind, k).start()
    for copy in small:
        copy.wait()
    for kind in range(2):
        for k in range(PIECES):
            piece_out(kind, k).wait()


def body(groups, n_scale, *args):
    tokens = args[0]
    hidden = args[9].shape[2]
    per_device = tokens.shape[0] // L0
    chunks = per_device // 2 // ITEMS
    devices = groups * n_scale
    unit_rows = 16 * devices
    pack_rows = -(-USED_ROWS // unit_rows) * unit_rows
    plane_size = groups // 8 * n_scale
    plane_rows = pack_rows // 2 // plane_size
    anywhere = pl.BlockSpec(memory_space=pl.ANY)
    vmem = pl.BlockSpec(memory_space=pltpu.VMEM)
    dma = pltpu.SemaphoreType.DMA
    turned = (
        args[:5]
        + (jnp.swapaxes(args[5], 0, 1).reshape(NL * SEASON_ROWS, L0),)
        + tuple(jnp.swapaxes(member, 1, 2) for member in args[6:8])
        + args[8:]
    )
    scratch = [pltpu.VMEM(member.shape, member.dtype) for member in turned[2:]]
    scratch += [
        dma((len(turned) - 2,)),
        pltpu.VMEM((chunks, CHUNK, LANES), BF16),
        pltpu.VMEM((chunks, CHUNK, LANES), BF16),
        pltpu.VMEM((chunks, CHUNK, LANES), BF16),
        pltpu.VMEM((chunks, CHUNK, LANES), BF16),
        pltpu.VMEM((chunks, CHUNK, LANES), F32),
        pltpu.VMEM((CHUNK, LANES), F32),
        pltpu.VMEM((CHUNK, LANES), F32),
        pltpu.VMEM((CHUNK, LANES), BF16),
        pltpu.VMEM((CHUNK, hidden), BF16),
        pltpu.VMEM((NL, CHUNK, LANES), F32),
        pltpu.VMEM((NL, CHUNK, LANES), F32),
        pltpu.VMEM((NL, CHUNK, LANES), BF16),
        pltpu.VMEM((NL, CHUNK, hidden), BF16),
        pltpu.VMEM((NL, CHUNK, hidden), BF16),
        pltpu.VMEM((NL, 4, 192, 2 * LANES), BF16),
        pltpu.VMEM((NL, 4, 96, 2 * LANES), BF16),
        pltpu.VMEM((NL, 4, 96, 2 * LANES), BF16),
        pltpu.VMEM((NL, 4, 96, 2 * LANES), BF16),
        pltpu.VMEM((NL, 4, 192, 2 * LANES), BF16),
        pltpu.VMEM((NL, 4, 192, 2 * LANES), BF16),
        pltpu.VMEM((NL, 3, 96, 192), BF16),
        pltpu.VMEM((NL, 3, 96, 96), BF16),
        pltpu.VMEM((NL, 3, 192, 96), BF16),
        pltpu.VMEM((NL, 3, 192, 192), BF16),
        pltpu.VMEM((NL, 3, 192, 96), BF16),
        pltpu.VMEM((NL, 3, 96, 96), BF16),
        pltpu.VMEM((NL, 3, 96, 192), BF16),
        pltpu.VMEM((NL, 3, 192, 192), BF16),
        pltpu.VMEM((4, 192, 192), BF16),
        pltpu.VMEM((4, 192, 192), BF16),
        pltpu.VMEM((NL, hidden, LANES), BF16),
        pltpu.VMEM((NL, LANES, hidden), BF16),
        pltpu.VMEM((NL, 3, 48, 96), F32),
        pltpu.VMEM((NL, 3, 48, 48), F32),
        pltpu.VMEM((NL, 3, 48, 96), F32),
        pltpu.VMEM((NL, 3, 96, 96), F32),
        pltpu.VMEM((NL, LANES, hidden), F32),
        pltpu.VMEM((NL, LANES, hidden), F32),
        pltpu.VMEM((NL, 8, hidden), F32),
        pltpu.VMEM((NL, 8, LANES), F32),
        pltpu.VMEM((NL, 8, LANES), F32),
        pltpu.VMEM((pack_rows, LANES), F32),
        pltpu.VMEM((pack_rows // 2, LANES), F32),
        pltpu.VMEM((pack_rows, LANES), BF16),
        pltpu.VMEM((plane_size, plane_rows, LANES), BF16),
        pltpu.VMEM((plane_rows, LANES), BF16),
        pltpu.VMEM((4, plane_rows // 4, LANES), BF16),
        pltpu.VMEM((2, chunks, 2, SIZES[2], LANES), BF16),
        dma((2, chunks, 2)),
        dma((2, chunks, 2)),
        dma((2, chunks, 8)),
        dma((2, chunks, 4)),
        dma((2, chunks, 4)),
        dma((2, chunks, 8)),
        dma((6, max(plane_size, 4))),
        dma((6, max(plane_size, 4))),
    ]
    mixed_out, input_grad, packed = pl.pallas_call(
        functools.partial(kernel_body, groups, n_scale, per_device, pack_rows),
        out_shape=[
            jax.ShapeDtypeStruct(tokens.shape, BF16),
            jax.ShapeDtypeStruct(tokens.shape, BF16),
            jax.ShapeDtypeStruct((pack_rows, LANES), BF16),
        ],
        in_specs=[anywhere] * len(turned),
        out_specs=[anywhere, anywhere, vmem],
        scratch_shapes=scratch,
        compiler_params=pltpu.CompilerParams(
            collective_id=0, has_side_effects=True, vmem_limit_bytes=58 << 20
        ),
    )(*turned)
    finals = [
        jax.ShapeDtypeStruct(shape, F32)
        for shape in (
            (NL, LANES),
            (NL, LANES),
            (NL * SEASON_ROWS, L0),
            (NL, L0 // 2, SEASON_ROWS),
            (NL, L0 // 2, TREND_ROWS),
            (NL, TREND_ROWS, L0),
            (NL, LANES, hidden),
            (NL, hidden),
            (NL, hidden, LANES),
        )
    ]
    outs = pl.pallas_call(
        functools.partial(unpack_body, groups),
        out_shape=[
            jax.ShapeDtypeStruct(tokens.shape, BF16),
            jax.ShapeDtypeStruct(tokens.shape, BF16),
            *finals,
        ],
        in_specs=[anywhere] * 5,
        out_specs=[anywhere] * 11,
        scratch_shapes=[pltpu.VMEM(member.shape, F32) for member in finals]
        + [
            pltpu.VMEM((pack_rows, LANES), BF16),
            pltpu.VMEM((2,) + tokens.shape, BF16),
            dma((2, PIECES)),
            dma((2, PIECES)),
            dma((len(finals) + 1,)),
        ],
        compiler_params=pltpu.CompilerParams(vmem_limit_bytes=58 << 20),
    )(tokens, args[1], mixed_out, input_grad, packed)
    return (
        *outs[:4],
        jnp.swapaxes(outs[4].reshape(SEASON_ROWS, NL, L0), 0, 1),
        jnp.swapaxes(outs[5], 1, 2),
        jnp.swapaxes(outs[6], 1, 2),
        *outs[7:],
    )


def solution(mesh):
    rows = P(("scale", "dp"), None)
    return jax.shard_map(
        functools.partial(body, mesh.shape["dp"], mesh.shape["scale"]),
        mesh=mesh,
        in_specs=(rows, rows, P("scale", None)) + (P(),) * 9,
        out_specs=(rows, rows) + (P(),) * 9,
        check_vma=False,
    )
```

```python
import functools

import jax
import jax.numpy as jnp
from jax import lax
from jax.experimental import pallas as pl
from jax.experimental.pallas import tpu as pltpu
from jax.sharding import PartitionSpec as P

L0 = 96
KERNEL = 25
NL = 2
SEASON_ROWS = 84
TREND_ROWS = 168
EPS = 1e-05
LANES = 128
ITEMS = 8
PAIR = 4
MESH = pl.DeviceIdType.MESH
F32 = jnp.float32
BF16 = jnp.bfloat16

LENGTHS = [L0 >> i for i in range(4)]
SIZES = [ITEMS * n for n in LENGTHS]
STARTS = [sum(SIZES[:i]) for i in range(4)]
CHUNK = sum(SIZES)
SLOTS = [1, 2, 4, 4]
SELF = [(0, 0), (0, 1), (1, 1), (3, 1)]
TILE = 480
SLABS = [(0, 192, 2), (1, 192, 1), (2, 96, 1), (3, 48, 1)]
UNITS = {1: (0, 1), 2: (2,), 3: (3,)}
WEIGHT_COUNT = {1: 2, 2: 4, 3: 4}
GRAD_COUNT = {1: 1, 2: 2, 3: 4}
DUE_FAR = {
    ("forward", 2): [(0, 0), (1, 0), (0, 1), (1, 1)],
    ("gathered", 0): [(0, 2), (1, 2)],
}
DUE_NEAR = {
    ("forward", 0): [(0, 0)],
    ("backward", 0): [(1, 0)],
    ("forward", 1): [(0, 1)],
    ("backward", 1): [(1, 1)],
    ("forward", 2): [(0, 2)],
    ("backward", 2): [(1, 2)],
}
AT_SEASON_IN = 8
AT_TREND_IN = AT_SEASON_IN + NL * SEASON_ROWS
AT_SEASON_OUT = AT_TREND_IN + NL * L0
AT_TREND_OUT = AT_SEASON_OUT + NL * L0 // 2
AT_FFN_IN = AT_TREND_OUT + NL * TREND_ROWS
AT_FFN_OUT = AT_FFN_IN + NL * 2 * LANES
USED_ROWS = AT_FFN_OUT + NL * 2 * LANES
PIECES = 4


def dot(a, b):
    return jnp.dot(a, b, preferred_element_type=F32)


def dot_nt(a, b):
    return lax.dot_general(a, b, (((1,), (1,)), ((), ())), preferred_element_type=F32)


def dot_tn(a, b):
    return lax.dot_general(a, b, (((0,), (0,)), ((), ())), preferred_element_type=F32)


def gelu_parts(v):
    cumulative = 0.5 * (1.0 + lax.erf(v * 0.7071067811865476))
    density = jnp.exp(-0.5 * (v * v)) * 0.3989422804014327
    return v * cumulative, cumulative + v * density


def iota(shape, dim):
    return lax.broadcasted_iota(jnp.int32, shape, dim)


def selection(rows, columns, count, length, base, turned=False, stride=1):
    shape = (columns, rows) if turned else (rows, columns)
    r = iota(shape, 1 if turned else 0)
    c = iota(shape, 0 if turned else 1)
    found = jnp.zeros(shape, jnp.bool_)
    for k in range(count):
        near = c == (r - k * length) * stride + base
        found = found | (near & (r >= k * length) & (r < (k + 1) * length))
    return found.astype(F32)


def block_mask(count, height, width, turned=False):
    shape = (count * width, count * height) if turned else (count * height, count * width)
    r = iota(shape, 1 if turned else 0)
    c = iota(shape, 0 if turned else 1)
    found = jnp.zeros(shape, jnp.bool_)
    for k in range(count):
        found = found | (
            (r >= k * height) & (r < (k + 1) * height) & (c >= k * width) & (c < (k + 1) * width)
        )
    return found.astype(F32)


def moving_counts(count, length, turned):
    size = count * length
    t = iota((size, size), 1 if turned else 0)
    u = iota((size, size), 0 if turned else 1)
    total = jnp.zeros((size, size), F32)
    half = (KERNEL - 1) // 2
    for k in range(count):
        low, high = k * length, (k + 1) * length - 1
        inside = (t >= low) & (t <= high) & (u >= low) & (u <= high)
        near = (jnp.abs(t - u) <= half).astype(F32)
        first = jnp.where(u == low, jnp.maximum(half - (t - low), 0), 0).astype(F32)
        last = jnp.where(u == high, jnp.maximum(half - (high - t), 0), 0).astype(F32)
        total = total + jnp.where(inside, near + first + last, 0.0)
    return total


def beside(value, height):
    return jnp.concatenate([value[k : k + height] for k in range(0, value.shape[0], height)], 1)


def drive(threads):
    active = list(threads)
    while active:
        rest = []
        for thread in active:
            if next(thread, None) is not None:
                rest.append(thread)
        active = rest


def fold_rows(value):
    return jnp.sum(value.reshape(-1, 8, value.shape[-1]), 0)


def group_of(groups, scale, slot, position):
    bounds = [0, groups // 2, 3 * groups // 4, 7 * groups // 8]
    offsets = [0, groups // 4, groups // 8, 3 * groups // 8]
    return position - bounds[scale] + offsets[slot]


def home_of(groups, scale, group):
    if scale == 0:
        return group, 0
    if scale == 1:
        return groups // 2 + lax.rem(group, groups // 4), lax.div(group, groups // 4)
    part = lax.div(group, groups // 8)
    slot = jnp.where(part == 1, 2, jnp.where(part == 2, 1, part))
    first = 3 * groups // 4 if scale == 2 else 7 * groups // 8
    return first + lax.rem(group, groups // 8), slot


def kernel_body(
    groups,
    n_scale,
    per_device,
    pack_rows,
    tokens,
    cotangent,
    item_mask_hbm,
    ln_gain_hbm,
    ln_bias_hbm,
    season_in_hbm,
    season_out_hbm,
    trend_in_hbm,
    trend_out_hbm,
    ffn_in_hbm,
    ffn_bias_hbm,
    ffn_out_hbm,
    mixed_out,
    input_grad,
    packed_out,
    item_mask,
    ln_gain,
    ln_bias,
    season_in,
    season_out,
    trend_in,
    trend_out,
    ffn_in,
    ffn_bias,
    ffn_out,
    param_sem,
    tok_buf,
    cot_buf,
    out_buf,
    grad_buf,
    live,
    field,
    grad,
    df_keep,
    da_keep,
    unit,
    inverse,
    z_keep,
    hidden,
    slope,
    season_src,
    trend_src,
    season_hid,
    season_slope,
    trend_hid,
    trend_slope,
    sa,
    sb,
    ta,
    tb,
    sa_t,
    sb_t,
    ta_t,
    tb_t,
    moving,
    moving_t,
    win_t,
    wout_t,
    d_sa,
    d_sb,
    d_ta,
    d_tb,
    d_win,
    d_wout,
    d_bias,
    d_gain,
    d_off,
    pack,
    half_in,
    half_bf,
    plane_in,
    plane_bf,
    pair_in,
    across_out,
    across_in,
    relay_buf,
    relay_send,
    relay_recv,
    in_send,
    in_recv,
    out_send,
    out_recv,
    ar_send,
    ar_recv,
):
    scale_index = lax.axis_index("scale")
    position = lax.axis_index("dp")
    worker_group = lax.rem(position, groups // 2)
    worker_half = lax.div(position, groups // 2)
    half_items = per_device // 2
    chunks = half_items // ITEMS
    bounds = [0, groups // 2, 3 * groups // 4, 7 * groups // 8, groups]

    params = [
        pltpu.make_async_copy(source, target, param_sem.at[k])
        for k, (source, target) in enumerate(
            (
                (item_mask_hbm, item_mask),
                (ln_gain_hbm, ln_gain),
                (ln_bias_hbm, ln_bias),
                (season_in_hbm, season_in),
                (season_out_hbm, season_out),
                (trend_in_hbm, trend_in),
                (trend_out_hbm, trend_out),
                (ffn_in_hbm, ffn_in),
                (ffn_bias_hbm, ffn_bias),
                (ffn_out_hbm, ffn_out),
            )
        )
    ]

    barrier = pltpu.get_barrier_semaphore()

    plane_dp = groups // 8
    plane_size = plane_dp * n_scale
    core = lax.rem(position, 2)
    place_dp = lax.rem(lax.div(position, 2), plane_dp)
    depth_index = lax.div(position, 2 * plane_dp)

    def greet(device):
        pl.semaphore_signal(barrier, inc=1, device_id=device, device_id_type=MESH)

    def greet_row(k, carry):
        greet((scale_index, lax.rem(position + k, groups)))
        return carry

    def greet_plane(k, carry):
        other = lax.rem(scale_index + 1 + lax.div(k, plane_dp), n_scale)
        greet((other, (depth_index * plane_dp + lax.rem(k, plane_dp)) * 2 + core))
        return carry

    lax.fori_loop(1, groups, greet_row, 0)
    lax.fori_loop(0, (n_scale - 1) * plane_dp, greet_plane, 0)
    pl.semaphore_wait(barrier, groups - 1 + (n_scale - 1) * plane_dp)

    def relayed(scale, slot, half):
        return half == 0 and ((scale == 2 and slot >= 2) or (scale == 3 and slot < 2))

    def inbound(kind, scale, slot, half, chunk):
        source = (tokens, cotangent)[kind]
        target = (tok_buf, cot_buf)[kind]
        length, size = LENGTHS[scale], SIZES[scale]
        first = (slot * per_device + half * half_items + chunk * ITEMS) * length
        src = source.at[pl.ds(pl.multiple_of(first, 16), size)]
        dst = target.at[chunk, pl.ds(STARTS[scale], size)]
        recv = in_recv.at[kind, chunk, scale]
        if (slot, half) == SELF[scale]:
            return pltpu.make_async_copy(src, dst, recv), False
        owner = half * (groups // 2) + group_of(groups, scale, slot, position)
        if relayed(scale, slot, half):
            owner = position + (groups // 8 if scale == 2 else -(groups // 8))
            dst = relay_buf.at[kind, chunk, slot % 2, pl.ds(0, size)]
            recv = relay_recv.at[kind, chunk, slot % 2]
        return (
            pltpu.make_async_remote_copy(
                src_ref=src,
                dst_ref=dst,
                send_sem=in_send.at[kind, chunk, slot * 2 + half],
                recv_sem=recv,
                device_id=(scale_index, owner),
                device_id_type=MESH,
            ),
            True,
        )

    def relay(kind, scale, slot, chunk):
        length, size = LENGTHS[scale], SIZES[scale]
        src = relay_buf.at[kind, chunk, slot % 2, pl.ds(0, size)]
        target = (tok_buf, cot_buf)[kind]
        partner = position + (groups // 8 if scale == 3 else -(groups // 8))
        return pltpu.make_async_remote_copy(
            src_ref=src,
            dst_ref=target.at[chunk, pl.ds(STARTS[scale], size)],
            send_sem=relay_send.at[kind, chunk, slot % 2],
            recv_sem=in_recv.at[kind, chunk, scale],
            device_id=(scale_index, group_of(groups, scale, slot, partner)),
            device_id_type=MESH,
        )

    def order(scale):
        moves = [(kind, slot, half) for kind in range(2) for slot in range(SLOTS[scale]) for half in (1, 0)]
        return sorted(moves, key=lambda move: (move[0], not relayed(scale, move[1], move[2])))

    def each_inbound(act, act_relay, low, high):
        for scale in range(4):

            @pl.when((position >= bounds[scale]) & (position < bounds[scale + 1]))
            def _():
                def one_chunk(chunk, carry):
                    for kind, slot, half in order(scale):
                        act(*inbound(kind, scale, slot, half, chunk))
                    if scale >= 2:
                        other = 5 - scale
                        for kind in range(2):
                            for slot in range(4):
                                if relayed(other, slot, 0):
                                    act_relay(relay(kind, other, slot, chunk), kind, slot, chunk)
                    return carry

                lax.fori_loop(low, high, one_chunk, 0)

    def pass_on(copy, kind, slot, chunk):
        size = SIZES[2 if slot >= 2 else 3]
        ref = relay_buf.at[kind, chunk, slot % 2, pl.ds(0, size)]
        pltpu.make_async_copy(ref, ref, relay_recv.at[kind, chunk, slot % 2]).wait()
        copy.start()

    def inbound_start(low, high):
        each_inbound(lambda copy, remote: copy.start(), pass_on, low, high)

    far = (position < groups // 4) | (position >= bounds[2])
    inbound_start(0, jnp.where(far, 1, chunks))
    for copy in params:
        copy.start()
    for copy in params:
        copy.wait()

    def inbound_wait(kind, chunk):
        target = (tok_buf, cot_buf)[kind]
        for scale in range(4):
            ref = target.at[chunk, pl.ds(STARTS[scale], SIZES[scale])]
            pltpu.make_async_copy(ref, ref, in_recv.at[kind, chunk, scale]).wait()

    def outbound(kind, scale, chunk):
        source = (out_buf, grad_buf)[kind]
        target = (mixed_out, input_grad)[kind]
        home, slot = home_of(groups, scale, worker_group)
        length, size = LENGTHS[scale], SIZES[scale]
        first = (slot * per_device + worker_half * half_items + chunk * ITEMS) * length
        src = source.at[chunk, pl.ds(STARTS[scale], size)]
        dst = target.at[pl.ds(pl.multiple_of(first, 16), size)]
        recv = out_recv.at[kind, chunk, slot * 2 + worker_half]
        local = pltpu.make_async_copy(src, dst, recv)
        remote = pltpu.make_async_remote_copy(
            src_ref=src,
            dst_ref=dst,
            send_sem=out_send.at[kind, chunk, scale],
            recv_sem=recv,
            device_id=(scale_index, home),
            device_id_type=MESH,
        )
        return home, local, remote

    def outbound_start(kind, chunk):
        for scale in range(4):
            home, local, remote = outbound(kind, scale, chunk)

            @pl.when(home == position)
            def _():
                local.start()

            @pl.when(home != position)
            def _():
                remote.start()

    def results_out(event, chunk):
        for is_far, due in ((True, DUE_FAR), (False, DUE_NEAR)):
            for at, sends in due.items():
                if at[0] == event:

                    @pl.when((far if is_far else jnp.logical_not(far)) & (chunk == at[1]))
                    def _():
                        for kind, done in sends:
                            outbound_start(kind, done)

    for layer in range(NL):
        for c in (1, 2, 3):
            count = WEIGHT_COUNT[c]
            fine, coarse = LENGTHS[c - 1], LENGTHS[c]
            at_season = L0 - fine
            at_trend = 2 * L0 - 2 * fine
            for whole, normal, turned, height, width, row, column, stride in (
                (season_in[...], sa, sa_t, coarse, fine, NL * at_season + layer, 0, NL),
                (season_out[layer], sb_t, sb, coarse, coarse, 0, at_season, 1),
                (trend_in[layer], ta_t, ta, coarse, fine, 0, at_trend, 1),
                (trend_out[layer], tb, tb_t, fine, fine, at_trend, 0, 1),
            ):
                rows = selection(count * height, whole.shape[0], count, height, row, stride=stride)
                columns = selection(count * width, whole.shape[1], count, width, column).astype(BF16)
                tall = dot(rows.astype(BF16), whole).astype(BF16)
                normal[layer, c - 1, : count * height, : count * width] = (
                    dot_nt(tall, columns) * block_mask(count, height, width)
                ).astype(BF16)
                turned[layer, c - 1, : count * width, : count * height] = (
                    dot_nt(columns, tall) * block_mask(count, height, width, True)
                ).astype(BF16)
        eye_in = selection(ffn_in.shape[2], ffn_in.shape[2], 1, ffn_in.shape[2], 0).astype(BF16)
        eye_out = selection(LANES, LANES, 1, LANES, 0).astype(BF16)
        win_t[layer] = dot_nt(eye_in, ffn_in[layer]).astype(BF16)
        wout_t[layer] = dot_nt(eye_out, ffn_out[layer]).astype(BF16)
    for scale, height, number in SLABS:
        for ref, is_turned in ((moving, False), (moving_t, True)):
            counts = moving_counts(height // LENGTHS[scale], LENGTHS[scale], is_turned)
            ref[scale, :height, :height] = counts.astype(BF16)
    mean_lanes = jnp.full((LANES, LANES), 1.0 / LANES, BF16)

    mask_rows = jnp.broadcast_to(item_mask[...].astype(F32), (LANES, item_mask.shape[1])).astype(BF16)
    first_item = worker_group * per_device + worker_half * half_items
    chosen = iota((32, item_mask.shape[1]), 1) == iota((32, item_mask.shape[1]), 0) + first_item
    item_live = dot_nt(chosen.astype(F32).astype(BF16), mask_rows).astype(BF16)
    for chunk in range(chunks):
        for i in range(4):
            place = (iota((SIZES[i], 32), 0).astype(F32) + 0.5) * (1.0 / LENGTHS[i])
            column = iota((SIZES[i], 32), 1).astype(F32) - float(chunk * ITEMS)
            one = ((place >= column) & (place < column + 1.0)).astype(F32).astype(BF16)
            live[chunk, STARTS[i] : STARTS[i] + SIZES[i], :] = dot(one, item_live)

    for total in (d_sa, d_sb, d_ta, d_tb, d_win, d_wout, d_bias, d_gain, d_off, pack):
        total[...] = jnp.zeros(total.shape, F32)

    taps = 1.0 / KERNEL

    def matrix(ref, layer, c, rows, columns):
        return ref[layer, c - 1, :rows, :columns]

    def sides(scale, height, j):
        half = SIZES[scale] // 2
        return [STARTS[scale] + side * half + j * height for side in range(2)]

    def forward(layer, chunk, found):
        gain = ln_gain[layer : layer + 1, :]
        offset = ln_bias[layer : layer + 1, :]
        offset_pair = jnp.concatenate([offset, offset], 1)
        bias = ffn_bias[layer : layer + 1, :]

        def rows_of(start, height):
            if layer == 0:
                return tok_buf[chunk, start : start + height, :].astype(F32)
            return field[start : start + height, :]

        def norm(scale, height, j):
            while layer > 0 and ("y", layer - 1, scale, j) not in found:
                yield 1
            parts = []
            for start in sides(scale, height, j):
                x = rows_of(start, height)
                centered = x - jnp.mean(x, -1, keepdims=True)
                yield 1
                inv = lax.rsqrt(dot((centered * centered).astype(BF16), mean_lanes) + EPS)
                n = centered * inv
                unit[layer, start : start + height, :] = n
                inverse[layer, start : start + height, :] = inv
                parts.append(n * gain)
                yield 1
            both = jnp.concatenate(parts, 1)
            average = dot(moving[scale, :height, :height], both.astype(BF16)) * taps
            found["n", layer, scale, j] = both + offset_pair
            found["s", layer, scale, j] = both - average
            found["t", layer, scale, j] = average + offset_pair

        def mixed(source, first, second, kept, hid, slp, u, layer_at, c, fine_to_coarse):
            a = source.astype(BF16)
            rows_in = a.shape[0]
            rows_out = rows_in // 2 if fine_to_coarse else rows_in * 2
            kept[layer_at, u, :rows_in, :] = a
            p = dot(matrix(first, layer_at, c, rows_out, rows_in), a)
            yield None
            h, slope_value = gelu_parts(p)
            h = h.astype(BF16)
            hid[layer_at, u, :rows_out, :] = h
            slp[layer_at, u, :rows_out, :] = slope_value.astype(BF16)
            yield None
            yield dot(matrix(second, layer_at, c, rows_out, rows_out), h)

        def season(c):
            results = []
            for j, u in enumerate(UNITS[c]):
                while ("S", layer, c - 1, j) not in found and not (
                    c == 1 and ("s", layer, 0, j) in found
                ):
                    yield 1
                source = found["s", layer, 0, j] if c == 1 else found["S", layer, c - 1, j]
                for value in mixed(
                    source, sa, sb, season_src, season_hid, season_slope, u, layer, c, True
                ):
                    if value is None:
                        yield 1
                    else:
                        results.append(value)
            mix = results[0] if len(results) == 1 else jnp.concatenate(results, 0)
            found["sm", layer, c, 0] = mix
            while ("s", layer, c, 0) not in found:
                yield 1
            found["S", layer, c, 0] = found["s", layer, c, 0] + mix

        def trend(c):
            while ("t" if c == 3 else "T", layer, c, 0) not in found:
                yield 1
            source = found["t" if c == 3 else "T", layer, c, 0]
            for j, u in enumerate(UNITS[c]):
                part = source[96 * j : 96 * (j + 1)] if c == 1 else source
                for value in mixed(part, ta, tb, trend_src, trend_hid, trend_slope, u, layer, c, False):
                    if value is None:
                        yield 1
                    else:
                        found["tm", layer, c - 1, j] = value
            if c > 1:
                while ("t", layer, c - 1, 0) not in found:
                    yield 1
                found["T", layer, c - 1, 0] = found["t", layer, c - 1, 0] + found["tm", layer, c - 1, 0]

        def ffn(scale, height, j):
            needed = [("n", layer, scale, j)]
            if scale > 0:
                needed.append(("sm", layer, scale, j))
            if scale < 3:
                needed.append(("tm", layer, scale, j))
            while not all(key in found for key in needed):
                yield 1
            value = found[needed[0]]
            for key in needed[1:]:
                value = value + found[key]
            value = value.astype(BF16)
            starts = sides(scale, height, j)
            halves = [value[:, :LANES], value[:, LANES:]]
            for start, z in zip(starts, halves):
                z_keep[layer, start : start + height, :] = z
            a = dot(jnp.concatenate(halves, 0), ffn_in[layer]) + bias
            yield 1
            h, slope_value = gelu_parts(a)
            h = h.astype(BF16)
            slope_value = slope_value.astype(BF16)
            for k, start in enumerate(starts):
                hidden[layer, start : start + height, :] = h[k * height : (k + 1) * height]
                slope[layer, start : start + height, :] = slope_value[k * height : (k + 1) * height]
            yield 1
            f = dot(h, ffn_out[layer])
            yield 1
            for k, start in enumerate(starts):
                y = rows_of(start, height) + live[chunk, start : start + height, :] * f[
                    k * height : (k + 1) * height
                ]
                if layer == NL - 1:
                    out_buf[chunk, start : start + height, :] = y.astype(BF16)
                else:
                    field[start : start + height, :] = y
            found["y", layer, scale, j] = True

        for scale, height, number in reversed(SLABS):
            for j in range(number):
                yield norm(scale, height, j)
        for c in (3, 2, 1):
            yield trend(c)
        for c in (1, 2, 3):
            yield season(c)
        for scale, height, number in (SLABS[1], SLABS[2], SLABS[0], SLABS[3]):
            for j in range(number):
                yield ffn(scale, height, j)

    def backward(layer, chunk, found):
        gain = ln_gain[layer : layer + 1, :]

        def rows_of(start, height):
            if layer == NL - 1:
                return cot_buf[chunk, start : start + height, :].astype(F32)
            return grad[start : start + height, :]

        def ffn(scale, height, j):
            while layer < NL - 1 and ("x", layer + 1, scale, j) not in found:
                yield 1
            starts = sides(scale, height, j)
            parts = []
            for start in starts:
                df = (live[chunk, start : start + height, :] * rows_of(start, height)).astype(BF16)
                df_keep[start : start + height, :] = df
                parts.append(df)
            dh = dot(jnp.concatenate(parts, 0), wout_t[layer])
            yield 1
            parts = []
            for k, start in enumerate(starts):
                da = dh[k * height : (k + 1) * height] * slope[layer, start : start + height, :].astype(F32)
                d_bias[layer] += fold_rows(da)
                da = da.astype(BF16)
                da_keep[start : start + height, :] = da
                parts.append(da)
            yield 1
            dz = dot(jnp.concatenate(parts, 0), win_t[layer])
            found["dz", layer, scale, j] = jnp.concatenate([dz[:height], dz[height:]], 1)

        def weight_grads():
            while not all(("dz", layer, scale, j) in found for scale, _, number in SLABS for j in range(number)):
                yield 1
            for t in range(0, CHUNK, TILE):
                d_win[layer] += dot_tn(z_keep[layer, t : t + TILE, :], da_keep[t : t + TILE, :])
                yield 1
                d_wout[layer] += dot_tn(df_keep[t : t + TILE, :], hidden[layer, t : t + TILE, :])
                yield 1

        def mixed(g, first_t, second_t, slp, u, c, fine_to_coarse):
            rows = g.shape[0]
            rows_out = rows * 2 if fine_to_coarse else rows // 2
            dh = dot(matrix(second_t, layer, c, rows, rows), g)
            yield None
            dp = (dh * slp[layer, u, :rows, :].astype(F32)).astype(BF16)
            yield dp
            yield dot(matrix(first_t, layer, c, rows_out, rows), dp)

        def trend(c):
            results, gs, dps = [], [], []
            for j, u in enumerate(UNITS[c]):
                key = ("dz", layer, 0, j) if c == 1 else ("dT", layer, c - 1, 0)
                while key not in found:
                    yield 1
                g = found[key].astype(BF16)
                gs.append(beside(g, 96))
                steps = []
                for value in mixed(g, ta_t, tb_t, trend_slope, u, c, False):
                    if value is not None:
                        steps.append(value)
                    yield 1
                dps.append(beside(steps[0], 96))
                results.append(steps[1])
            total = results[0] if len(results) == 1 else jnp.concatenate(results, 0)
            found["gT", layer, c, 0] = total
            while ("dz", layer, c, 0) not in found:
                yield 1
            found["dT", layer, c, 0] = found["dz", layer, c, 0] + total
            rows = 48 if c == 3 else 96
            kept = [beside(trend_hid[layer, u, : 2 * rows, :], 96) for u in UNITS[c]]
            d_tb[layer, c - 1] += dot_nt(jnp.concatenate(gs, 1), jnp.concatenate(kept, 1))
            yield 1
            kept = [beside(trend_src[layer, u, :rows, :], 48) for u in UNITS[c]]
            d_ta[layer, c - 1] += dot_nt(jnp.concatenate(kept, 1), jnp.concatenate(dps, 1))

        def season(c):
            key = ("dz", layer, 3, 0) if c == 3 else ("dS", layer, c, 0)
            while key not in found:
                yield 1
            gs, dps = [], []
            for j, u in enumerate(UNITS[c]):
                g = found[key].astype(BF16)
                if c == 1:
                    g = g[96 * j : 96 * (j + 1)]
                gs.append(beside(g, 48))
                steps = []
                for value in mixed(g, sa_t, sb_t, season_slope, u, c, True):
                    if value is not None:
                        steps.append(value)
                    yield 1
                dps.append(beside(steps[0], 48))
                found["gS", layer, c - 1, j] = steps[1]
            if c > 1:
                while ("dz", layer, c - 1, 0) not in found:
                    yield 1
                found["dS", layer, c - 1, 0] = found["dz", layer, c - 1, 0] + found["gS", layer, c - 1, 0]
            rows = 48 if c == 3 else 96
            kept = [beside(season_hid[layer, u, :rows, :], 48) for u in UNITS[c]]
            d_sb[layer, c - 1] += dot_nt(jnp.concatenate(kept, 1), jnp.concatenate(gs, 1))
            yield 1
            kept = [beside(season_src[layer, u, : 2 * rows, :], 96) for u in UNITS[c]]
            d_sa[layer, c - 1] += dot_nt(jnp.concatenate(dps, 1), jnp.concatenate(kept, 1))

        def norm(scale, height, j):
            needed = [("dz", layer, scale, j)]
            if scale < 3:
                needed.append(("gS", layer, scale, j))
            if scale > 0:
                needed.append(("gT", layer, scale, j))
            while not all(key in found for key in needed):
                yield 1
            value = found[needed[0]]
            if scale == 0:
                moved = -found[needed[1]]
                value = value + found[needed[1]]
            elif scale == 3:
                moved = found[needed[1]]
            else:
                moved = found[needed[2]] - found[needed[1]]
                value = value + found[needed[1]]
            value = value + dot(moving_t[scale, :height, :height], moved.astype(BF16)) * taps
            yield 1
            for side, start in enumerate(sides(scale, height, j)):
                d = value[:, side * LANES : (side + 1) * LANES]
                n = unit[layer, start : start + height, :]
                dn = d * n
                d_gain[layer] += fold_rows(dn)
                d_off[layer] += fold_rows(d)
                q = d * gain
                qn = dn * gain
                mean_q = dot(q.astype(BF16), mean_lanes)
                mean_qn = dot(qn.astype(BF16), mean_lanes)
                yield 1
                x = rows_of(start, height) + inverse[layer, start : start + height, :] * (
                    q - mean_q - n * mean_qn
                )
                if layer == 0:
                    grad_buf[chunk, start : start + height, :] = x.astype(BF16)
                else:
                    grad[start : start + height, :] = x
                yield 1
            found["x", layer, scale, j] = True

        for scale, height, number in (SLABS[0], SLABS[3], SLABS[1], SLABS[2]):
            for j in range(number):
                yield ffn(scale, height, j)
        for c in (1, 2, 3):
            yield trend(c)
        for c in (3, 2, 1):
            yield season(c)
        for scale, height, number in reversed(SLABS):
            for j in range(number):
                yield norm(scale, height, j)
        yield weight_grads()

    def one_chunk(chunk, carry):
        inbound_wait(0, chunk)
        found = {}
        drive([thread for layer in range(NL) for thread in forward(layer, chunk, found)])
        inbound_start(chunk + 1, jnp.where(far & (chunk < chunks - 1), chunk + 2, chunk + 1))

        results_out("forward", chunk)
        inbound_wait(1, chunk)
        found = {}
        drive([thread for layer in reversed(range(NL)) for thread in backward(layer, chunk, found)])
        results_out("backward", chunk)
        return carry

    lax.fori_loop(0, chunks, one_chunk, 0)

    for layer in range(NL):
        parts = [None] * 4
        for c in (1, 2, 3):
            count = GRAD_COUNT[c]
            fine, coarse = LENGTHS[c - 1], LENGTHS[c]
            at_season = L0 - fine
            at_trend = 2 * L0 - 2 * fine
            for k, (value, height, width, rows, row, lanes, lane, stride) in enumerate(
                (
                    (d_sa, coarse, fine, NL * SEASON_ROWS, NL * at_season + layer, LANES, 0, NL),
                    (d_sb, coarse, coarse, L0 // 2, 0, LANES, at_season, 1),
                    (d_ta, coarse, fine, L0 // 2, 0, 2 * LANES, at_trend, 1),
                    (d_tb, fine, fine, TREND_ROWS, at_trend, LANES, 0, 1),
                )
            ):
                masked = (value[layer, c - 1] * block_mask(count, height, width)).astype(BF16)
                place = selection(count * height, rows, count, height, row, True, stride).astype(BF16)
                lay = selection(count * width, lanes, count, width, lane).astype(BF16)
                found = dot(dot(place, masked).astype(BF16), lay)
                parts[k] = found if parts[k] is None else parts[k] + found
        pack[layer : layer + 1, :] = jnp.sum(d_gain[layer], 0, keepdims=True)
        pack[NL + layer : NL + layer + 1, :] = jnp.sum(d_off[layer], 0, keepdims=True)
        bias_sum = jnp.sum(d_bias[layer], 0, keepdims=True)
        pack[AT_SEASON_IN : AT_SEASON_IN + NL * SEASON_ROWS, :] += parts[0]
        row = AT_SEASON_OUT + layer * L0 // 2
        pack[row : row + L0 // 2, :] = parts[1]
        row = AT_TREND_OUT + layer * TREND_ROWS
        pack[row : row + TREND_ROWS, :] = parts[3]
        for side in range(2):
            lanes = slice(side * LANES, (side + 1) * LANES)
            row = 2 * NL + 2 * layer + side
            pack[row : row + 1, :] = bias_sum[:, lanes]
            row = AT_TREND_IN + layer * L0 + side * L0 // 2
            pack[row : row + L0 // 2, :] = parts[2][:, lanes]
            row = AT_FFN_IN + (2 * layer + side) * LANES
            pack[row : row + LANES, :] = d_win[layer, :, lanes]
            row = AT_FFN_OUT + (2 * layer + side) * LANES
            pack[row : row + LANES, :] = d_wout[layer, :, lanes].T

    plane_index = scale_index * plane_dp + place_dp
    half_rows = pack_rows // 2
    plane_rows = half_rows // plane_size

    def core_id():
        return (scale_index, position + 1 - 2 * core)

    def plane_id(index):
        return (
            lax.div(index, plane_dp),
            depth_index * (2 * plane_dp) + lax.rem(index, plane_dp) * 2 + core,
        )

    def depth_id(index):
        return (scale_index, index * (2 * plane_dp) + place_dp * 2 + core)

    def remote(src, dst, stage, slot_out, slot_in, device):
        return pltpu.make_async_remote_copy(
            src_ref=src,
            dst_ref=dst,
            send_sem=ar_send.at[stage, slot_out],
            recv_sem=ar_recv.at[stage, slot_in],
            device_id=device,
            device_id_type=MESH,
        )

    def arrived(ref, stage, slot):
        pltpu.make_async_copy(ref, ref, ar_recv.at[stage, slot]).wait()

    mine = pl.multiple_of(core * half_rows, 16)
    theirs = pl.multiple_of((1 - core) * half_rows, 16)
    first_copy = remote(pack.at[pl.ds(theirs, half_rows)], half_in, 0, 0, 0, core_id())
    first_copy.start()
    results_out("packed", 0)
    first_copy.wait_send()
    arrived(half_in, 0, 0)
    half_bf[pl.ds(mine, half_rows)] = (pack[pl.ds(mine, half_rows)] + half_in[...]).astype(BF16)

    def plane_piece(index):
        return pl.ds(pl.multiple_of(mine + index * plane_rows, 16), plane_rows)

    def plane_round(act):
        def one(k, carry):
            other = lax.rem(plane_index + k, plane_size)
            back = lax.rem(plane_index + plane_size - k, plane_size)
            act(other, back, k)
            return carry

        lax.fori_loop(1, plane_size, one, 0)

    def plane_scatter(other, back, k):
        remote(half_bf.at[plane_piece(other)], plane_in.at[k], 1, k, k, plane_id(other)).start()

    plane_round(plane_scatter)
    results_out("planed", 0)
    plane_sum = pack[plane_piece(plane_index)] + half_in[
        pl.ds(pl.multiple_of(plane_index * plane_rows, 16), plane_rows)
    ]

    def plane_wait(k, carry):
        remote(half_bf.at[plane_piece(0)], plane_in.at[k], 1, k, k, core_id()).wait_send()
        arrived(plane_in.at[k], 1, k)
        return carry

    lax.fori_loop(1, plane_size, plane_wait, 0)
    for k in range(1, plane_size):
        plane_sum = plane_sum + plane_in[k].astype(F32)
    plane_bf[...] = plane_sum.astype(BF16)

    outer = jnp.where(depth_index < 2, 0, 3)
    inner = jnp.where(depth_index < 2, 1, 2)
    own_plane = plane_piece(plane_index)
    give = remote(plane_bf, pair_in, 2, 0, 0, depth_id(outer))
    across = remote(across_out, across_in, 3, 0, 0, depth_id(3 - outer))
    back = remote(packed_out.at[own_plane], packed_out.at[own_plane], 4, 0, 0, depth_id(inner))

    @pl.when(depth_index == inner)
    def _():
        give.start()

    results_out("paired", 0)

    @pl.when(depth_index == inner)
    def _():
        give.wait_send()
        arrived(packed_out.at[own_plane], 4, 0)

    @pl.when(depth_index == outer)
    def _():
        arrived(pair_in, 2, 0)
        across_out[...] = (plane_bf[...].astype(F32) + pair_in[...].astype(F32)).astype(BF16)
        across.start()
        across.wait_send()
        arrived(across_in, 3, 0)
        packed_out[own_plane] = (across_out[...].astype(F32) + across_in[...].astype(F32)).astype(BF16)
        back.start()

    results_out("gathered", 0)

    @pl.when(depth_index == outer)
    def _():
        back.wait_send()


    def plane_gather(other, back, k):
        remote(packed_out.at[own_plane], packed_out.at[own_plane], 5, k, k, plane_id(other)).start()

    plane_round(plane_gather)

    def plane_gathered(other, back, k):
        remote(packed_out.at[own_plane], packed_out.at[own_plane], 5, k, k, core_id()).wait_send()
        arrived(packed_out.at[plane_piece(back)], 5, k)

    plane_round(plane_gathered)
    own_half = pl.ds(mine, half_rows)
    last_copy = remote(packed_out.at[own_half], packed_out.at[own_half], 6, 0, 0, core_id())
    last_copy.start()
    last_copy.wait_send()
    arrived(packed_out.at[pl.ds(theirs, half_rows)], 6, 0)

    def sent(copy, remote_copy):
        if remote_copy:
            copy.wait_send()

    each_inbound(sent, lambda copy, kind, slot, chunk: copy.wait_send(), 0, chunks)

    def finish(chunk, carry):
        for kind in range(2):
            for scale in range(4):
                home, local, remote_copy = outbound(kind, scale, chunk)

                @pl.when(home != position)
                def _():
                    remote_copy.wait_send()

            for scale in range(4):

                @pl.when((position >= bounds[scale]) & (position < bounds[scale + 1]))
                def _():
                    for slot in range(SLOTS[scale]):
                        for half in range(2):
                            first = (slot * per_device + half * half_items + chunk * ITEMS) * LENGTHS[scale]
                            ref = (mixed_out, input_grad)[kind].at[
                                pl.ds(pl.multiple_of(first, 16), SIZES[scale])
                            ]
                            pltpu.make_async_copy(ref, ref, out_recv.at[kind, chunk, slot * 2 + half]).wait()

        return carry

    lax.fori_loop(0, chunks, finish, 0)


def unpack_body(
    groups,
    tokens,
    cotangent,
    mixed,
    grad,
    packed_hbm,
    mixed_out,
    input_grad,
    *refs,
):
    finals, (packed, staged, in_sem, out_sem, small_sem) = refs[:9], refs[18:]
    (
        gain_grad,
        bias_grad,
        season_in_grad,
        season_out_grad,
        trend_in_grad,
        trend_out_grad,
        ffn_in_grad,
        ffn_bias_grad,
        ffn_out_grad,
    ) = refs[9:18]
    packed_copy = pltpu.make_async_copy(packed_hbm, packed, small_sem.at[9])
    packed_copy.start()
    padded = lax.axis_index("dp") >= 7 * groups // 8
    size = tokens.shape[0] // PIECES
    for kind, (own, other) in enumerate(((mixed, tokens), (grad, cotangent))):
        for k in range(PIECES):
            rows = pl.ds(k * size, size)
            usual = pltpu.make_async_copy(own.at[rows], staged.at[kind, rows], in_sem.at[kind, k])
            if k < PIECES // 2:
                usual.start()
            else:
                rest = pltpu.make_async_copy(other.at[rows], staged.at[kind, rows], in_sem.at[kind, k])

                @pl.when(padded)
                def _():
                    rest.start()

                @pl.when(jnp.logical_not(padded))
                def _():
                    usual.start()

    def piece_out(kind, k):
        rows = pl.ds(k * size, size)
        target = (mixed_out, input_grad)[kind]
        return pltpu.make_async_copy(staged.at[kind, rows], target.at[rows], out_sem.at[kind, k])

    packed_copy.wait()
    top = packed[0:16, :].astype(F32)
    gain_grad[...] = top[0:NL]
    bias_grad[...] = top[NL : 2 * NL]
    for layer in range(NL):
        for side in range(2):
            lanes = slice(side * LANES, (side + 1) * LANES)
            row = 2 * NL + 2 * layer + side
            ffn_bias_grad[layer : layer + 1, lanes] = top[row : row + 1]
            row = AT_FFN_IN + (2 * layer + side) * LANES
            ffn_in_grad[layer, :, lanes] = packed[row : row + LANES, :].astype(F32)
            row = AT_FFN_OUT + (2 * layer + side) * LANES
            ffn_out_grad[layer, side * LANES : (side + 1) * LANES, :] = packed[row : row + LANES, :].astype(F32)
        row = AT_SEASON_OUT + layer * L0 // 2
        season_out_grad[layer] = packed[row : row + L0 // 2, :SEASON_ROWS].astype(F32)
        row = AT_TREND_IN + layer * L0
        trend_in_grad[layer, :, :LANES] = packed[row : row + L0 // 2, :].astype(F32)
        trend_in_grad[layer, :, LANES:] = packed[
            row + L0 // 2 : row + L0, : TREND_ROWS - LANES
        ].astype(F32)
        row = AT_TREND_OUT + layer * TREND_ROWS
        trend_out_grad[layer] = packed[row : row + TREND_ROWS, :L0].astype(F32)
    season_in_grad[...] = packed[AT_SEASON_IN : AT_SEASON_IN + NL * SEASON_ROWS, :L0].astype(F32)
    small = [
        pltpu.make_async_copy(source, target, small_sem.at[k])
        for k, (source, target) in enumerate(zip(refs[9:18], finals))
    ]
    for copy in small:
        copy.start()
    for kind in range(2):
        for k in range(PIECES):
            rows = pl.ds(k * size, size)
            pltpu.make_async_copy(mixed.at[rows], staged.at[kind, rows], in_sem.at[kind, k]).wait()
            piece_out(kind, k).start()
    for copy in small:
        copy.wait()
    for kind in range(2):
        for k in range(PIECES):
            piece_out(kind, k).wait()


def body(groups, n_scale, *args):
    tokens = args[0]
    hidden = args[9].shape[2]
    per_device = tokens.shape[0] // L0
    chunks = per_device // 2 // ITEMS
    devices = groups * n_scale
    unit_rows = 16 * devices
    pack_rows = -(-USED_ROWS // unit_rows) * unit_rows
    plane_size = groups // 8 * n_scale
    plane_rows = pack_rows // 2 // plane_size
    anywhere = pl.BlockSpec(memory_space=pl.ANY)
    vmem = pl.BlockSpec(memory_space=pltpu.VMEM)
    dma = pltpu.SemaphoreType.DMA
    turned = (
        args[:5]
        + (jnp.swapaxes(args[5], 0, 1).reshape(NL * SEASON_ROWS, L0),)
        + tuple(jnp.swapaxes(member, 1, 2) for member in args[6:8])
        + args[8:]
    )
    scratch = [pltpu.VMEM(member.shape, member.dtype) for member in turned[2:]]
    scratch += [
        dma((len(turned) - 2,)),
        pltpu.VMEM((chunks, CHUNK, LANES), BF16),
        pltpu.VMEM((chunks, CHUNK, LANES), BF16),
        pltpu.VMEM((chunks, CHUNK, LANES), BF16),
        pltpu.VMEM((chunks, CHUNK, LANES), BF16),
        pltpu.VMEM((chunks, CHUNK, LANES), F32),
        pltpu.VMEM((CHUNK, LANES), F32),
        pltpu.VMEM((CHUNK, LANES), F32),
        pltpu.VMEM((CHUNK, LANES), BF16),
        pltpu.VMEM((CHUNK, hidden), BF16),
        pltpu.VMEM((NL, CHUNK, LANES), F32),
        pltpu.VMEM((NL, CHUNK, LANES), F32),
        pltpu.VMEM((NL, CHUNK, LANES), BF16),
        pltpu.VMEM((NL, CHUNK, hidden), BF16),
        pltpu.VMEM((NL, CHUNK, hidden), BF16),
        pltpu.VMEM((NL, 4, 192, 2 * LANES), BF16),
        pltpu.VMEM((NL, 4, 96, 2 * LANES), BF16),
        pltpu.VMEM((NL, 4, 96, 2 * LANES), BF16),
        pltpu.VMEM((NL, 4, 96, 2 * LANES), BF16),
        pltpu.VMEM((NL, 4, 192, 2 * LANES), BF16),
        pltpu.VMEM((NL, 4, 192, 2 * LANES), BF16),
        pltpu.VMEM((NL, 3, 96, 192), BF16),
        pltpu.VMEM((NL, 3, 96, 96), BF16),
        pltpu.VMEM((NL, 3, 192, 96), BF16),
        pltpu.VMEM((NL, 3, 192, 192), BF16),
        pltpu.VMEM((NL, 3, 192, 96), BF16),
        pltpu.VMEM((NL, 3, 96, 96), BF16),
        pltpu.VMEM((NL, 3, 96, 192), BF16),
        pltpu.VMEM((NL, 3, 192, 192), BF16),
        pltpu.VMEM((4, 192, 192), BF16),
        pltpu.VMEM((4, 192, 192), BF16),
        pltpu.VMEM((NL, hidden, LANES), BF16),
        pltpu.VMEM((NL, LANES, hidden), BF16),
        pltpu.VMEM((NL, 3, 48, 96), F32),
        pltpu.VMEM((NL, 3, 48, 48), F32),
        pltpu.VMEM((NL, 3, 48, 96), F32),
        pltpu.VMEM((NL, 3, 96, 96), F32),
        pltpu.VMEM((NL, LANES, hidden), F32),
        pltpu.VMEM((NL, LANES, hidden), F32),
        pltpu.VMEM((NL, 8, hidden), F32),
        pltpu.VMEM((NL, 8, LANES), F32),
        pltpu.VMEM((NL, 8, LANES), F32),
        pltpu.VMEM((pack_rows, LANES), F32),
        pltpu.VMEM((pack_rows // 2, LANES), F32),
        pltpu.VMEM((pack_rows, LANES), BF16),
        pltpu.VMEM((plane_size, plane_rows, LANES), BF16),
        pltpu.VMEM((plane_rows, LANES), BF16),
        pltpu.VMEM((plane_rows, LANES), BF16),
        pltpu.VMEM((plane_rows, LANES), BF16),
        pltpu.VMEM((plane_rows, LANES), BF16),
        pltpu.VMEM((2, chunks, 2, SIZES[2], LANES), BF16),
        dma((2, chunks, 2)),
        dma((2, chunks, 2)),
        dma((2, chunks, 8)),
        dma((2, chunks, 4)),
        dma((2, chunks, 4)),
        dma((2, chunks, 8)),
        dma((7, plane_size)),
        dma((7, plane_size)),
    ]
    mixed_out, input_grad, packed = pl.pallas_call(
        functools.partial(kernel_body, groups, n_scale, per_device, pack_rows),
        out_shape=[
            jax.ShapeDtypeStruct(tokens.shape, BF16),
            jax.ShapeDtypeStruct(tokens.shape, BF16),
            jax.ShapeDtypeStruct((pack_rows, LANES), BF16),
        ],
        in_specs=[anywhere] * len(turned),
        out_specs=[anywhere, anywhere, vmem],
        scratch_shapes=scratch,
        compiler_params=pltpu.CompilerParams(
            collective_id=0, has_side_effects=True, vmem_limit_bytes=58 << 20
        ),
    )(*turned)
    finals = [
        jax.ShapeDtypeStruct(shape, F32)
        for shape in (
            (NL, LANES),
            (NL, LANES),
            (NL * SEASON_ROWS, L0),
            (NL, L0 // 2, SEASON_ROWS),
            (NL, L0 // 2, TREND_ROWS),
            (NL, TREND_ROWS, L0),
            (NL, LANES, hidden),
            (NL, hidden),
            (NL, hidden, LANES),
        )
    ]
    outs = pl.pallas_call(
        functools.partial(unpack_body, groups),
        out_shape=[
            jax.ShapeDtypeStruct(tokens.shape, BF16),
            jax.ShapeDtypeStruct(tokens.shape, BF16),
            *finals,
        ],
        in_specs=[anywhere] * 5,
        out_specs=[anywhere] * 11,
        scratch_shapes=[pltpu.VMEM(member.shape, F32) for member in finals]
        + [
            pltpu.VMEM((pack_rows, LANES), BF16),
            pltpu.VMEM((2,) + tokens.shape, BF16),
            dma((2, PIECES)),
            dma((2, PIECES)),
            dma((len(finals) + 1,)),
        ],
        compiler_params=pltpu.CompilerParams(vmem_limit_bytes=58 << 20),
    )(tokens, args[1], mixed_out, input_grad, packed)
    return (
        *outs[:4],
        jnp.swapaxes(outs[4].reshape(SEASON_ROWS, NL, L0), 0, 1),
        jnp.swapaxes(outs[5], 1, 2),
        jnp.swapaxes(outs[6], 1, 2),
        *outs[7:],
    )


def solution(mesh):
    rows = P(("scale", "dp"), None)
    return jax.shard_map(
        functools.partial(body, mesh.shape["dp"], mesh.shape["scale"]),
        mesh=mesh,
        in_specs=(rows, rows, P("scale", None)) + (P(),) * 9,
        out_specs=(rows, rows) + (P(),) * 9,
        check_vma=False,
    )
```

```python
import functools

import jax
import jax.numpy as jnp
from jax import lax
from jax.experimental import pallas as pl
from jax.experimental.pallas import tpu as pltpu
from jax.sharding import PartitionSpec as P

L0 = 96
KERNEL = 25
NL = 2
SEASON_ROWS = 84
TREND_ROWS = 168
EPS = 1e-05
LANES = 128
ITEMS = 8
PAIR = 4
MESH = pl.DeviceIdType.MESH
F32 = jnp.float32
BF16 = jnp.bfloat16

LENGTHS = [L0 >> i for i in range(4)]
SIZES = [ITEMS * n for n in LENGTHS]
STARTS = [sum(SIZES[:i]) for i in range(4)]
CHUNK = sum(SIZES)
SLOTS = [1, 2, 4, 4]
SELF = [(0, 0), (0, 1), (1, 1), (3, 1)]
TILE = 480
SLABS = [(0, 192, 2), (1, 192, 1), (2, 96, 1), (3, 48, 1)]
UNITS = {1: (0, 1), 2: (2,), 3: (3,)}
WEIGHT_COUNT = {1: 2, 2: 4, 3: 4}
GRAD_COUNT = {1: 1, 2: 2, 3: 4}
DUE_FAR = {
    ("forward", 2): [(0, 0), (1, 0), (0, 1), (1, 1)],
    ("gathered", 0): [(0, 2), (1, 2)],
}
DUE_NEAR = {
    ("forward", 0): [(0, 0)],
    ("backward", 0): [(1, 0)],
    ("forward", 1): [(0, 1)],
    ("backward", 1): [(1, 1)],
    ("forward", 2): [(0, 2)],
    ("backward", 2): [(1, 2)],
}
AT_SEASON_IN = 8
AT_TREND_IN = AT_SEASON_IN + NL * SEASON_ROWS
AT_SEASON_OUT = AT_TREND_IN + NL * L0
AT_TREND_OUT = AT_SEASON_OUT + NL * L0 // 2
AT_FFN_IN = AT_TREND_OUT + NL * TREND_ROWS
AT_FFN_OUT = AT_FFN_IN + NL * 2 * LANES
USED_ROWS = AT_FFN_OUT + NL * 2 * LANES
PIECES = 4


def dot(a, b):
    return jnp.dot(a, b, preferred_element_type=F32)


def dot_nt(a, b):
    return lax.dot_general(a, b, (((1,), (1,)), ((), ())), preferred_element_type=F32)


def dot_tn(a, b):
    return lax.dot_general(a, b, (((0,), (0,)), ((), ())), preferred_element_type=F32)


def gelu_parts(v):
    cumulative = 0.5 * (1.0 + lax.erf(v * 0.7071067811865476))
    density = jnp.exp(-0.5 * (v * v)) * 0.3989422804014327
    return v * cumulative, cumulative + v * density


def iota(shape, dim):
    return lax.broadcasted_iota(jnp.int32, shape, dim)


def selection(rows, columns, count, length, base, turned=False, stride=1):
    shape = (columns, rows) if turned else (rows, columns)
    r = iota(shape, 1 if turned else 0)
    c = iota(shape, 0 if turned else 1)
    found = jnp.zeros(shape, jnp.bool_)
    for k in range(count):
        near = c == (r - k * length) * stride + base
        found = found | (near & (r >= k * length) & (r < (k + 1) * length))
    return found.astype(F32)


def block_mask(count, height, width, turned=False):
    shape = (count * width, count * height) if turned else (count * height, count * width)
    r = iota(shape, 1 if turned else 0)
    c = iota(shape, 0 if turned else 1)
    found = jnp.zeros(shape, jnp.bool_)
    for k in range(count):
        found = found | (
            (r >= k * height) & (r < (k + 1) * height) & (c >= k * width) & (c < (k + 1) * width)
        )
    return found.astype(F32)


def moving_counts(count, length, turned):
    size = count * length
    t = iota((size, size), 1 if turned else 0)
    u = iota((size, size), 0 if turned else 1)
    total = jnp.zeros((size, size), F32)
    half = (KERNEL - 1) // 2
    for k in range(count):
        low, high = k * length, (k + 1) * length - 1
        inside = (t >= low) & (t <= high) & (u >= low) & (u <= high)
        near = (jnp.abs(t - u) <= half).astype(F32)
        first = jnp.where(u == low, jnp.maximum(half - (t - low), 0), 0).astype(F32)
        last = jnp.where(u == high, jnp.maximum(half - (high - t), 0), 0).astype(F32)
        total = total + jnp.where(inside, near + first + last, 0.0)
    return total


def beside(value, height):
    return jnp.concatenate([value[k : k + height] for k in range(0, value.shape[0], height)], 1)


def drive(threads):
    active = list(threads)
    while active:
        rest = []
        for thread in active:
            if next(thread, None) is not None:
                rest.append(thread)
        active = rest


def fold_rows(value):
    return jnp.sum(value.reshape(-1, 8, value.shape[-1]), 0)


def group_of(groups, scale, slot, position):
    bounds = [0, groups // 2, 3 * groups // 4, 7 * groups // 8]
    offsets = [0, groups // 4, groups // 8, 3 * groups // 8]
    return position - bounds[scale] + offsets[slot]


def home_of(groups, scale, group):
    if scale == 0:
        return group, 0
    if scale == 1:
        return groups // 2 + lax.rem(group, groups // 4), lax.div(group, groups // 4)
    part = lax.div(group, groups // 8)
    slot = jnp.where(part == 1, 2, jnp.where(part == 2, 1, part))
    first = 3 * groups // 4 if scale == 2 else 7 * groups // 8
    return first + lax.rem(group, groups // 8), slot


def kernel_body(
    groups,
    n_scale,
    per_device,
    pack_rows,
    tokens,
    cotangent,
    item_mask_hbm,
    ln_gain_hbm,
    ln_bias_hbm,
    season_in_hbm,
    season_out_hbm,
    trend_in_hbm,
    trend_out_hbm,
    ffn_in_hbm,
    ffn_bias_hbm,
    ffn_out_hbm,
    mixed_out,
    input_grad,
    packed_out,
    item_mask,
    ln_gain,
    ln_bias,
    season_in,
    season_out,
    trend_in,
    trend_out,
    ffn_in,
    ffn_bias,
    ffn_out,
    param_sem,
    tok_buf,
    cot_buf,
    out_buf,
    grad_buf,
    live,
    field,
    grad,
    df_keep,
    da_keep,
    unit,
    inverse,
    z_keep,
    hidden,
    slope,
    season_src,
    trend_src,
    season_hid,
    season_slope,
    trend_hid,
    trend_slope,
    sa,
    sb,
    ta,
    tb,
    sa_t,
    sb_t,
    ta_t,
    tb_t,
    moving,
    moving_t,
    win_t,
    wout_t,
    d_sa,
    d_sb,
    d_ta,
    d_tb,
    d_win,
    d_wout,
    d_bias,
    d_gain,
    d_off,
    pack,
    half_in,
    half_bf,
    plane_in,
    plane_bf,
    pair_in,
    across_out,
    across_in,
    pad_sem,
    relay_buf,
    relay_send,
    relay_recv,
    in_send,
    in_recv,
    out_send,
    out_recv,
    ar_send,
    ar_recv,
):
    scale_index = lax.axis_index("scale")
    position = lax.axis_index("dp")
    worker_group = lax.rem(position, groups // 2)
    worker_half = lax.div(position, groups // 2)
    half_items = per_device // 2
    chunks = half_items // ITEMS
    bounds = [0, groups // 2, 3 * groups // 4, 7 * groups // 8, groups]

    params = [
        pltpu.make_async_copy(source, target, param_sem.at[k])
        for k, (source, target) in enumerate(
            (
                (item_mask_hbm, item_mask),
                (ln_gain_hbm, ln_gain),
                (ln_bias_hbm, ln_bias),
                (season_in_hbm, season_in),
                (season_out_hbm, season_out),
                (trend_in_hbm, trend_in),
                (trend_out_hbm, trend_out),
                (ffn_in_hbm, ffn_in),
                (ffn_bias_hbm, ffn_bias),
                (ffn_out_hbm, ffn_out),
            )
        )
    ]

    barrier = pltpu.get_barrier_semaphore()

    plane_dp = groups // 8
    plane_size = plane_dp * n_scale
    core = lax.rem(position, 2)
    place_dp = lax.rem(lax.div(position, 2), plane_dp)
    depth_index = lax.div(position, 2 * plane_dp)

    def greet(device):
        pl.semaphore_signal(barrier, inc=1, device_id=device, device_id_type=MESH)

    def greet_row(k, carry):
        greet((scale_index, lax.rem(position + k, groups)))
        return carry

    def greet_plane(k, carry):
        other = lax.rem(scale_index + 1 + lax.div(k, plane_dp), n_scale)
        greet((other, (depth_index * plane_dp + lax.rem(k, plane_dp)) * 2 + core))
        return carry

    lax.fori_loop(1, groups, greet_row, 0)
    lax.fori_loop(0, (n_scale - 1) * plane_dp, greet_plane, 0)
    pl.semaphore_wait(barrier, groups - 1 + (n_scale - 1) * plane_dp)

    def relayed(scale, slot, half):
        return half == 0 and ((scale == 2 and slot >= 2) or (scale == 3 and slot < 2))

    def inbound(kind, scale, slot, half, chunk):
        source = (tokens, cotangent)[kind]
        target = (tok_buf, cot_buf)[kind]
        length, size = LENGTHS[scale], SIZES[scale]
        first = (slot * per_device + half * half_items + chunk * ITEMS) * length
        src = source.at[pl.ds(pl.multiple_of(first, 16), size)]
        dst = target.at[chunk, pl.ds(STARTS[scale], size)]
        recv = in_recv.at[kind, chunk, scale]
        if (slot, half) == SELF[scale]:
            return pltpu.make_async_copy(src, dst, recv), False
        owner = half * (groups // 2) + group_of(groups, scale, slot, position)
        if relayed(scale, slot, half):
            owner = position + (groups // 8 if scale == 2 else -(groups // 8))
            dst = relay_buf.at[kind, chunk, slot % 2, pl.ds(0, size)]
            recv = relay_recv.at[kind, chunk, slot % 2]
        return (
            pltpu.make_async_remote_copy(
                src_ref=src,
                dst_ref=dst,
                send_sem=in_send.at[kind, chunk, slot * 2 + half],
                recv_sem=recv,
                device_id=(scale_index, owner),
                device_id_type=MESH,
            ),
            True,
        )

    def relay(kind, scale, slot, chunk):
        length, size = LENGTHS[scale], SIZES[scale]
        src = relay_buf.at[kind, chunk, slot % 2, pl.ds(0, size)]
        target = (tok_buf, cot_buf)[kind]
        partner = position + (groups // 8 if scale == 3 else -(groups // 8))
        return pltpu.make_async_remote_copy(
            src_ref=src,
            dst_ref=target.at[chunk, pl.ds(STARTS[scale], size)],
            send_sem=relay_send.at[kind, chunk, slot % 2],
            recv_sem=in_recv.at[kind, chunk, scale],
            device_id=(scale_index, group_of(groups, scale, slot, partner)),
            device_id_type=MESH,
        )

    def order(scale):
        moves = [(kind, slot, half) for kind in range(2) for slot in range(SLOTS[scale]) for half in (1, 0)]
        return sorted(moves, key=lambda move: (move[0], not relayed(scale, move[1], move[2])))

    def each_inbound(act, act_relay, low, high):
        for scale in range(4):

            @pl.when((position >= bounds[scale]) & (position < bounds[scale + 1]))
            def _():
                def one_chunk(chunk, carry):
                    for kind, slot, half in order(scale):
                        act(*inbound(kind, scale, slot, half, chunk))
                    if scale >= 2:
                        other = 5 - scale
                        for kind in range(2):
                            for slot in range(4):
                                if relayed(other, slot, 0):
                                    act_relay(relay(kind, other, slot, chunk), kind, slot, chunk)
                    return carry

                lax.fori_loop(low, high, one_chunk, 0)

    def pass_on(copy, kind, slot, chunk):
        size = SIZES[2 if slot >= 2 else 3]
        ref = relay_buf.at[kind, chunk, slot % 2, pl.ds(0, size)]
        pltpu.make_async_copy(ref, ref, relay_recv.at[kind, chunk, slot % 2]).wait()
        copy.start()

    def inbound_start(low, high):
        each_inbound(lambda copy, remote: copy.start(), pass_on, low, high)

    far = (position < groups // 4) | (position >= bounds[2])
    inbound_start(0, jnp.where(far, 1, chunks))
    for copy in params:
        copy.start()
    for copy in params:
        copy.wait()

    def inbound_wait(kind, chunk):
        target = (tok_buf, cot_buf)[kind]
        for scale in range(4):
            ref = target.at[chunk, pl.ds(STARTS[scale], SIZES[scale])]
            pltpu.make_async_copy(ref, ref, in_recv.at[kind, chunk, scale]).wait()

    pad_rows = SLOTS[3] * per_device * LENGTHS[3]

    def padding():
        rows = pl.ds(pad_rows, tokens.shape[0] - pad_rows)
        return [
            pltpu.make_async_copy(tokens.at[rows], mixed_out.at[rows], pad_sem.at[0]),
            pltpu.make_async_copy(cotangent.at[rows], input_grad.at[rows], pad_sem.at[1]),
        ]

    @pl.when(position >= bounds[3])
    def _():
        for copy in padding():
            copy.start()

    def outbound(kind, scale, chunk):
        source = (out_buf, grad_buf)[kind]
        target = (mixed_out, input_grad)[kind]
        home, slot = home_of(groups, scale, worker_group)
        length, size = LENGTHS[scale], SIZES[scale]
        first = (slot * per_device + worker_half * half_items + chunk * ITEMS) * length
        src = source.at[chunk, pl.ds(STARTS[scale], size)]
        dst = target.at[pl.ds(pl.multiple_of(first, 16), size)]
        recv = out_recv.at[kind, chunk, slot * 2 + worker_half]
        local = pltpu.make_async_copy(src, dst, recv)
        remote = pltpu.make_async_remote_copy(
            src_ref=src,
            dst_ref=dst,
            send_sem=out_send.at[kind, chunk, scale],
            recv_sem=recv,
            device_id=(scale_index, home),
            device_id_type=MESH,
        )
        return home, local, remote

    def outbound_start(kind, chunk):
        for scale in range(4):
            home, local, remote = outbound(kind, scale, chunk)

            @pl.when(home == position)
            def _():
                local.start()

            @pl.when(home != position)
            def _():
                remote.start()

    def results_out(event, chunk):
        for is_far, due in ((True, DUE_FAR), (False, DUE_NEAR)):
            for at, sends in due.items():
                if at[0] == event:

                    @pl.when((far if is_far else jnp.logical_not(far)) & (chunk == at[1]))
                    def _():
                        for kind, done in sends:
                            outbound_start(kind, done)

    for layer in range(NL):
        for c in (1, 2, 3):
            count = WEIGHT_COUNT[c]
            fine, coarse = LENGTHS[c - 1], LENGTHS[c]
            at_season = L0 - fine
            at_trend = 2 * L0 - 2 * fine
            for whole, normal, turned, height, width, row, column, stride in (
                (season_in[...], sa, sa_t, coarse, fine, NL * at_season + layer, 0, NL),
                (season_out[layer], sb_t, sb, coarse, coarse, 0, at_season, 1),
                (trend_in[layer], ta_t, ta, coarse, fine, 0, at_trend, 1),
                (trend_out[layer], tb, tb_t, fine, fine, at_trend, 0, 1),
            ):
                rows = selection(count * height, whole.shape[0], count, height, row, stride=stride)
                columns = selection(count * width, whole.shape[1], count, width, column).astype(BF16)
                tall = dot(rows.astype(BF16), whole).astype(BF16)
                normal[layer, c - 1, : count * height, : count * width] = (
                    dot_nt(tall, columns) * block_mask(count, height, width)
                ).astype(BF16)
                turned[layer, c - 1, : count * width, : count * height] = (
                    dot_nt(columns, tall) * block_mask(count, height, width, True)
                ).astype(BF16)
        eye_in = selection(ffn_in.shape[2], ffn_in.shape[2], 1, ffn_in.shape[2], 0).astype(BF16)
        eye_out = selection(LANES, LANES, 1, LANES, 0).astype(BF16)
        win_t[layer] = dot_nt(eye_in, ffn_in[layer]).astype(BF16)
        wout_t[layer] = dot_nt(eye_out, ffn_out[layer]).astype(BF16)
    for scale, height, number in SLABS:
        for ref, is_turned in ((moving, False), (moving_t, True)):
            counts = moving_counts(height // LENGTHS[scale], LENGTHS[scale], is_turned)
            ref[scale, :height, :height] = counts.astype(BF16)
    mean_lanes = jnp.full((LANES, LANES), 1.0 / LANES, BF16)

    mask_rows = jnp.broadcast_to(item_mask[...].astype(F32), (LANES, item_mask.shape[1])).astype(BF16)
    first_item = worker_group * per_device + worker_half * half_items
    chosen = iota((32, item_mask.shape[1]), 1) == iota((32, item_mask.shape[1]), 0) + first_item
    item_live = dot_nt(chosen.astype(F32).astype(BF16), mask_rows).astype(BF16)
    for chunk in range(chunks):
        for i in range(4):
            place = (iota((SIZES[i], 32), 0).astype(F32) + 0.5) * (1.0 / LENGTHS[i])
            column = iota((SIZES[i], 32), 1).astype(F32) - float(chunk * ITEMS)
            one = ((place >= column) & (place < column + 1.0)).astype(F32).astype(BF16)
            live[chunk, STARTS[i] : STARTS[i] + SIZES[i], :] = dot(one, item_live)

    for total in (d_sa, d_sb, d_ta, d_tb, d_win, d_wout, d_bias, d_gain, d_off, pack):
        total[...] = jnp.zeros(total.shape, F32)

    taps = 1.0 / KERNEL

    def matrix(ref, layer, c, rows, columns):
        return ref[layer, c - 1, :rows, :columns]

    def sides(scale, height, j):
        half = SIZES[scale] // 2
        return [STARTS[scale] + side * half + j * height for side in range(2)]

    def forward(layer, chunk, found):
        gain = ln_gain[layer : layer + 1, :]
        offset = ln_bias[layer : layer + 1, :]
        offset_pair = jnp.concatenate([offset, offset], 1)
        bias = ffn_bias[layer : layer + 1, :]

        def rows_of(start, height):
            if layer == 0:
                return tok_buf[chunk, start : start + height, :].astype(F32)
            return field[start : start + height, :]

        def norm(scale, height, j):
            while layer > 0 and ("y", layer - 1, scale, j) not in found:
                yield 1
            parts = []
            for start in sides(scale, height, j):
                x = rows_of(start, height)
                centered = x - jnp.mean(x, -1, keepdims=True)
                yield 1
                inv = lax.rsqrt(dot((centered * centered).astype(BF16), mean_lanes) + EPS)
                n = centered * inv
                unit[layer, start : start + height, :] = n
                inverse[layer, start : start + height, :] = inv
                parts.append(n * gain)
                yield 1
            both = jnp.concatenate(parts, 1)
            average = dot(moving[scale, :height, :height], both.astype(BF16)) * taps
            found["n", layer, scale, j] = both + offset_pair
            found["s", layer, scale, j] = both - average
            found["t", layer, scale, j] = average + offset_pair

        def mixed(source, first, second, kept, hid, slp, u, layer_at, c, fine_to_coarse):
            a = source.astype(BF16)
            rows_in = a.shape[0]
            rows_out = rows_in // 2 if fine_to_coarse else rows_in * 2
            kept[layer_at, u, :rows_in, :] = a
            p = dot(matrix(first, layer_at, c, rows_out, rows_in), a)
            yield None
            h, slope_value = gelu_parts(p)
            h = h.astype(BF16)
            hid[layer_at, u, :rows_out, :] = h
            slp[layer_at, u, :rows_out, :] = slope_value.astype(BF16)
            yield None
            yield dot(matrix(second, layer_at, c, rows_out, rows_out), h)

        def season(c):
            results = []
            for j, u in enumerate(UNITS[c]):
                while ("S", layer, c - 1, j) not in found and not (
                    c == 1 and ("s", layer, 0, j) in found
                ):
                    yield 1
                source = found["s", layer, 0, j] if c == 1 else found["S", layer, c - 1, j]
                for value in mixed(
                    source, sa, sb, season_src, season_hid, season_slope, u, layer, c, True
                ):
                    if value is None:
                        yield 1
                    else:
                        results.append(value)
            mix = results[0] if len(results) == 1 else jnp.concatenate(results, 0)
            found["sm", layer, c, 0] = mix
            while ("s", layer, c, 0) not in found:
                yield 1
            found["S", layer, c, 0] = found["s", layer, c, 0] + mix

        def trend(c):
            while ("t" if c == 3 else "T", layer, c, 0) not in found:
                yield 1
            source = found["t" if c == 3 else "T", layer, c, 0]
            for j, u in enumerate(UNITS[c]):
                part = source[96 * j : 96 * (j + 1)] if c == 1 else source
                for value in mixed(part, ta, tb, trend_src, trend_hid, trend_slope, u, layer, c, False):
                    if value is None:
                        yield 1
                    else:
                        found["tm", layer, c - 1, j] = value
            if c > 1:
                while ("t", layer, c - 1, 0) not in found:
                    yield 1
                found["T", layer, c - 1, 0] = found["t", layer, c - 1, 0] + found["tm", layer, c - 1, 0]

        def ffn(scale, height, j):
            needed = [("n", layer, scale, j)]
            if scale > 0:
                needed.append(("sm", layer, scale, j))
            if scale < 3:
                needed.append(("tm", layer, scale, j))
            while not all(key in found for key in needed):
                yield 1
            value = found[needed[0]]
            for key in needed[1:]:
                value = value + found[key]
            value = value.astype(BF16)
            starts = sides(scale, height, j)
            halves = [value[:, :LANES], value[:, LANES:]]
            for start, z in zip(starts, halves):
                z_keep[layer, start : start + height, :] = z
            a = dot(jnp.concatenate(halves, 0), ffn_in[layer]) + bias
            yield 1
            h, slope_value = gelu_parts(a)
            h = h.astype(BF16)
            slope_value = slope_value.astype(BF16)
            for k, start in enumerate(starts):
                hidden[layer, start : start + height, :] = h[k * height : (k + 1) * height]
                slope[layer, start : start + height, :] = slope_value[k * height : (k + 1) * height]
            yield 1
            f = dot(h, ffn_out[layer])
            yield 1
            for k, start in enumerate(starts):
                y = rows_of(start, height) + live[chunk, start : start + height, :] * f[
                    k * height : (k + 1) * height
                ]
                if layer == NL - 1:
                    out_buf[chunk, start : start + height, :] = y.astype(BF16)
                else:
                    field[start : start + height, :] = y
            found["y", layer, scale, j] = True

        for scale, height, number in reversed(SLABS):
            for j in range(number):
                yield norm(scale, height, j)
        for c in (3, 2, 1):
            yield trend(c)
        for c in (1, 2, 3):
            yield season(c)
        for scale, height, number in (SLABS[1], SLABS[2], SLABS[0], SLABS[3]):
            for j in range(number):
                yield ffn(scale, height, j)

    def backward(layer, chunk, found):
        gain = ln_gain[layer : layer + 1, :]

        def rows_of(start, height):
            if layer == NL - 1:
                return cot_buf[chunk, start : start + height, :].astype(F32)
            return grad[start : start + height, :]

        def ffn(scale, height, j):
            while layer < NL - 1 and ("x", layer + 1, scale, j) not in found:
                yield 1
            starts = sides(scale, height, j)
            parts = []
            for start in starts:
                df = (live[chunk, start : start + height, :] * rows_of(start, height)).astype(BF16)
                df_keep[start : start + height, :] = df
                parts.append(df)
            dh = dot(jnp.concatenate(parts, 0), wout_t[layer])
            yield 1
            parts = []
            for k, start in enumerate(starts):
                da = dh[k * height : (k + 1) * height] * slope[layer, start : start + height, :].astype(F32)
                d_bias[layer] += fold_rows(da)
                da = da.astype(BF16)
                da_keep[start : start + height, :] = da
                parts.append(da)
            yield 1
            dz = dot(jnp.concatenate(parts, 0), win_t[layer])
            found["dz", layer, scale, j] = jnp.concatenate([dz[:height], dz[height:]], 1)

        def weight_grads():
            while not all(("dz", layer, scale, j) in found for scale, _, number in SLABS for j in range(number)):
                yield 1
            for t in range(0, CHUNK, TILE):
                d_win[layer] += dot_tn(z_keep[layer, t : t + TILE, :], da_keep[t : t + TILE, :])
                yield 1
                d_wout[layer] += dot_tn(df_keep[t : t + TILE, :], hidden[layer, t : t + TILE, :])
                yield 1

        def mixed(g, first_t, second_t, slp, u, c, fine_to_coarse):
            rows = g.shape[0]
            rows_out = rows * 2 if fine_to_coarse else rows // 2
            dh = dot(matrix(second_t, layer, c, rows, rows), g)
            yield None
            dp = (dh * slp[layer, u, :rows, :].astype(F32)).astype(BF16)
            yield dp
            yield dot(matrix(first_t, layer, c, rows_out, rows), dp)

        def trend(c):
            results, gs, dps = [], [], []
            for j, u in enumerate(UNITS[c]):
                key = ("dz", layer, 0, j) if c == 1 else ("dT", layer, c - 1, 0)
                while key not in found:
                    yield 1
                g = found[key].astype(BF16)
                gs.append(beside(g, 96))
                steps = []
                for value in mixed(g, ta_t, tb_t, trend_slope, u, c, False):
                    if value is not None:
                        steps.append(value)
                    yield 1
                dps.append(beside(steps[0], 96))
                results.append(steps[1])
            total = results[0] if len(results) == 1 else jnp.concatenate(results, 0)
            found["gT", layer, c, 0] = total
            while ("dz", layer, c, 0) not in found:
                yield 1
            found["dT", layer, c, 0] = found["dz", layer, c, 0] + total
            rows = 48 if c == 3 else 96
            kept = [beside(trend_hid[layer, u, : 2 * rows, :], 96) for u in UNITS[c]]
            d_tb[layer, c - 1] += dot_nt(jnp.concatenate(gs, 1), jnp.concatenate(kept, 1))
            yield 1
            kept = [beside(trend_src[layer, u, :rows, :], 48) for u in UNITS[c]]
            d_ta[layer, c - 1] += dot_nt(jnp.concatenate(kept, 1), jnp.concatenate(dps, 1))

        def season(c):
            key = ("dz", layer, 3, 0) if c == 3 else ("dS", layer, c, 0)
            while key not in found:
                yield 1
            gs, dps = [], []
            for j, u in enumerate(UNITS[c]):
                g = found[key].astype(BF16)
                if c == 1:
                    g = g[96 * j : 96 * (j + 1)]
                gs.append(beside(g, 48))
                steps = []
                for value in mixed(g, sa_t, sb_t, season_slope, u, c, True):
                    if value is not None:
                        steps.append(value)
                    yield 1
                dps.append(beside(steps[0], 48))
                found["gS", layer, c - 1, j] = steps[1]
            if c > 1:
                while ("dz", layer, c - 1, 0) not in found:
                    yield 1
                found["dS", layer, c - 1, 0] = found["dz", layer, c - 1, 0] + found["gS", layer, c - 1, 0]
            rows = 48 if c == 3 else 96
            kept = [beside(season_hid[layer, u, :rows, :], 48) for u in UNITS[c]]
            d_sb[layer, c - 1] += dot_nt(jnp.concatenate(kept, 1), jnp.concatenate(gs, 1))
            yield 1
            kept = [beside(season_src[layer, u, : 2 * rows, :], 96) for u in UNITS[c]]
            d_sa[layer, c - 1] += dot_nt(jnp.concatenate(dps, 1), jnp.concatenate(kept, 1))

        def norm(scale, height, j):
            needed = [("dz", layer, scale, j)]
            if scale < 3:
                needed.append(("gS", layer, scale, j))
            if scale > 0:
                needed.append(("gT", layer, scale, j))
            while not all(key in found for key in needed):
                yield 1
            value = found[needed[0]]
            if scale == 0:
                moved = -found[needed[1]]
                value = value + found[needed[1]]
            elif scale == 3:
                moved = found[needed[1]]
            else:
                moved = found[needed[2]] - found[needed[1]]
                value = value + found[needed[1]]
            value = value + dot(moving_t[scale, :height, :height], moved.astype(BF16)) * taps
            yield 1
            for side, start in enumerate(sides(scale, height, j)):
                d = value[:, side * LANES : (side + 1) * LANES]
                n = unit[layer, start : start + height, :]
                dn = d * n
                d_gain[layer] += fold_rows(dn)
                d_off[layer] += fold_rows(d)
                q = d * gain
                qn = dn * gain
                mean_q = dot(q.astype(BF16), mean_lanes)
                mean_qn = dot(qn.astype(BF16), mean_lanes)
                yield 1
                x = rows_of(start, height) + inverse[layer, start : start + height, :] * (
                    q - mean_q - n * mean_qn
                )
                if layer == 0:
                    grad_buf[chunk, start : start + height, :] = x.astype(BF16)
                else:
                    grad[start : start + height, :] = x
                yield 1
            found["x", layer, scale, j] = True

        for scale, height, number in (SLABS[0], SLABS[3], SLABS[1], SLABS[2]):
            for j in range(number):
                yield ffn(scale, height, j)
        for c in (1, 2, 3):
            yield trend(c)
        for c in (3, 2, 1):
            yield season(c)
        for scale, height, number in reversed(SLABS):
            for j in range(number):
                yield norm(scale, height, j)
        yield weight_grads()

    def one_chunk(chunk, carry):
        inbound_wait(0, chunk)
        found = {}
        drive([thread for layer in range(NL) for thread in forward(layer, chunk, found)])
        inbound_start(chunk + 1, jnp.where(far & (chunk < chunks - 1), chunk + 2, chunk + 1))

        results_out("forward", chunk)
        inbound_wait(1, chunk)
        found = {}
        drive([thread for layer in reversed(range(NL)) for thread in backward(layer, chunk, found)])
        results_out("backward", chunk)
        return carry

    lax.fori_loop(0, chunks, one_chunk, 0)

    for layer in range(NL):
        parts = [None] * 4
        for c in (1, 2, 3):
            count = GRAD_COUNT[c]
            fine, coarse = LENGTHS[c - 1], LENGTHS[c]
            at_season = L0 - fine
            at_trend = 2 * L0 - 2 * fine
            for k, (value, height, width, rows, row, lanes, lane, stride) in enumerate(
                (
                    (d_sa, coarse, fine, NL * SEASON_ROWS, NL * at_season + layer, LANES, 0, NL),
                    (d_sb, coarse, coarse, L0 // 2, 0, LANES, at_season, 1),
                    (d_ta, coarse, fine, L0 // 2, 0, 2 * LANES, at_trend, 1),
                    (d_tb, fine, fine, TREND_ROWS, at_trend, LANES, 0, 1),
                )
            ):
                masked = (value[layer, c - 1] * block_mask(count, height, width)).astype(BF16)
                place = selection(count * height, rows, count, height, row, True, stride).astype(BF16)
                lay = selection(count * width, lanes, count, width, lane).astype(BF16)
                found = dot(dot(place, masked).astype(BF16), lay)
                parts[k] = found if parts[k] is None else parts[k] + found
        pack[layer : layer + 1, :] = jnp.sum(d_gain[layer], 0, keepdims=True)
        pack[NL + layer : NL + layer + 1, :] = jnp.sum(d_off[layer], 0, keepdims=True)
        bias_sum = jnp.sum(d_bias[layer], 0, keepdims=True)
        pack[AT_SEASON_IN : AT_SEASON_IN + NL * SEASON_ROWS, :] += parts[0]
        row = AT_SEASON_OUT + layer * L0 // 2
        pack[row : row + L0 // 2, :] = parts[1]
        row = AT_TREND_OUT + layer * TREND_ROWS
        pack[row : row + TREND_ROWS, :] = parts[3]
        for side in range(2):
            lanes = slice(side * LANES, (side + 1) * LANES)
            row = 2 * NL + 2 * layer + side
            pack[row : row + 1, :] = bias_sum[:, lanes]
            row = AT_TREND_IN + layer * L0 + side * L0 // 2
            pack[row : row + L0 // 2, :] = parts[2][:, lanes]
            row = AT_FFN_IN + (2 * layer + side) * LANES
            pack[row : row + LANES, :] = d_win[layer, :, lanes]
            row = AT_FFN_OUT + (2 * layer + side) * LANES
            pack[row : row + LANES, :] = d_wout[layer, :, lanes].T

    plane_index = scale_index * plane_dp + place_dp
    half_rows = pack_rows // 2
    plane_rows = half_rows // plane_size

    def core_id():
        return (scale_index, position + 1 - 2 * core)

    def plane_id(index):
        return (
            lax.div(index, plane_dp),
            depth_index * (2 * plane_dp) + lax.rem(index, plane_dp) * 2 + core,
        )

    def depth_id(index):
        return (scale_index, index * (2 * plane_dp) + place_dp * 2 + core)

    def remote(src, dst, stage, slot_out, slot_in, device):
        return pltpu.make_async_remote_copy(
            src_ref=src,
            dst_ref=dst,
            send_sem=ar_send.at[stage, slot_out],
            recv_sem=ar_recv.at[stage, slot_in],
            device_id=device,
            device_id_type=MESH,
        )

    def arrived(ref, stage, slot):
        pltpu.make_async_copy(ref, ref, ar_recv.at[stage, slot]).wait()

    mine = pl.multiple_of(core * half_rows, 16)
    theirs = pl.multiple_of((1 - core) * half_rows, 16)
    first_copy = remote(pack.at[pl.ds(theirs, half_rows)], half_in, 0, 0, 0, core_id())
    first_copy.start()
    results_out("packed", 0)
    first_copy.wait_send()
    arrived(half_in, 0, 0)
    half_bf[pl.ds(mine, half_rows)] = (pack[pl.ds(mine, half_rows)] + half_in[...]).astype(BF16)

    def plane_piece(index):
        return pl.ds(pl.multiple_of(mine + index * plane_rows, 16), plane_rows)

    def plane_round(act):
        def one(k, carry):
            other = lax.rem(plane_index + k, plane_size)
            back = lax.rem(plane_index + plane_size - k, plane_size)
            act(other, back, k)
            return carry

        lax.fori_loop(1, plane_size, one, 0)

    def plane_scatter(other, back, k):
        remote(half_bf.at[plane_piece(other)], plane_in.at[k], 1, k, k, plane_id(other)).start()

    plane_round(plane_scatter)
    results_out("planed", 0)
    plane_sum = pack[plane_piece(plane_index)] + half_in[
        pl.ds(pl.multiple_of(plane_index * plane_rows, 16), plane_rows)
    ]

    def plane_wait(k, carry):
        remote(half_bf.at[plane_piece(0)], plane_in.at[k], 1, k, k, core_id()).wait_send()
        arrived(plane_in.at[k], 1, k)
        return carry

    lax.fori_loop(1, plane_size, plane_wait, 0)
    for k in range(1, plane_size):
        plane_sum = plane_sum + plane_in[k].astype(F32)
    plane_bf[...] = plane_sum.astype(BF16)

    outer = jnp.where(depth_index < 2, 0, 3)
    inner = jnp.where(depth_index < 2, 1, 2)
    own_plane = plane_piece(plane_index)
    give = remote(plane_bf, pair_in, 2, 0, 0, depth_id(outer))
    across = remote(across_out, across_in, 3, 0, 0, depth_id(3 - outer))
    back = remote(packed_out.at[own_plane], packed_out.at[own_plane], 4, 0, 0, depth_id(inner))

    @pl.when(depth_index == inner)
    def _():
        give.start()

    results_out("paired", 0)

    @pl.when(depth_index == inner)
    def _():
        give.wait_send()
        arrived(packed_out.at[own_plane], 4, 0)

    @pl.when(depth_index == outer)
    def _():
        arrived(pair_in, 2, 0)
        across_out[...] = (plane_bf[...].astype(F32) + pair_in[...].astype(F32)).astype(BF16)
        across.start()
        across.wait_send()
        arrived(across_in, 3, 0)
        packed_out[own_plane] = (across_out[...].astype(F32) + across_in[...].astype(F32)).astype(BF16)
        back.start()

    results_out("gathered", 0)

    @pl.when(depth_index == outer)
    def _():
        back.wait_send()


    def plane_gather(other, back, k):
        remote(packed_out.at[own_plane], packed_out.at[own_plane], 5, k, k, plane_id(other)).start()

    plane_round(plane_gather)

    def plane_gathered(other, back, k):
        remote(packed_out.at[own_plane], packed_out.at[own_plane], 5, k, k, core_id()).wait_send()
        arrived(packed_out.at[plane_piece(back)], 5, k)

    plane_round(plane_gathered)
    own_half = pl.ds(mine, half_rows)
    last_copy = remote(packed_out.at[own_half], packed_out.at[own_half], 6, 0, 0, core_id())
    last_copy.start()
    last_copy.wait_send()
    arrived(packed_out.at[pl.ds(theirs, half_rows)], 6, 0)

    @pl.when(position >= bounds[3])
    def _():
        for copy in padding():
            copy.wait()

    def sent(copy, remote_copy):
        if remote_copy:
            copy.wait_send()

    each_inbound(sent, lambda copy, kind, slot, chunk: copy.wait_send(), 0, chunks)

    def finish(chunk, carry):
        for kind in range(2):
            for scale in range(4):
                home, local, remote_copy = outbound(kind, scale, chunk)

                @pl.when(home != position)
                def _():
                    remote_copy.wait_send()

            for scale in range(4):

                @pl.when((position >= bounds[scale]) & (position < bounds[scale + 1]))
                def _():
                    for slot in range(SLOTS[scale]):
                        for half in range(2):
                            first = (slot * per_device + half * half_items + chunk * ITEMS) * LENGTHS[scale]
                            ref = (mixed_out, input_grad)[kind].at[
                                pl.ds(pl.multiple_of(first, 16), SIZES[scale])
                            ]
                            pltpu.make_async_copy(ref, ref, out_recv.at[kind, chunk, slot * 2 + half]).wait()

        return carry

    lax.fori_loop(0, chunks, finish, 0)


def unpack_body(mixed, grad, packed, mixed_out, input_grad, *refs):
    finals, small_sem, big_sem = refs[:9], refs[18], refs[19]
    (
        gain_grad,
        bias_grad,
        season_in_grad,
        season_out_grad,
        trend_in_grad,
        trend_out_grad,
        ffn_in_grad,
        ffn_bias_grad,
        ffn_out_grad,
    ) = refs[9:18]
    size = mixed.shape[0] // PIECES
    big = []
    for kind, (source, target) in enumerate(((mixed, mixed_out), (grad, input_grad))):
        for k in range(PIECES):
            rows = pl.ds(k * size, size)
            big.append(pltpu.make_async_copy(source.at[rows], target.at[rows], big_sem.at[kind, k]))
    for copy in big:
        copy.start()
    top = packed[0:16, :].astype(F32)
    gain_grad[...] = top[0:NL]
    bias_grad[...] = top[NL : 2 * NL]
    for layer in range(NL):
        for side in range(2):
            lanes = slice(side * LANES, (side + 1) * LANES)
            row = 2 * NL + 2 * layer + side
            ffn_bias_grad[layer : layer + 1, lanes] = top[row : row + 1]
            row = AT_FFN_IN + (2 * layer + side) * LANES
            ffn_in_grad[layer, :, lanes] = packed[row : row + LANES, :].astype(F32)
            row = AT_FFN_OUT + (2 * layer + side) * LANES
            ffn_out_grad[layer, side * LANES : (side + 1) * LANES, :] = packed[row : row + LANES, :].astype(F32)
        row = AT_SEASON_OUT + layer * L0 // 2
        season_out_grad[layer] = packed[row : row + L0 // 2, :SEASON_ROWS].astype(F32)
        row = AT_TREND_IN + layer * L0
        trend_in_grad[layer, :, :LANES] = packed[row : row + L0 // 2, :].astype(F32)
        trend_in_grad[layer, :, LANES:] = packed[
            row + L0 // 2 : row + L0, : TREND_ROWS - LANES
        ].astype(F32)
        row = AT_TREND_OUT + layer * TREND_ROWS
        trend_out_grad[layer] = packed[row : row + TREND_ROWS, :L0].astype(F32)
    season_in_grad[...] = packed[AT_SEASON_IN : AT_SEASON_IN + NL * SEASON_ROWS, :L0].astype(F32)
    small = [
        pltpu.make_async_copy(source, target, small_sem.at[k])
        for k, (source, target) in enumerate(zip(refs[9:18], finals))
    ]
    for copy in small:
        copy.start()
    for copy in small + big:
        copy.wait()


def body(groups, n_scale, *args):
    tokens = args[0]
    hidden = args[9].shape[2]
    per_device = tokens.shape[0] // L0
    chunks = per_device // 2 // ITEMS
    devices = groups * n_scale
    unit_rows = 16 * devices
    pack_rows = -(-USED_ROWS // unit_rows) * unit_rows
    plane_size = groups // 8 * n_scale
    plane_rows = pack_rows // 2 // plane_size
    anywhere = pl.BlockSpec(memory_space=pl.ANY)
    vmem = pl.BlockSpec(memory_space=pltpu.VMEM)
    dma = pltpu.SemaphoreType.DMA
    turned = (
        args[:5]
        + (jnp.swapaxes(args[5], 0, 1).reshape(NL * SEASON_ROWS, L0),)
        + tuple(jnp.swapaxes(member, 1, 2) for member in args[6:8])
        + args[8:]
    )
    scratch = [pltpu.VMEM(member.shape, member.dtype) for member in turned[2:]]
    scratch += [
        dma((len(turned) - 2,)),
        pltpu.VMEM((chunks, CHUNK, LANES), BF16),
        pltpu.VMEM((chunks, CHUNK, LANES), BF16),
        pltpu.VMEM((chunks, CHUNK, LANES), BF16),
        pltpu.VMEM((chunks, CHUNK, LANES), BF16),
        pltpu.VMEM((chunks, CHUNK, LANES), F32),
        pltpu.VMEM((CHUNK, LANES), F32),
        pltpu.VMEM((CHUNK, LANES), F32),
        pltpu.VMEM((CHUNK, LANES), BF16),
        pltpu.VMEM((CHUNK, hidden), BF16),
        pltpu.VMEM((NL, CHUNK, LANES), F32),
        pltpu.VMEM((NL, CHUNK, LANES), F32),
        pltpu.VMEM((NL, CHUNK, LANES), BF16),
        pltpu.VMEM((NL, CHUNK, hidden), BF16),
        pltpu.VMEM((NL, CHUNK, hidden), BF16),
        pltpu.VMEM((NL, 4, 192, 2 * LANES), BF16),
        pltpu.VMEM((NL, 4, 96, 2 * LANES), BF16),
        pltpu.VMEM((NL, 4, 96, 2 * LANES), BF16),
        pltpu.VMEM((NL, 4, 96, 2 * LANES), BF16),
        pltpu.VMEM((NL, 4, 192, 2 * LANES), BF16),
        pltpu.VMEM((NL, 4, 192, 2 * LANES), BF16),
        pltpu.VMEM((NL, 3, 96, 192), BF16),
        pltpu.VMEM((NL, 3, 96, 96), BF16),
        pltpu.VMEM((NL, 3, 192, 96), BF16),
        pltpu.VMEM((NL, 3, 192, 192), BF16),
        pltpu.VMEM((NL, 3, 192, 96), BF16),
        pltpu.VMEM((NL, 3, 96, 96), BF16),
        pltpu.VMEM((NL, 3, 96, 192), BF16),
        pltpu.VMEM((NL, 3, 192, 192), BF16),
        pltpu.VMEM((4, 192, 192), BF16),
        pltpu.VMEM((4, 192, 192), BF16),
        pltpu.VMEM((NL, hidden, LANES), BF16),
        pltpu.VMEM((NL, LANES, hidden), BF16),
        pltpu.VMEM((NL, 3, 48, 96), F32),
        pltpu.VMEM((NL, 3, 48, 48), F32),
        pltpu.VMEM((NL, 3, 48, 96), F32),
        pltpu.VMEM((NL, 3, 96, 96), F32),
        pltpu.VMEM((NL, LANES, hidden), F32),
        pltpu.VMEM((NL, LANES, hidden), F32),
        pltpu.VMEM((NL, 8, hidden), F32),
        pltpu.VMEM((NL, 8, LANES), F32),
        pltpu.VMEM((NL, 8, LANES), F32),
        pltpu.VMEM((pack_rows, LANES), F32),
        pltpu.VMEM((pack_rows // 2, LANES), F32),
        pltpu.VMEM((pack_rows, LANES), BF16),
        pltpu.VMEM((plane_size, plane_rows, LANES), BF16),
        pltpu.VMEM((plane_rows, LANES), BF16),
        pltpu.VMEM((plane_rows, LANES), BF16),
        pltpu.VMEM((plane_rows, LANES), BF16),
        pltpu.VMEM((plane_rows, LANES), BF16),
        dma((2,)),
        pltpu.VMEM((2, chunks, 2, SIZES[2], LANES), BF16),
        dma((2, chunks, 2)),
        dma((2, chunks, 2)),
        dma((2, chunks, 8)),
        dma((2, chunks, 4)),
        dma((2, chunks, 4)),
        dma((2, chunks, 8)),
        dma((7, plane_size)),
        dma((7, plane_size)),
    ]
    mixed_out, input_grad, packed = pl.pallas_call(
        functools.partial(kernel_body, groups, n_scale, per_device, pack_rows),
        out_shape=[
            pltpu.VMEM(tokens.shape, BF16),
            pltpu.VMEM(tokens.shape, BF16),
            pltpu.VMEM((pack_rows, LANES), BF16),
        ],
        in_specs=[anywhere] * len(turned),
        out_specs=[vmem, vmem, vmem],
        scratch_shapes=scratch,
        compiler_params=pltpu.CompilerParams(
            collective_id=0, has_side_effects=True, vmem_limit_bytes=58 << 20
        ),
    )(*turned)
    finals = [
        jax.ShapeDtypeStruct(shape, F32)
        for shape in (
            (NL, LANES),
            (NL, LANES),
            (NL * SEASON_ROWS, L0),
            (NL, L0 // 2, SEASON_ROWS),
            (NL, L0 // 2, TREND_ROWS),
            (NL, TREND_ROWS, L0),
            (NL, LANES, hidden),
            (NL, hidden),
            (NL, hidden, LANES),
        )
    ]
    outs = pl.pallas_call(
        unpack_body,
        out_shape=[
            jax.ShapeDtypeStruct(tokens.shape, BF16),
            jax.ShapeDtypeStruct(tokens.shape, BF16),
            *finals,
        ],
        in_specs=[vmem] * 3,
        out_specs=[anywhere] * 11,
        scratch_shapes=[pltpu.VMEM(member.shape, F32) for member in finals]
        + [dma((len(finals),)), dma((2, PIECES))],
        compiler_params=pltpu.CompilerParams(vmem_limit_bytes=16 << 20),
    )(*(pltpu.with_memory_space_constraint(member, pltpu.VMEM) for member in (mixed_out, input_grad, packed)))
    return (
        *outs[:4],
        jnp.swapaxes(outs[4].reshape(SEASON_ROWS, NL, L0), 0, 1),
        jnp.swapaxes(outs[5], 1, 2),
        jnp.swapaxes(outs[6], 1, 2),
        *outs[7:],
    )


def solution(mesh):
    rows = P(("scale", "dp"), None)
    return jax.shard_map(
        functools.partial(body, mesh.shape["dp"], mesh.shape["scale"]),
        mesh=mesh,
        in_specs=(rows, rows, P("scale", None)) + (P(),) * 9,
        out_specs=(rows, rows) + (P(),) * 9,
        check_vma=False,
    )
```

```python
import functools

import jax
import jax.numpy as jnp
from jax import lax
from jax.experimental import pallas as pl
from jax.experimental.pallas import tpu as pltpu
from jax.sharding import PartitionSpec as P

L0 = 96
KERNEL = 25
NL = 2
SEASON_ROWS = 84
TREND_ROWS = 168
EPS = 1e-05
LANES = 128
ITEMS = 8
PAIR = 4
MESH = pl.DeviceIdType.MESH
F32 = jnp.float32
BF16 = jnp.bfloat16

LENGTHS = [L0 >> i for i in range(4)]
SIZES = [ITEMS * n for n in LENGTHS]
STARTS = [sum(SIZES[:i]) for i in range(4)]
CHUNK = sum(SIZES)
SLOTS = [1, 2, 4, 4]
SELF = [(0, 0), (0, 1), (1, 1), (3, 1)]
TILE = 480
SLABS = [(0, 192, 2), (1, 192, 1), (2, 96, 1), (3, 48, 1)]
UNITS = {1: (0, 1), 2: (2,), 3: (3,)}
WEIGHT_COUNT = {1: 2, 2: 4, 3: 4}
GRAD_COUNT = {1: 1, 2: 2, 3: 4}
AT_SEASON_IN = 8
AT_TREND_IN = AT_SEASON_IN + NL * SEASON_ROWS
AT_SEASON_OUT = AT_TREND_IN + NL * L0
AT_TREND_OUT = AT_SEASON_OUT + NL * L0 // 2
AT_FFN_IN = AT_TREND_OUT + NL * TREND_ROWS
AT_FFN_OUT = AT_FFN_IN + NL * 2 * LANES
USED_ROWS = AT_FFN_OUT + NL * 2 * LANES
PIECES = 4
FIRST_STEPS = 3


def dot(a, b):
    return jnp.dot(a, b, preferred_element_type=F32)


def dot_nt(a, b):
    return lax.dot_general(a, b, (((1,), (1,)), ((), ())), preferred_element_type=F32)


def dot_tn(a, b):
    return lax.dot_general(a, b, (((0,), (0,)), ((), ())), preferred_element_type=F32)


def gelu_parts(v):
    cumulative = 0.5 * (1.0 + lax.erf(v * 0.7071067811865476))
    density = jnp.exp(-0.5 * (v * v)) * 0.3989422804014327
    return v * cumulative, cumulative + v * density


def iota(shape, dim):
    return lax.broadcasted_iota(jnp.int32, shape, dim)


def selection(rows, columns, count, length, base, turned=False, stride=1):
    shape = (columns, rows) if turned else (rows, columns)
    r = iota(shape, 1 if turned else 0)
    c = iota(shape, 0 if turned else 1)
    found = jnp.zeros(shape, jnp.bool_)
    for k in range(count):
        near = c == (r - k * length) * stride + base
        found = found | (near & (r >= k * length) & (r < (k + 1) * length))
    return found.astype(F32)


def block_mask(count, height, width, turned=False):
    shape = (count * width, count * height) if turned else (count * height, count * width)
    r = iota(shape, 1 if turned else 0)
    c = iota(shape, 0 if turned else 1)
    found = jnp.zeros(shape, jnp.bool_)
    for k in range(count):
        found = found | (
            (r >= k * height) & (r < (k + 1) * height) & (c >= k * width) & (c < (k + 1) * width)
        )
    return found.astype(F32)


def moving_counts(count, length, turned):
    size = count * length
    t = iota((size, size), 1 if turned else 0)
    u = iota((size, size), 0 if turned else 1)
    total = jnp.zeros((size, size), F32)
    half = (KERNEL - 1) // 2
    for k in range(count):
        low, high = k * length, (k + 1) * length - 1
        inside = (t >= low) & (t <= high) & (u >= low) & (u <= high)
        near = (jnp.abs(t - u) <= half).astype(F32)
        first = jnp.where(u == low, jnp.maximum(half - (t - low), 0), 0).astype(F32)
        last = jnp.where(u == high, jnp.maximum(half - (high - t), 0), 0).astype(F32)
        total = total + jnp.where(inside, near + first + last, 0.0)
    return total


def beside(value, height):
    return jnp.concatenate([value[k : k + height] for k in range(0, value.shape[0], height)], 1)


def drive(threads):
    active = list(threads)
    while active:
        rest = []
        for thread in active:
            if next(thread, None) is not None:
                rest.append(thread)
        active = rest


def fold_rows(value):
    return jnp.sum(value.reshape(-1, 8, value.shape[-1]), 0)


def group_of(groups, scale, slot, position):
    bounds = [0, groups // 2, 3 * groups // 4, 7 * groups // 8]
    offsets = [0, groups // 4, groups // 8, 3 * groups // 8]
    return position - bounds[scale] + offsets[slot]


def home_of(groups, scale, group):
    if scale == 0:
        return group, 0
    if scale == 1:
        return groups // 2 + lax.rem(group, groups // 4), lax.div(group, groups // 4)
    part = lax.div(group, groups // 8)
    slot = jnp.where(part == 1, 2, jnp.where(part == 2, 1, part))
    first = 3 * groups // 4 if scale == 2 else 7 * groups // 8
    return first + lax.rem(group, groups // 8), slot


def chunk_counts(per_device):
    total = per_device // ITEMS
    return total - total // 3, total // 3


def due_results(per_device):
    lower_chunks, upper_chunks = chunk_counts(per_device)

    def at_once(count):
        return {("forward", c): [(0, c)] for c in range(count)} | {("backward", c): [(1, c)] for c in range(count)}

    last, top = lower_chunks - 1, upper_chunks - 1
    return {
        (True, False): {("forward", c + 1): [(0, c)] for c in range(last)}
        | {("backward", c): [(1, c)] for c in range(last)}
        | {("gathered", 0): [(0, last), (1, last)]},
        (False, False): at_once(lower_chunks),
        (False, True): at_once(upper_chunks) | {("backward", top): [], ("paired", 0): [(1, top)]},
        (True, True): {
            ("crossed", 0): [(kind, c) for c in range(upper_chunks) for kind in range(2)][:-1],
            ("gathered", 0): [(1, top)],
        },
    }


def kernel_body(
    groups,
    n_scale,
    per_device,
    pack_rows,
    tokens,
    cotangent,
    item_mask_hbm,
    ln_gain_hbm,
    ln_bias_hbm,
    season_in_hbm,
    season_out_hbm,
    trend_in_hbm,
    trend_out_hbm,
    ffn_in_hbm,
    ffn_bias_hbm,
    ffn_out_hbm,
    mixed_out,
    input_grad,
    packed_out,
    item_mask,
    ln_gain,
    ln_bias,
    season_in,
    season_out,
    trend_in,
    trend_out,
    ffn_in,
    ffn_bias,
    ffn_out,
    param_sem,
    tok_buf,
    cot_buf,
    out_buf,
    grad_buf,
    live,
    field,
    grad,
    df_keep,
    da_keep,
    unit_all,
    inverse_all,
    z_keep_all,
    hidden_all,
    slope_all,
    season_src_all,
    trend_src_all,
    season_hid_all,
    season_slope_all,
    trend_hid_all,
    trend_slope_all,
    sa,
    sb,
    ta,
    tb,
    sa_t,
    sb_t,
    ta_t,
    tb_t,
    moving,
    moving_t,
    win_t,
    wout_t,
    d_sa,
    d_sb,
    d_ta,
    d_tb,
    d_win,
    d_wout,
    d_bias,
    d_gain,
    d_off,
    pack,
    half_in,
    half_bf,
    plane_in,
    plane_bf,
    pair_in,
    across_out,
    across_in,
    pad_sem,
    come_down,
    relay_buf,
    relay_send,
    relay_recv,
    in_send,
    in_recv,
    out_send,
    out_recv,
    ar_send,
    ar_recv,
    *pack_refs,
):
    scale_index = lax.axis_index("scale")
    position = lax.axis_index("dp")
    worker_group = lax.rem(position, groups // 2)
    worker_half = lax.div(position, groups // 2)
    upper = position >= groups // 2
    lower_chunks, upper_chunks = chunk_counts(per_device)
    chunks = jnp.where(upper, upper_chunks, lower_chunks)
    bounds = [0, groups // 2, 3 * groups // 4, 7 * groups // 8, groups]

    masks, places, lays = pack_refs[0:4], pack_refs[4:8], pack_refs[8:12]
    params = [
        pltpu.make_async_copy(source, target, param_sem.at[k])
        for k, (source, target) in enumerate(
            (
                (item_mask_hbm, item_mask),
                (ln_gain_hbm, ln_gain),
                (ln_bias_hbm, ln_bias),
                (season_in_hbm, season_in),
                (season_out_hbm, season_out),
                (trend_in_hbm, trend_in),
                (trend_out_hbm, trend_out),
                (ffn_in_hbm, ffn_in),
                (ffn_bias_hbm, ffn_bias),
                (ffn_out_hbm, ffn_out),
            )
        )
    ]

    barrier = pltpu.get_barrier_semaphore()

    plane_dp = groups // 8
    plane_size = plane_dp * n_scale
    core = lax.rem(position, 2)
    place_dp = lax.rem(lax.div(position, 2), plane_dp)
    depth_index = lax.div(position, 2 * plane_dp)

    def greet(device):
        pl.semaphore_signal(barrier, inc=1, device_id=device, device_id_type=MESH)

    def greet_row(k, carry):
        greet((scale_index, lax.rem(position + k, groups)))
        return carry

    def greet_plane(k, carry):
        other = lax.rem(scale_index + 1 + lax.div(k, plane_dp), n_scale)
        greet((other, (depth_index * plane_dp + lax.rem(k, plane_dp)) * 2 + core))
        return carry

    lax.fori_loop(1, groups, greet_row, 0)
    lax.fori_loop(0, (n_scale - 1) * plane_dp, greet_plane, 0)
    pl.semaphore_wait(barrier, groups - 1 + (n_scale - 1) * plane_dp)

    def relayed(scale, slot, half):
        return half == 0 and ((scale == 2 and slot >= 2) or (scale == 3 and slot < 2))

    def inbound(kind, scale, slot, half, chunk):
        source = (tokens, cotangent)[kind]
        target = (tok_buf, cot_buf)[kind]
        length, size = LENGTHS[scale], SIZES[scale]
        first = (slot * per_device + (half * lower_chunks + chunk) * ITEMS) * length
        src = source.at[pl.ds(pl.multiple_of(first, 16), size)]
        dst = target.at[chunk, pl.ds(STARTS[scale], size)]
        recv = in_recv.at[kind, chunk, scale]
        if (slot, half) == SELF[scale]:
            return pltpu.make_async_copy(src, dst, recv), False
        owner = half * (groups // 2) + group_of(groups, scale, slot, position)
        if relayed(scale, slot, half):
            owner = position + (groups // 8 if scale == 2 else -(groups // 8))
            dst = relay_buf.at[kind, chunk, slot % 2, pl.ds(0, size)]
            recv = relay_recv.at[kind, chunk, slot % 2]
        return (
            pltpu.make_async_remote_copy(
                src_ref=src,
                dst_ref=dst,
                send_sem=in_send.at[kind, chunk, slot * 2 + half],
                recv_sem=recv,
                device_id=(scale_index, owner),
                device_id_type=MESH,
            ),
            True,
        )

    def relay(kind, scale, slot, chunk):
        length, size = LENGTHS[scale], SIZES[scale]
        src = relay_buf.at[kind, chunk, slot % 2, pl.ds(0, size)]
        target = (tok_buf, cot_buf)[kind]
        partner = position + (groups // 8 if scale == 3 else -(groups // 8))
        return pltpu.make_async_remote_copy(
            src_ref=src,
            dst_ref=target.at[chunk, pl.ds(STARTS[scale], size)],
            send_sem=relay_send.at[kind, chunk, slot % 2],
            recv_sem=in_recv.at[kind, chunk, scale],
            device_id=(scale_index, group_of(groups, scale, slot, partner)),
            device_id_type=MESH,
        )

    def order(scale):
        moves = [(kind, slot, half) for kind in range(2) for slot in range(SLOTS[scale]) for half in (1, 0)]
        return sorted(moves, key=lambda move: (move[0], not relayed(scale, move[1], move[2])))

    def each_inbound(act, act_relay, low, high):
        for scale in range(4):

            @pl.when((position >= bounds[scale]) & (position < bounds[scale + 1]))
            def _():
                def one_step(step, carry):
                    for kind, slot, half in order(scale):
                        chunk = step - kind

                        @pl.when((chunk >= 0) & (chunk < (upper_chunks if half else lower_chunks)))
                        def _():
                            act(*inbound(kind, scale, slot, half, chunk))

                    if scale >= 2:
                        other = 5 - scale
                        for kind in range(2):
                            chunk = step - kind

                            @pl.when((chunk >= 0) & (chunk < lower_chunks))
                            def _():
                                for slot in range(4):
                                    if relayed(other, slot, 0):
                                        act_relay(relay(kind, other, slot, chunk), kind, slot, chunk)

                    return carry

                lax.fori_loop(low, high, one_step, 0)

    def pass_on(copy, kind, slot, chunk):
        size = SIZES[2 if slot >= 2 else 3]
        ref = relay_buf.at[kind, chunk, slot % 2, pl.ds(0, size)]
        pltpu.make_async_copy(ref, ref, relay_recv.at[kind, chunk, slot % 2]).wait()
        copy.start()

    def inbound_start(low, high):
        each_inbound(lambda copy, remote: copy.start(), pass_on, low, high)

    far = (position < groups // 4) | (position >= bounds[2])
    inbound_start(0, jnp.where(far, FIRST_STEPS, lower_chunks + 1))
    for copy in params:
        copy.start()
    for copy in params:
        copy.wait()

    def inbound_wait(kind, chunk):
        target = (tok_buf, cot_buf)[kind]
        for scale in range(4):
            ref = target.at[chunk, pl.ds(STARTS[scale], SIZES[scale])]
            pltpu.make_async_copy(ref, ref, in_recv.at[kind, chunk, scale]).wait()

    pad_rows = SLOTS[3] * per_device * LENGTHS[3]

    def padding():
        rows = pl.ds(pad_rows, tokens.shape[0] - pad_rows)
        return [
            pltpu.make_async_copy(tokens.at[rows], mixed_out.at[rows], pad_sem.at[0]),
            pltpu.make_async_copy(cotangent.at[rows], input_grad.at[rows], pad_sem.at[1]),
        ]

    @pl.when(position >= bounds[3])
    def _():
        for copy in padding():
            copy.start()

    def outbound(kind, scale, chunk):
        source = (out_buf, grad_buf)[kind]
        target = (mixed_out, input_grad)[kind]
        home, slot = home_of(groups, scale, worker_group)
        length, size = LENGTHS[scale], SIZES[scale]
        first = (slot * per_device + (worker_half * lower_chunks + chunk) * ITEMS) * length
        src = source.at[chunk, pl.ds(STARTS[scale], size)]
        dst = target.at[pl.ds(pl.multiple_of(first, 16), size)]
        recv = out_recv.at[kind, chunk, slot * 2 + worker_half]
        local = pltpu.make_async_copy(src, dst, recv)
        remote = pltpu.make_async_remote_copy(
            src_ref=src,
            dst_ref=dst,
            send_sem=out_send.at[kind, chunk, scale],
            recv_sem=recv,
            device_id=(scale_index, home),
            device_id_type=MESH,
        )
        return home, local, remote

    def outbound_start(kind, chunk):
        for scale in range(4):
            home, local, remote = outbound(kind, scale, chunk)

            @pl.when(home == position)
            def _():
                local.start()

            @pl.when(home != position)
            def _():
                remote.start()

    def results_out(event, chunk):
        for (is_far, is_upper), due in due_results(per_device).items():
            for at, sends in due.items():
                if at[0] == event and sends:

                    @pl.when((far == is_far) & (upper == is_upper) & (chunk == at[1]))
                    def _():
                        for kind, done in sends:
                            outbound_start(kind, done)

    for layer in range(NL):
        for c in (1, 2, 3):
            count = WEIGHT_COUNT[c]
            fine, coarse = LENGTHS[c - 1], LENGTHS[c]
            at_season = L0 - fine
            at_trend = 2 * L0 - 2 * fine
            for whole, normal, turned, height, width, row, column, stride in (
                (season_in[...], sa, sa_t, coarse, fine, NL * at_season + layer, 0, NL),
                (season_out[layer], sb_t, sb, coarse, coarse, 0, at_season, 1),
                (trend_in[layer], ta_t, ta, coarse, fine, 0, at_trend, 1),
                (trend_out[layer], tb, tb_t, fine, fine, at_trend, 0, 1),
            ):
                rows = selection(count * height, whole.shape[0], count, height, row, stride=stride)
                columns = selection(count * width, whole.shape[1], count, width, column).astype(BF16)
                tall = dot(rows.astype(BF16), whole).astype(BF16)
                normal[layer, c - 1, : count * height, : count * width] = (
                    dot_nt(tall, columns) * block_mask(count, height, width)
                ).astype(BF16)
                turned[layer, c - 1, : count * width, : count * height] = (
                    dot_nt(columns, tall) * block_mask(count, height, width, True)
                ).astype(BF16)
        eye_in = selection(ffn_in.shape[2], ffn_in.shape[2], 1, ffn_in.shape[2], 0).astype(BF16)
        eye_out = selection(LANES, LANES, 1, LANES, 0).astype(BF16)
        win_t[layer] = dot_nt(eye_in, ffn_in[layer]).astype(BF16)
        wout_t[layer] = dot_nt(eye_out, ffn_out[layer]).astype(BF16)
    for c in (1, 2, 3):
        count = GRAD_COUNT[c]
        fine, coarse = LENGTHS[c - 1], LENGTHS[c]
        at_season = L0 - fine
        at_trend = 2 * L0 - 2 * fine
        for k, (height, width, row, lane, stride) in enumerate(
            (
                (coarse, fine, NL * at_season, 0, NL),
                (coarse, coarse, 0, at_season, 1),
                (coarse, fine, 0, at_trend, 1),
                (fine, fine, at_trend, 0, 1),
            )
        ):
            masks[k][c - 1] = block_mask(count, height, width)
            rows, lanes = places[k].shape[2], lays[k].shape[2]
            for layer in range(NL):
                start = row + layer if stride > 1 else row
                place = selection(count * height, rows, count, height, start, True, stride)
                places[k][layer, c - 1] = place.astype(BF16)
            lays[k][c - 1] = selection(count * width, lanes, count, width, lane).astype(BF16)
    for scale, height, number in SLABS:
        for ref, is_turned in ((moving, False), (moving_t, True)):
            counts = moving_counts(height // LENGTHS[scale], LENGTHS[scale], is_turned)
            ref[scale, :height, :height] = counts.astype(BF16)
    mean_lanes = jnp.full((LANES, LANES), 1.0 / LANES, BF16)

    mask_rows = jnp.broadcast_to(item_mask[...].astype(F32), (LANES, item_mask.shape[1])).astype(BF16)
    first_item = worker_group * per_device + worker_half * lower_chunks * ITEMS
    chosen = iota((32, item_mask.shape[1]), 1) == iota((32, item_mask.shape[1]), 0) + first_item
    item_live = dot_nt(chosen.astype(F32).astype(BF16), mask_rows).astype(BF16)
    for chunk in range(lower_chunks):
        for i in range(4):
            place = (iota((SIZES[i], 32), 0).astype(F32) + 0.5) * (1.0 / LENGTHS[i])
            column = iota((SIZES[i], 32), 1).astype(F32) - float(chunk * ITEMS)
            one = ((place >= column) & (place < column + 1.0)).astype(F32).astype(BF16)
            live[chunk, STARTS[i] : STARTS[i] + SIZES[i], :] = dot(one, item_live)

    for total in (d_sa, d_sb, d_ta, d_tb, d_win, d_wout, d_bias, d_gain, d_off, pack):
        total[...] = jnp.zeros(total.shape, F32)

    taps = 1.0 / KERNEL

    def matrix(ref, layer, c, rows, columns):
        return ref[layer, c - 1, :rows, :columns]

    def sides(scale, height, j):
        half = SIZES[scale] // 2
        return [STARTS[scale] + side * half + j * height for side in range(2)]

    def kept_of(chunk):
        return [
            ref.at[lax.rem(chunk, 2)]
            for ref in (
                unit_all,
                inverse_all,
                z_keep_all,
                hidden_all,
                slope_all,
                season_src_all,
                trend_src_all,
                season_hid_all,
                season_slope_all,
                trend_hid_all,
                trend_slope_all,
            )
        ]

    def forward(layer, chunk, found):
        (
            unit,
            inverse,
            z_keep,
            hidden,
            slope,
            season_src,
            trend_src,
            season_hid,
            season_slope,
            trend_hid,
            trend_slope,
        ) = kept_of(chunk)
        gain = ln_gain[layer : layer + 1, :]
        offset = ln_bias[layer : layer + 1, :]
        offset_pair = jnp.concatenate([offset, offset], 1)
        bias = ffn_bias[layer : layer + 1, :]

        def rows_of(start, height):
            if layer == 0:
                return tok_buf[chunk, start : start + height, :].astype(F32)
            return field[start : start + height, :]

        def norm(scale, height, j):
            while layer > 0 and ("y", layer - 1, scale, j) not in found:
                yield 1
            parts = []
            for start in sides(scale, height, j):
                x = rows_of(start, height)
                centered = x - jnp.mean(x, -1, keepdims=True)
                yield 1
                inv = lax.rsqrt(dot((centered * centered).astype(BF16), mean_lanes) + EPS)
                n = centered * inv
                unit[layer, start : start + height, :] = n
                inverse[layer, start : start + height, :] = inv
                parts.append(n * gain)
                yield 1
            both = jnp.concatenate(parts, 1)
            average = dot(moving[scale, :height, :height], both.astype(BF16)) * taps
            found["n", layer, scale, j] = both + offset_pair
            found["s", layer, scale, j] = both - average
            found["t", layer, scale, j] = average + offset_pair

        def mixed(source, first, second, kept, hid, slp, u, layer_at, c, fine_to_coarse):
            a = source.astype(BF16)
            rows_in = a.shape[0]
            rows_out = rows_in // 2 if fine_to_coarse else rows_in * 2
            kept[layer_at, u, :rows_in, :] = a
            p = dot(matrix(first, layer_at, c, rows_out, rows_in), a)
            yield None
            h, slope_value = gelu_parts(p)
            h = h.astype(BF16)
            hid[layer_at, u, :rows_out, :] = h
            slp[layer_at, u, :rows_out, :] = slope_value.astype(BF16)
            yield None
            yield dot(matrix(second, layer_at, c, rows_out, rows_out), h)

        def season(c):
            results = []
            for j, u in enumerate(UNITS[c]):
                while ("S", layer, c - 1, j) not in found and not (
                    c == 1 and ("s", layer, 0, j) in found
                ):
                    yield 1
                source = found["s", layer, 0, j] if c == 1 else found["S", layer, c - 1, j]
                for value in mixed(
                    source, sa, sb, season_src, season_hid, season_slope, u, layer, c, True
                ):
                    if value is None:
                        yield 1
                    else:
                        results.append(value)
            mix = results[0] if len(results) == 1 else jnp.concatenate(results, 0)
            found["sm", layer, c, 0] = mix
            while ("s", layer, c, 0) not in found:
                yield 1
            found["S", layer, c, 0] = found["s", layer, c, 0] + mix

        def trend(c):
            while ("t" if c == 3 else "T", layer, c, 0) not in found:
                yield 1
            source = found["t" if c == 3 else "T", layer, c, 0]
            for j, u in enumerate(UNITS[c]):
                part = source[96 * j : 96 * (j + 1)] if c == 1 else source
                for value in mixed(part, ta, tb, trend_src, trend_hid, trend_slope, u, layer, c, False):
                    if value is None:
                        yield 1
                    else:
                        found["tm", layer, c - 1, j] = value
            if c > 1:
                while ("t", layer, c - 1, 0) not in found:
                    yield 1
                found["T", layer, c - 1, 0] = found["t", layer, c - 1, 0] + found["tm", layer, c - 1, 0]

        def ffn(scale, height, j):
            needed = [("n", layer, scale, j)]
            if scale > 0:
                needed.append(("sm", layer, scale, j))
            if scale < 3:
                needed.append(("tm", layer, scale, j))
            while not all(key in found for key in needed):
                yield 1
            value = found[needed[0]]
            for key in needed[1:]:
                value = value + found[key]
            value = value.astype(BF16)
            starts = sides(scale, height, j)
            halves = [value[:, :LANES], value[:, LANES:]]
            for start, z in zip(starts, halves):
                z_keep[layer, start : start + height, :] = z
            a = dot(jnp.concatenate(halves, 0), ffn_in[layer]) + bias
            yield 1
            h, slope_value = gelu_parts(a)
            h = h.astype(BF16)
            slope_value = slope_value.astype(BF16)
            for k, start in enumerate(starts):
                hidden[layer, start : start + height, :] = h[k * height : (k + 1) * height]
                slope[layer, start : start + height, :] = slope_value[k * height : (k + 1) * height]
            yield 1
            f = dot(h, ffn_out[layer])
            yield 1
            for k, start in enumerate(starts):
                y = rows_of(start, height) + live[chunk, start : start + height, :] * f[
                    k * height : (k + 1) * height
                ]
                if layer == NL - 1:
                    out_buf[chunk, start : start + height, :] = y.astype(BF16)
                else:
                    field[start : start + height, :] = y
            found["y", layer, scale, j] = True

        for scale, height, number in reversed(SLABS):
            for j in range(number):
                yield norm(scale, height, j)
        for c in (3, 2, 1):
            yield trend(c)
        for c in (1, 2, 3):
            yield season(c)
        for scale, height, number in (SLABS[1], SLABS[2], SLABS[0], SLABS[3]):
            for j in range(number):
                yield ffn(scale, height, j)

    def backward(layer, chunk, found):
        (
            unit,
            inverse,
            z_keep,
            hidden,
            slope,
            season_src,
            trend_src,
            season_hid,
            season_slope,
            trend_hid,
            trend_slope,
        ) = kept_of(chunk)
        gain = ln_gain[layer : layer + 1, :]

        def rows_of(start, height):
            if layer == NL - 1:
                return cot_buf[chunk, start : start + height, :].astype(F32)
            return grad[start : start + height, :]

        def ffn(scale, height, j):
            while layer < NL - 1 and ("x", layer + 1, scale, j) not in found:
                yield 1
            starts = sides(scale, height, j)
            parts = []
            for start in starts:
                df = (live[chunk, start : start + height, :] * rows_of(start, height)).astype(BF16)
                df_keep[start : start + height, :] = df
                parts.append(df)
            dh = dot(jnp.concatenate(parts, 0), wout_t[layer])
            yield 1
            parts = []
            for k, start in enumerate(starts):
                da = dh[k * height : (k + 1) * height] * slope[layer, start : start + height, :].astype(F32)
                d_bias[layer] += fold_rows(da)
                da = da.astype(BF16)
                da_keep[start : start + height, :] = da
                parts.append(da)
            yield 1
            dz = dot(jnp.concatenate(parts, 0), win_t[layer])
            found["dz", layer, scale, j] = jnp.concatenate([dz[:height], dz[height:]], 1)

        def weight_grads():
            while not all(("dz", layer, scale, j) in found for scale, _, number in SLABS for j in range(number)):
                yield 1
            for t in range(0, CHUNK, TILE):
                d_win[layer] += dot_tn(z_keep[layer, t : t + TILE, :], da_keep[t : t + TILE, :])
                yield 1
                d_wout[layer] += dot_tn(df_keep[t : t + TILE, :], hidden[layer, t : t + TILE, :])
                yield 1

        def mixed(g, first_t, second_t, slp, u, c, fine_to_coarse):
            rows = g.shape[0]
            rows_out = rows * 2 if fine_to_coarse else rows // 2
            dh = dot(matrix(second_t, layer, c, rows, rows), g)
            yield None
            dp = (dh * slp[layer, u, :rows, :].astype(F32)).astype(BF16)
            yield dp
            yield dot(matrix(first_t, layer, c, rows_out, rows), dp)

        def trend(c):
            results, gs, dps = [], [], []
            for j, u in enumerate(UNITS[c]):
                key = ("dz", layer, 0, j) if c == 1 else ("dT", layer, c - 1, 0)
                while key not in found:
                    yield 1
                g = found[key].astype(BF16)
                gs.append(beside(g, 96))
                steps = []
                for value in mixed(g, ta_t, tb_t, trend_slope, u, c, False):
                    if value is not None:
                        steps.append(value)
                    yield 1
                dps.append(beside(steps[0], 96))
                results.append(steps[1])
            total = results[0] if len(results) == 1 else jnp.concatenate(results, 0)
            found["gT", layer, c, 0] = total
            while ("dz", layer, c, 0) not in found:
                yield 1
            found["dT", layer, c, 0] = found["dz", layer, c, 0] + total
            rows = 48 if c == 3 else 96
            kept = [beside(trend_hid[layer, u, : 2 * rows, :], 96) for u in UNITS[c]]
            d_tb[layer, c - 1] += dot_nt(jnp.concatenate(gs, 1), jnp.concatenate(kept, 1))
            yield 1
            kept = [beside(trend_src[layer, u, :rows, :], 48) for u in UNITS[c]]
            d_ta[layer, c - 1] += dot_nt(jnp.concatenate(kept, 1), jnp.concatenate(dps, 1))

        def season(c):
            key = ("dz", layer, 3, 0) if c == 3 else ("dS", layer, c, 0)
            while key not in found:
                yield 1
            gs, dps = [], []
            for j, u in enumerate(UNITS[c]):
                g = found[key].astype(BF16)
                if c == 1:
                    g = g[96 * j : 96 * (j + 1)]
                gs.append(beside(g, 48))
                steps = []
                for value in mixed(g, sa_t, sb_t, season_slope, u, c, True):
                    if value is not None:
                        steps.append(value)
                    yield 1
                dps.append(beside(steps[0], 48))
                found["gS", layer, c - 1, j] = steps[1]
            if c > 1:
                while ("dz", layer, c - 1, 0) not in found:
                    yield 1
                found["dS", layer, c - 1, 0] = found["dz", layer, c - 1, 0] + found["gS", layer, c - 1, 0]
            rows = 48 if c == 3 else 96
            kept = [beside(season_hid[layer, u, :rows, :], 48) for u in UNITS[c]]
            d_sb[layer, c - 1] += dot_nt(jnp.concatenate(kept, 1), jnp.concatenate(gs, 1))
            yield 1
            kept = [beside(season_src[layer, u, : 2 * rows, :], 96) for u in UNITS[c]]
            d_sa[layer, c - 1] += dot_nt(jnp.concatenate(dps, 1), jnp.concatenate(kept, 1))

        def norm(scale, height, j):
            needed = [("dz", layer, scale, j)]
            if scale < 3:
                needed.append(("gS", layer, scale, j))
            if scale > 0:
                needed.append(("gT", layer, scale, j))
            while not all(key in found for key in needed):
                yield 1
            value = found[needed[0]]
            if scale == 0:
                moved = -found[needed[1]]
                value = value + found[needed[1]]
            elif scale == 3:
                moved = found[needed[1]]
            else:
                moved = found[needed[2]] - found[needed[1]]
                value = value + found[needed[1]]
            value = value + dot(moving_t[scale, :height, :height], moved.astype(BF16)) * taps
            yield 1
            for side, start in enumerate(sides(scale, height, j)):
                d = value[:, side * LANES : (side + 1) * LANES]
                n = unit[layer, start : start + height, :]
                dn = d * n
                d_gain[layer] += fold_rows(dn)
                d_off[layer] += fold_rows(d)
                q = d * gain
                qn = dn * gain
                mean_q = dot(q.astype(BF16), mean_lanes)
                mean_qn = dot(qn.astype(BF16), mean_lanes)
                yield 1
                x = rows_of(start, height) + inverse[layer, start : start + height, :] * (
                    q - mean_q - n * mean_qn
                )
                if layer == 0:
                    grad_buf[chunk, start : start + height, :] = x.astype(BF16)
                else:
                    grad[start : start + height, :] = x
                yield 1
            found["x", layer, scale, j] = True

        for scale, height, number in (SLABS[0], SLABS[3], SLABS[1], SLABS[2]):
            for j in range(number):
                yield ffn(scale, height, j)
        for c in (1, 2, 3):
            yield trend(c)
        for c in (3, 2, 1):
            yield season(c)
        for scale, height, number in reversed(SLABS):
            for j in range(number):
                yield norm(scale, height, j)
        yield weight_grads()

    def one_step(step, carry):
        @pl.when(step < chunks)
        def _():
            inbound_wait(0, step)
            found = {}
            drive([thread for layer in range(NL) for thread in forward(layer, step, found)])
            later = step + FIRST_STEPS
            inbound_start(later, jnp.where(far & (later <= lower_chunks), later + 1, later))
            results_out("forward", step)

        @pl.when(step > 0)
        def _():
            chunk = step - 1
            inbound_wait(1, chunk)

            @pl.when(jnp.logical_not(upper | far) & (chunk == lower_chunks - 1))
            def _():
                pl.semaphore_signal(
                    come_down,
                    inc=1,
                    device_id=(scale_index, position + groups // 2),
                    device_id_type=MESH,
                )

            found = {}
            drive([thread for layer in reversed(range(NL)) for thread in backward(layer, chunk, found)])
            results_out("backward", chunk)

        return carry

    lax.fori_loop(0, chunks + 1, one_step, 0)
    rest = chunks + FIRST_STEPS
    inbound_start(rest, jnp.where(far & upper, lower_chunks + 1, rest))

    for layer in range(NL):
        parts = [None] * 4
        for c in (1, 2, 3):
            for k, value in enumerate((d_sa, d_sb, d_ta, d_tb)):
                masked = (value[layer, c - 1] * masks[k][c - 1]).astype(BF16)
                found = dot(dot(places[k][layer, c - 1], masked).astype(BF16), lays[k][c - 1])
                parts[k] = found if parts[k] is None else parts[k] + found
        pack[layer : layer + 1, :] = jnp.sum(d_gain[layer], 0, keepdims=True)
        pack[NL + layer : NL + layer + 1, :] = jnp.sum(d_off[layer], 0, keepdims=True)
        bias_sum = jnp.sum(d_bias[layer], 0, keepdims=True)
        pack[AT_SEASON_IN : AT_SEASON_IN + NL * SEASON_ROWS, :] += parts[0]
        row = AT_SEASON_OUT + layer * L0 // 2
        pack[row : row + L0 // 2, :] = parts[1]
        row = AT_TREND_OUT + layer * TREND_ROWS
        pack[row : row + TREND_ROWS, :] = parts[3]
        for side in range(2):
            lanes = slice(side * LANES, (side + 1) * LANES)
            row = 2 * NL + 2 * layer + side
            pack[row : row + 1, :] = bias_sum[:, lanes]
            row = AT_TREND_IN + layer * L0 + side * L0 // 2
            pack[row : row + L0 // 2, :] = parts[2][:, lanes]
            row = AT_FFN_IN + (2 * layer + side) * LANES
            pack[row : row + LANES, :] = d_win[layer, :, lanes]
            row = AT_FFN_OUT + (2 * layer + side) * LANES
            pack[row : row + LANES, :] = d_wout[layer, :, lanes].T

    plane_index = scale_index * plane_dp + place_dp
    half_rows = pack_rows // 2
    plane_rows = half_rows // plane_size

    def core_id():
        return (scale_index, position + 1 - 2 * core)

    def plane_id(index):
        return (
            lax.div(index, plane_dp),
            depth_index * (2 * plane_dp) + lax.rem(index, plane_dp) * 2 + core,
        )

    def depth_id(index):
        return (scale_index, index * (2 * plane_dp) + place_dp * 2 + core)

    def remote(src, dst, stage, slot_out, slot_in, device):
        return pltpu.make_async_remote_copy(
            src_ref=src,
            dst_ref=dst,
            send_sem=ar_send.at[stage, slot_out],
            recv_sem=ar_recv.at[stage, slot_in],
            device_id=device,
            device_id_type=MESH,
        )

    def arrived(ref, stage, slot):
        pltpu.make_async_copy(ref, ref, ar_recv.at[stage, slot]).wait()

    mine = pl.multiple_of(core * half_rows, 16)
    theirs = pl.multiple_of((1 - core) * half_rows, 16)
    first_copy = remote(pack.at[pl.ds(theirs, half_rows)], half_in, 0, 0, 0, core_id())
    first_copy.start()
    results_out("packed", 0)
    first_copy.wait_send()
    arrived(half_in, 0, 0)
    half_bf[pl.ds(mine, half_rows)] = (pack[pl.ds(mine, half_rows)] + half_in[...]).astype(BF16)

    def plane_piece(index):
        return pl.ds(pl.multiple_of(mine + index * plane_rows, 16), plane_rows)

    def plane_round(act):
        def one(k, carry):
            other = lax.rem(plane_index + k, plane_size)
            back = lax.rem(plane_index + plane_size - k, plane_size)
            act(other, back, k)
            return carry

        lax.fori_loop(1, plane_size, one, 0)

    def plane_scatter(other, back, k):
        remote(half_bf.at[plane_piece(other)], plane_in.at[k], 1, k, k, plane_id(other)).start()

    plane_round(plane_scatter)
    results_out("planed", 0)
    plane_sum = pack[plane_piece(plane_index)] + half_in[
        pl.ds(pl.multiple_of(plane_index * plane_rows, 16), plane_rows)
    ]

    def plane_wait(k, carry):
        remote(half_bf.at[plane_piece(0)], plane_in.at[k], 1, k, k, core_id()).wait_send()
        arrived(plane_in.at[k], 1, k)
        return carry

    lax.fori_loop(1, plane_size, plane_wait, 0)
    for k in range(1, plane_size):
        plane_sum = plane_sum + plane_in[k].astype(F32)
    plane_bf[...] = plane_sum.astype(BF16)

    outer = jnp.where(depth_index < 2, 0, 3)
    inner = jnp.where(depth_index < 2, 1, 2)
    own_plane = plane_piece(plane_index)
    give = remote(plane_bf, pair_in, 2, 0, 0, depth_id(outer))
    across = remote(across_out, across_in, 3, 0, 0, depth_id(3 - outer))
    back = remote(packed_out.at[own_plane], packed_out.at[own_plane], 4, 0, 0, depth_id(inner))

    @pl.when(depth_index == inner)
    def _():
        give.start()

    results_out("paired", 0)

    @pl.when(depth_index == inner)
    def _():
        give.wait_send()
        arrived(packed_out.at[own_plane], 4, 0)

    @pl.when(depth_index == outer)
    def _():
        arrived(pair_in, 2, 0)
        across_out[...] = (plane_bf[...].astype(F32) + pair_in[...].astype(F32)).astype(BF16)
        across.start()

    @pl.when(far & upper)
    def _():
        pl.semaphore_wait(come_down, 1)

    results_out("crossed", 0)

    @pl.when(depth_index == outer)
    def _():
        across.wait_send()
        arrived(across_in, 3, 0)
        packed_out[own_plane] = (across_out[...].astype(F32) + across_in[...].astype(F32)).astype(BF16)
        back.start()

    results_out("gathered", 0)

    @pl.when(depth_index == outer)
    def _():
        back.wait_send()


    def plane_gather(other, back, k):
        remote(packed_out.at[own_plane], packed_out.at[own_plane], 5, k, k, plane_id(other)).start()

    plane_round(plane_gather)

    def plane_gathered(other, back, k):
        remote(packed_out.at[own_plane], packed_out.at[own_plane], 5, k, k, core_id()).wait_send()
        arrived(packed_out.at[plane_piece(back)], 5, k)

    plane_round(plane_gathered)
    own_half = pl.ds(mine, half_rows)
    last_copy = remote(packed_out.at[own_half], packed_out.at[own_half], 6, 0, 0, core_id())
    last_copy.start()
    last_copy.wait_send()
    arrived(packed_out.at[pl.ds(theirs, half_rows)], 6, 0)

    @pl.when(position >= bounds[3])
    def _():
        for copy in padding():
            copy.wait()

    def sent(copy, remote_copy):
        if remote_copy:
            copy.wait_send()

    each_inbound(sent, lambda copy, kind, slot, chunk: copy.wait_send(), 0, lower_chunks + 1)

    def finish(chunk, carry):
        for kind in range(2):
            for scale in range(4):
                home, local, remote_copy = outbound(kind, scale, chunk)

                @pl.when((home != position) & (chunk < chunks))
                def _():
                    remote_copy.wait_send()

            for scale in range(4):

                @pl.when((position >= bounds[scale]) & (position < bounds[scale + 1]))
                def _():
                    for slot in range(SLOTS[scale]):
                        for half in range(2):

                            @pl.when(chunk < (upper_chunks if half else lower_chunks))
                            def _():
                                place = half * lower_chunks + chunk
                                first = (slot * per_device + place * ITEMS) * LENGTHS[scale]
                                ref = (mixed_out, input_grad)[kind].at[
                                    pl.ds(pl.multiple_of(first, 16), SIZES[scale])
                                ]
                                sem = out_recv.at[kind, chunk, slot * 2 + half]
                                pltpu.make_async_copy(ref, ref, sem).wait()

        return carry

    lax.fori_loop(0, lower_chunks, finish, 0)


def unpack_body(mixed, grad, packed, mixed_out, input_grad, *refs):
    finals, small_sem, big_sem = refs[:9], refs[18], refs[19]
    (
        gain_grad,
        bias_grad,
        season_in_grad,
        season_out_grad,
        trend_in_grad,
        trend_out_grad,
        ffn_in_grad,
        ffn_bias_grad,
        ffn_out_grad,
    ) = refs[9:18]
    size = mixed.shape[0] // PIECES
    big = []
    for kind, (source, target) in enumerate(((mixed, mixed_out), (grad, input_grad))):
        for k in range(PIECES):
            rows = pl.ds(k * size, size)
            big.append(pltpu.make_async_copy(source.at[rows], target.at[rows], big_sem.at[kind, k]))
    for copy in big:
        copy.start()
    top = packed[0:16, :].astype(F32)
    gain_grad[...] = top[0:NL]
    bias_grad[...] = top[NL : 2 * NL]
    for layer in range(NL):
        for side in range(2):
            lanes = slice(side * LANES, (side + 1) * LANES)
            row = 2 * NL + 2 * layer + side
            ffn_bias_grad[layer : layer + 1, lanes] = top[row : row + 1]
            row = AT_FFN_IN + (2 * layer + side) * LANES
            ffn_in_grad[layer, :, lanes] = packed[row : row + LANES, :].astype(F32)
            row = AT_FFN_OUT + (2 * layer + side) * LANES
            ffn_out_grad[layer, side * LANES : (side + 1) * LANES, :] = packed[row : row + LANES, :].astype(F32)
        row = AT_SEASON_OUT + layer * L0 // 2
        season_out_grad[layer] = packed[row : row + L0 // 2, :SEASON_ROWS].astype(F32)
        row = AT_TREND_IN + layer * L0
        trend_in_grad[layer, :, :LANES] = packed[row : row + L0 // 2, :].astype(F32)
        trend_in_grad[layer, :, LANES:] = packed[
            row + L0 // 2 : row + L0, : TREND_ROWS - LANES
        ].astype(F32)
        row = AT_TREND_OUT + layer * TREND_ROWS
        trend_out_grad[layer] = packed[row : row + TREND_ROWS, :L0].astype(F32)
    season_in_grad[...] = packed[AT_SEASON_IN : AT_SEASON_IN + NL * SEASON_ROWS, :L0].astype(F32)
    small = [
        pltpu.make_async_copy(source, target, small_sem.at[k])
        for k, (source, target) in enumerate(zip(refs[9:18], finals))
    ]
    for copy in small:
        copy.start()
    for copy in small + big:
        copy.wait()


def body(groups, n_scale, *args):
    tokens = args[0]
    hidden = args[9].shape[2]
    per_device = tokens.shape[0] // L0
    chunks = max(chunk_counts(per_device))
    unit_rows = 16 * 2 * (groups // 8) * n_scale
    pack_rows = -(-USED_ROWS // unit_rows) * unit_rows
    plane_size = groups // 8 * n_scale
    plane_rows = pack_rows // 2 // plane_size
    anywhere = pl.BlockSpec(memory_space=pl.ANY)
    vmem = pl.BlockSpec(memory_space=pltpu.VMEM)
    dma = pltpu.SemaphoreType.DMA
    turned = (
        args[:5]
        + (jnp.swapaxes(args[5], 0, 1).reshape(NL * SEASON_ROWS, L0),)
        + tuple(jnp.swapaxes(member, 1, 2) for member in args[6:8])
        + args[8:]
    )
    scratch = [pltpu.VMEM(member.shape, member.dtype) for member in turned[2:]]
    scratch += [
        dma((len(turned) - 2,)),
        pltpu.VMEM((chunks, CHUNK, LANES), BF16),
        pltpu.VMEM((chunks, CHUNK, LANES), BF16),
        pltpu.VMEM((chunks, CHUNK, LANES), BF16),
        pltpu.VMEM((chunks, CHUNK, LANES), BF16),
        pltpu.VMEM((chunks, CHUNK, LANES), F32),
        pltpu.VMEM((CHUNK, LANES), F32),
        pltpu.VMEM((CHUNK, LANES), F32),
        pltpu.VMEM((CHUNK, LANES), BF16),
        pltpu.VMEM((CHUNK, hidden), BF16),
        pltpu.VMEM((2, NL, CHUNK, LANES), F32),
        pltpu.VMEM((2, NL, CHUNK, LANES), F32),
        pltpu.VMEM((2, NL, CHUNK, LANES), BF16),
        pltpu.VMEM((2, NL, CHUNK, hidden), BF16),
        pltpu.VMEM((2, NL, CHUNK, hidden), BF16),
        pltpu.VMEM((2, NL, 4, 192, 2 * LANES), BF16),
        pltpu.VMEM((2, NL, 4, 96, 2 * LANES), BF16),
        pltpu.VMEM((2, NL, 4, 96, 2 * LANES), BF16),
        pltpu.VMEM((2, NL, 4, 96, 2 * LANES), BF16),
        pltpu.VMEM((2, NL, 4, 192, 2 * LANES), BF16),
        pltpu.VMEM((2, NL, 4, 192, 2 * LANES), BF16),
        pltpu.VMEM((NL, 3, 96, 192), BF16),
        pltpu.VMEM((NL, 3, 96, 96), BF16),
        pltpu.VMEM((NL, 3, 192, 96), BF16),
        pltpu.VMEM((NL, 3, 192, 192), BF16),
        pltpu.VMEM((NL, 3, 192, 96), BF16),
        pltpu.VMEM((NL, 3, 96, 96), BF16),
        pltpu.VMEM((NL, 3, 96, 192), BF16),
        pltpu.VMEM((NL, 3, 192, 192), BF16),
        pltpu.VMEM((4, 192, 192), BF16),
        pltpu.VMEM((4, 192, 192), BF16),
        pltpu.VMEM((NL, hidden, LANES), BF16),
        pltpu.VMEM((NL, LANES, hidden), BF16),
        pltpu.VMEM((NL, 3, 48, 96), F32),
        pltpu.VMEM((NL, 3, 48, 48), F32),
        pltpu.VMEM((NL, 3, 48, 96), F32),
        pltpu.VMEM((NL, 3, 96, 96), F32),
        pltpu.VMEM((NL, LANES, hidden), F32),
        pltpu.VMEM((NL, LANES, hidden), F32),
        pltpu.VMEM((NL, 8, hidden), F32),
        pltpu.VMEM((NL, 8, LANES), F32),
        pltpu.VMEM((NL, 8, LANES), F32),
        pltpu.VMEM((pack_rows, LANES), F32),
        pltpu.VMEM((pack_rows // 2, LANES), F32),
        pltpu.VMEM((pack_rows, LANES), BF16),
        pltpu.VMEM((plane_size, plane_rows, LANES), BF16),
        pltpu.VMEM((plane_rows, LANES), BF16),
        pltpu.VMEM((plane_rows, LANES), BF16),
        pltpu.VMEM((plane_rows, LANES), BF16),
        pltpu.VMEM((plane_rows, LANES), BF16),
        dma((2,)),
        pltpu.SemaphoreType.REGULAR,
        pltpu.VMEM((2, chunks, 2, SIZES[2], LANES), BF16),
        dma((2, chunks, 2)),
        dma((2, chunks, 2)),
        dma((2, chunks, 8)),
        dma((2, chunks, 4)),
        dma((2, chunks, 4)),
        dma((2, chunks, 8)),
        dma((7, plane_size)),
        dma((7, plane_size)),
        pltpu.VMEM((3, 48, 96), F32),
        pltpu.VMEM((3, 48, 48), F32),
        pltpu.VMEM((3, 48, 96), F32),
        pltpu.VMEM((3, 96, 96), F32),
        pltpu.VMEM((NL, 3, NL * SEASON_ROWS, 48), BF16),
        pltpu.VMEM((NL, 3, L0 // 2, 48), BF16),
        pltpu.VMEM((NL, 3, L0 // 2, 48), BF16),
        pltpu.VMEM((NL, 3, TREND_ROWS, 96), BF16),
        pltpu.VMEM((3, 96, LANES), BF16),
        pltpu.VMEM((3, 48, LANES), BF16),
        pltpu.VMEM((3, 96, 2 * LANES), BF16),
        pltpu.VMEM((3, 96, LANES), BF16),
    ]
    mixed_out, input_grad, packed = pl.pallas_call(
        functools.partial(kernel_body, groups, n_scale, per_device, pack_rows),
        out_shape=[
            pltpu.VMEM(tokens.shape, BF16),
            pltpu.VMEM(tokens.shape, BF16),
            pltpu.VMEM((pack_rows, LANES), BF16),
        ],
        in_specs=[anywhere] * len(turned),
        out_specs=[vmem, vmem, vmem],
        scratch_shapes=scratch,
        compiler_params=pltpu.CompilerParams(
            collective_id=0, has_side_effects=True, vmem_limit_bytes=58 << 20
        ),
    )(*turned)
    finals = [
        jax.ShapeDtypeStruct(shape, F32)
        for shape in (
            (NL, LANES),
            (NL, LANES),
            (NL * SEASON_ROWS, L0),
            (NL, L0 // 2, SEASON_ROWS),
            (NL, L0 // 2, TREND_ROWS),
            (NL, TREND_ROWS, L0),
            (NL, LANES, hidden),
            (NL, hidden),
            (NL, hidden, LANES),
        )
    ]
    outs = pl.pallas_call(
        unpack_body,
        out_shape=[
            jax.ShapeDtypeStruct(tokens.shape, BF16),
            jax.ShapeDtypeStruct(tokens.shape, BF16),
            *finals,
        ],
        in_specs=[vmem] * 3,
        out_specs=[anywhere] * 11,
        scratch_shapes=[pltpu.VMEM(member.shape, F32) for member in finals]
        + [dma((len(finals),)), dma((2, PIECES))],
        compiler_params=pltpu.CompilerParams(vmem_limit_bytes=16 << 20),
    )(*(pltpu.with_memory_space_constraint(member, pltpu.VMEM) for member in (mixed_out, input_grad, packed)))
    return (
        *outs[:4],
        jnp.swapaxes(outs[4].reshape(SEASON_ROWS, NL, L0), 0, 1),
        jnp.swapaxes(outs[5], 1, 2),
        jnp.swapaxes(outs[6], 1, 2),
        *outs[7:],
    )


def solution(mesh):
    rows = P(("scale", "dp"), None)
    return jax.shard_map(
        functools.partial(body, mesh.shape["dp"], mesh.shape["scale"]),
        mesh=mesh,
        in_specs=(rows, rows, P("scale", None)) + (P(),) * 9,
        out_specs=(rows, rows) + (P(),) * 9,
        check_vma=False,
    )
```

```python
import functools

import jax
import jax.numpy as jnp
from jax import lax
from jax.experimental import pallas as pl
from jax.experimental.pallas import tpu as pltpu
from jax.sharding import PartitionSpec as P

L0 = 96
KERNEL = 25
NL = 2
SEASON_ROWS = 84
TREND_ROWS = 168
EPS = 1e-05
LANES = 128
ITEMS = 8
PAIR = 4
MESH = pl.DeviceIdType.MESH
F32 = jnp.float32
BF16 = jnp.bfloat16

LENGTHS = [L0 >> i for i in range(4)]
SIZES = [ITEMS * n for n in LENGTHS]
STARTS = [sum(SIZES[:i]) for i in range(4)]
CHUNK = sum(SIZES)
SLOTS = [1, 2, 4, 4]
SELF = [(0, 0), (0, 1), (1, 1), (3, 1)]
TILE = 480
SLABS = [(0, 192, 2), (1, 192, 1), (2, 96, 1), (3, 48, 1)]
UNITS = {1: (0, 1), 2: (2,), 3: (3,)}
WEIGHT_COUNT = {1: 2, 2: 4, 3: 4}
GRAD_COUNT = {1: 1, 2: 2, 3: 4}
AT_SEASON_IN = 16
AT_TREND_IN = AT_SEASON_IN + 176
AT_SEASON_OUT = AT_TREND_IN + NL * L0
AT_TREND_OUT = AT_SEASON_OUT + NL * L0 // 2
TREND_STEP = 176
AT_FFN_IN = AT_TREND_OUT + NL * TREND_STEP
AT_FFN_OUT = AT_FFN_IN + NL * 2 * LANES
USED_ROWS = AT_FFN_OUT + NL * 2 * LANES
PIECES = 4
FIRST_STEPS = 3


def dot(a, b):
    return jnp.dot(a, b, preferred_element_type=F32)


def dot_nt(a, b):
    return lax.dot_general(a, b, (((1,), (1,)), ((), ())), preferred_element_type=F32)


def dot_tn(a, b):
    return lax.dot_general(a, b, (((0,), (0,)), ((), ())), preferred_element_type=F32)


def gelu_parts(v):
    cumulative = 0.5 * (1.0 + lax.erf(v * 0.7071067811865476))
    density = jnp.exp(-0.5 * (v * v)) * 0.3989422804014327
    return v * cumulative, cumulative + v * density


def iota(shape, dim):
    return lax.broadcasted_iota(jnp.int32, shape, dim)


def selection(rows, columns, count, length, base, turned=False, stride=1):
    shape = (columns, rows) if turned else (rows, columns)
    r = iota(shape, 1 if turned else 0)
    c = iota(shape, 0 if turned else 1)
    found = jnp.zeros(shape, jnp.bool_)
    for k in range(count):
        near = c == (r - k * length) * stride + base
        found = found | (near & (r >= k * length) & (r < (k + 1) * length))
    return found.astype(F32)


def block_mask(count, height, width, turned=False):
    shape = (count * width, count * height) if turned else (count * height, count * width)
    r = iota(shape, 1 if turned else 0)
    c = iota(shape, 0 if turned else 1)
    found = jnp.zeros(shape, jnp.bool_)
    for k in range(count):
        found = found | (
            (r >= k * height) & (r < (k + 1) * height) & (c >= k * width) & (c < (k + 1) * width)
        )
    return found.astype(F32)


def moving_counts(count, length, turned):
    size = count * length
    t = iota((size, size), 1 if turned else 0)
    u = iota((size, size), 0 if turned else 1)
    total = jnp.zeros((size, size), F32)
    half = (KERNEL - 1) // 2
    for k in range(count):
        low, high = k * length, (k + 1) * length - 1
        inside = (t >= low) & (t <= high) & (u >= low) & (u <= high)
        near = (jnp.abs(t - u) <= half).astype(F32)
        first = jnp.where(u == low, jnp.maximum(half - (t - low), 0), 0).astype(F32)
        last = jnp.where(u == high, jnp.maximum(half - (high - t), 0), 0).astype(F32)
        total = total + jnp.where(inside, near + first + last, 0.0)
    return total


def beside(value, height):
    return jnp.concatenate([value[k : k + height] for k in range(0, value.shape[0], height)], 1)


def drive(threads):
    active = list(threads)
    while active:
        rest = []
        for thread in active:
            if next(thread, None) is not None:
                rest.append(thread)
        active = rest


def fold_rows(value):
    return jnp.sum(value.reshape(-1, 8, value.shape[-1]), 0)


def group_of(groups, scale, slot, position):
    bounds = [0, groups // 2, 3 * groups // 4, 7 * groups // 8]
    offsets = [0, groups // 4, groups // 8, 3 * groups // 8]
    return position - bounds[scale] + offsets[slot]


def home_of(groups, scale, group):
    if scale == 0:
        return group, 0
    if scale == 1:
        return groups // 2 + lax.rem(group, groups // 4), lax.div(group, groups // 4)
    part = lax.div(group, groups // 8)
    slot = jnp.where(part == 1, 2, jnp.where(part == 2, 1, part))
    first = 3 * groups // 4 if scale == 2 else 7 * groups // 8
    return first + lax.rem(group, groups // 8), slot


def chunk_counts(per_device):
    total = per_device // ITEMS
    return total - total // 3, total // 3


def due_results(per_device):
    lower_chunks, upper_chunks = chunk_counts(per_device)

    def at_once(count):
        return {("forward", c): [(0, c)] for c in range(count)} | {("backward", c): [(1, c)] for c in range(count)}

    last, top = lower_chunks - 1, upper_chunks - 1
    return {
        (True, False): {("forward", c + 1): [(0, c)] for c in range(last)}
        | {("backward", c): [(1, c)] for c in range(last)}
        | {("forward", last): [(0, last - 1), (0, last)], ("gathered", 0): [(1, last)]},
        (False, False): at_once(lower_chunks) | {("backward", last): [], ("paired", 0): [(1, last)]},
        (False, True): at_once(upper_chunks) | {("backward", top): [], ("paired", 0): [(1, top)]},
        (True, True): {
            ("crossed", 0): [(kind, c) for c in range(upper_chunks) for kind in range(2)][:-1],
            ("gathered", 0): [(1, top)],
        },
    }


def kernel_body(
    groups,
    n_scale,
    per_device,
    pack_rows,
    tokens,
    cotangent,
    item_mask_hbm,
    ln_gain_hbm,
    ln_bias_hbm,
    season_in,
    season_out_hbm,
    trend_in_hbm,
    trend_out_hbm,
    ffn_in_hbm,
    ffn_bias_hbm,
    ffn_out_hbm,
    mixed_out,
    input_grad,
    packed_out,
    item_mask,
    ln_gain,
    ln_bias,
    season_out,
    trend_in,
    trend_out,
    ffn_in,
    ffn_bias,
    ffn_out,
    param_sem,
    tok_buf,
    cot_buf,
    out_buf,
    grad_buf,
    live,
    field,
    grad,
    df_keep,
    da_keep,
    unit_all,
    inverse_all,
    z_keep_all,
    hidden_all,
    slope_all,
    season_src_all,
    trend_src_all,
    season_hid_all,
    season_slope_all,
    trend_hid_all,
    trend_slope_all,
    sa,
    sb,
    ta,
    tb,
    sa_t,
    sb_t,
    ta_t,
    tb_t,
    moving,
    moving_t,
    win_t,
    wout_t,
    d_sa,
    d_sb,
    d_ta,
    d_tb,
    d_win,
    d_wout,
    d_bias,
    d_gain,
    d_off,
    pack,
    half_in,
    half_bf,
    plane_in,
    plane_bf,
    pair_in,
    across_out,
    across_in,
    pad_sem,
    come_down,
    relay_buf,
    relay_send,
    relay_recv,
    in_send,
    in_recv,
    out_send,
    out_recv,
    ar_send,
    ar_recv,
    *pack_refs,
):
    scale_index = lax.axis_index("scale")
    position = lax.axis_index("dp")
    worker_group = lax.rem(position, groups // 2)
    worker_half = lax.div(position, groups // 2)
    upper = position >= groups // 2
    lower_chunks, upper_chunks = chunk_counts(per_device)
    chunks = jnp.where(upper, upper_chunks, lower_chunks)
    bounds = [0, groups // 2, 3 * groups // 4, 7 * groups // 8, groups]

    masks, places, lays = pack_refs[0:4], pack_refs[4:8], pack_refs[8:12]
    params = [
        pltpu.make_async_copy(source, target, param_sem.at[k])
        for k, (source, target) in enumerate(
            (
                (item_mask_hbm, item_mask),
                (ln_gain_hbm, ln_gain),
                (ln_bias_hbm, ln_bias),
                (season_out_hbm, season_out),
                (trend_in_hbm, trend_in),
                (trend_out_hbm, trend_out),
                (ffn_in_hbm, ffn_in),
                (ffn_bias_hbm, ffn_bias),
                (ffn_out_hbm, ffn_out),
            )
        )
    ]

    barrier = pltpu.get_barrier_semaphore()

    plane_dp = groups // 8
    plane_size = plane_dp * n_scale
    core = lax.rem(position, 2)
    place_dp = lax.rem(lax.div(position, 2), plane_dp)
    depth_index = lax.div(position, 2 * plane_dp)

    def greet(device):
        pl.semaphore_signal(barrier, inc=1, device_id=device, device_id_type=MESH)

    def greet_row(k, carry):
        greet((scale_index, lax.rem(position + k, groups)))
        return carry

    def greet_plane(k, carry):
        other = lax.rem(scale_index + 1 + lax.div(k, plane_dp), n_scale)
        greet((other, (depth_index * plane_dp + lax.rem(k, plane_dp)) * 2 + core))
        return carry

    lax.fori_loop(1, groups, greet_row, 0)
    lax.fori_loop(0, (n_scale - 1) * plane_dp, greet_plane, 0)
    pl.semaphore_wait(barrier, groups - 1 + (n_scale - 1) * plane_dp)

    def relayed(scale, slot, half):
        return half == 0 and ((scale == 2 and slot >= 2) or (scale == 3 and slot < 2))

    def inbound(kind, scale, slot, half, chunk):
        source = (tokens, cotangent)[kind]
        target = (tok_buf, cot_buf)[kind]
        length, size = LENGTHS[scale], SIZES[scale]
        first = (slot * per_device + (half * lower_chunks + chunk) * ITEMS) * length
        src = source.at[pl.ds(pl.multiple_of(first, 16), size)]
        dst = target.at[chunk, pl.ds(STARTS[scale], size)]
        recv = in_recv.at[kind, chunk, scale]
        if (slot, half) == SELF[scale]:
            return pltpu.make_async_copy(src, dst, recv), False
        owner = half * (groups // 2) + group_of(groups, scale, slot, position)
        if relayed(scale, slot, half):
            owner = position + (groups // 8 if scale == 2 else -(groups // 8))
            dst = relay_buf.at[kind, chunk, slot % 2, pl.ds(0, size)]
            recv = relay_recv.at[kind, chunk, slot % 2]
        return (
            pltpu.make_async_remote_copy(
                src_ref=src,
                dst_ref=dst,
                send_sem=in_send.at[kind, chunk, slot * 2 + half],
                recv_sem=recv,
                device_id=(scale_index, owner),
                device_id_type=MESH,
            ),
            True,
        )

    def relay(kind, scale, slot, chunk):
        length, size = LENGTHS[scale], SIZES[scale]
        src = relay_buf.at[kind, chunk, slot % 2, pl.ds(0, size)]
        target = (tok_buf, cot_buf)[kind]
        partner = position + (groups // 8 if scale == 3 else -(groups // 8))
        return pltpu.make_async_remote_copy(
            src_ref=src,
            dst_ref=target.at[chunk, pl.ds(STARTS[scale], size)],
            send_sem=relay_send.at[kind, chunk, slot % 2],
            recv_sem=in_recv.at[kind, chunk, scale],
            device_id=(scale_index, group_of(groups, scale, slot, partner)),
            device_id_type=MESH,
        )

    def order(scale):
        moves = [(kind, slot, half) for kind in range(2) for slot in range(SLOTS[scale]) for half in (1, 0)]
        return sorted(moves, key=lambda move: (move[0], not relayed(scale, move[1], move[2])))

    def each_inbound(act, act_relay, low, high):
        for scale in range(4):

            @pl.when((position >= bounds[scale]) & (position < bounds[scale + 1]))
            def _():
                def one_step(step, carry):
                    for kind, slot, half in order(scale):
                        chunk = step - kind

                        @pl.when((chunk >= 0) & (chunk < (upper_chunks if half else lower_chunks)))
                        def _():
                            act(*inbound(kind, scale, slot, half, chunk))

                    if scale >= 2:
                        other = 5 - scale
                        for kind in range(2):
                            chunk = step - kind

                            @pl.when((chunk >= 0) & (chunk < lower_chunks))
                            def _():
                                for slot in range(4):
                                    if relayed(other, slot, 0):
                                        act_relay(relay(kind, other, slot, chunk), kind, slot, chunk)

                    return carry

                lax.fori_loop(low, high, one_step, 0)

    def pass_on(copy, kind, slot, chunk):
        size = SIZES[2 if slot >= 2 else 3]
        ref = relay_buf.at[kind, chunk, slot % 2, pl.ds(0, size)]
        pltpu.make_async_copy(ref, ref, relay_recv.at[kind, chunk, slot % 2]).wait()
        copy.start()

    def inbound_start(low, high):
        each_inbound(lambda copy, remote: copy.start(), pass_on, low, high)

    far = (position < groups // 4) | (position >= bounds[2])
    inbound_start(0, jnp.where(far, FIRST_STEPS, lower_chunks + 1))
    for copy in params:
        copy.start()
    for copy in params:
        copy.wait()

    def inbound_wait(kind, chunk):
        target = (tok_buf, cot_buf)[kind]
        for scale in range(4):
            ref = target.at[chunk, pl.ds(STARTS[scale], SIZES[scale])]
            pltpu.make_async_copy(ref, ref, in_recv.at[kind, chunk, scale]).wait()

    pad_rows = SLOTS[3] * per_device * LENGTHS[3]

    def padding():
        rows = pl.ds(pad_rows, tokens.shape[0] - pad_rows)
        return [
            pltpu.make_async_copy(tokens.at[rows], mixed_out.at[rows], pad_sem.at[0]),
            pltpu.make_async_copy(cotangent.at[rows], input_grad.at[rows], pad_sem.at[1]),
        ]

    @pl.when(position >= bounds[3])
    def _():
        for copy in padding():
            copy.start()

    def outbound(kind, scale, chunk):
        source = (out_buf, grad_buf)[kind]
        target = (mixed_out, input_grad)[kind]
        home, slot = home_of(groups, scale, worker_group)
        length, size = LENGTHS[scale], SIZES[scale]
        first = (slot * per_device + (worker_half * lower_chunks + chunk) * ITEMS) * length
        src = source.at[chunk, pl.ds(STARTS[scale], size)]
        dst = target.at[pl.ds(pl.multiple_of(first, 16), size)]
        recv = out_recv.at[kind, chunk, slot * 2 + worker_half]
        local = pltpu.make_async_copy(src, dst, recv)
        remote = pltpu.make_async_remote_copy(
            src_ref=src,
            dst_ref=dst,
            send_sem=out_send.at[kind, chunk, scale],
            recv_sem=recv,
            device_id=(scale_index, home),
            device_id_type=MESH,
        )
        return home, local, remote

    def outbound_start(kind, chunk):
        for scale in range(4):
            home, local, remote = outbound(kind, scale, chunk)

            @pl.when(home == position)
            def _():
                local.start()

            @pl.when(home != position)
            def _():
                remote.start()

    def results_out(event, chunk):
        for (is_far, is_upper), due in due_results(per_device).items():
            for at, sends in due.items():
                if at[0] == event and sends:

                    @pl.when((far == is_far) & (upper == is_upper) & (chunk == at[1]))
                    def _():
                        for kind, done in sends:
                            outbound_start(kind, done)

    for layer in range(NL):
        for c in (1, 2, 3):
            count = WEIGHT_COUNT[c]
            fine, coarse = LENGTHS[c - 1], LENGTHS[c]
            at_season = L0 - fine
            at_trend = 2 * L0 - 2 * fine
            for whole, normal, turned, height, width, row, column, stride in (
                (season_in[...], sa, sa_t, coarse, fine, NL * at_season + layer, 0, NL),
                (season_out[layer], sb_t, sb, coarse, coarse, 0, at_season, 1),
                (trend_in[layer], ta_t, ta, coarse, fine, 0, at_trend, 1),
                (trend_out[...], tb, tb_t, fine, fine, TREND_ROWS * layer + at_trend, 0, 1),
            ):
                rows = selection(count * height, whole.shape[0], count, height, row, stride=stride)
                columns = selection(count * width, whole.shape[1], count, width, column).astype(BF16)
                tall = dot(rows.astype(BF16), whole).astype(BF16)
                normal[layer, c - 1, : count * height, : count * width] = (
                    dot_nt(tall, columns) * block_mask(count, height, width)
                ).astype(BF16)
                turned[layer, c - 1, : count * width, : count * height] = (
                    dot_nt(columns, tall) * block_mask(count, height, width, True)
                ).astype(BF16)
        eye_in = selection(ffn_in.shape[2], ffn_in.shape[2], 1, ffn_in.shape[2], 0).astype(BF16)
        eye_out = selection(LANES, LANES, 1, LANES, 0).astype(BF16)
        win_t[layer] = dot_nt(eye_in, ffn_in[layer]).astype(BF16)
        wout_t[layer] = dot_nt(eye_out, ffn_out[layer]).astype(BF16)
    for c in (1, 2, 3):
        count = GRAD_COUNT[c]
        fine, coarse = LENGTHS[c - 1], LENGTHS[c]
        at_season = L0 - fine
        at_trend = 2 * L0 - 2 * fine
        for k, (height, width, row, lane, stride) in enumerate(
            (
                (coarse, fine, NL * at_season, 0, NL),
                (coarse, coarse, 0, at_season, 1),
                (coarse, fine, 0, at_trend, 1),
                (fine, fine, at_trend, 0, 1),
            )
        ):
            masks[k][c - 1] = block_mask(count, height, width)
            rows, lanes = places[k].shape[2], lays[k].shape[2]
            for layer in range(NL):
                start = row + layer if stride > 1 else row
                place = selection(count * height, rows, count, height, start, True, stride)
                places[k][layer, c - 1] = place.astype(BF16)
            lays[k][c - 1] = selection(count * width, lanes, count, width, lane).astype(BF16)
    for scale, height, number in SLABS:
        for ref, is_turned in ((moving, False), (moving_t, True)):
            counts = moving_counts(height // LENGTHS[scale], LENGTHS[scale], is_turned)
            ref[scale, :height, :height] = counts.astype(BF16)
    mean_lanes = jnp.full((LANES, LANES), 1.0 / LANES, BF16)

    mask_rows = jnp.broadcast_to(item_mask[...].astype(F32), (LANES, item_mask.shape[1])).astype(BF16)
    first_item = worker_group * per_device + worker_half * lower_chunks * ITEMS
    chosen = iota((32, item_mask.shape[1]), 1) == iota((32, item_mask.shape[1]), 0) + first_item
    item_live = dot_nt(chosen.astype(F32).astype(BF16), mask_rows).astype(BF16)
    for chunk in range(lower_chunks):
        for i in range(4):
            place = (iota((SIZES[i], 32), 0).astype(F32) + 0.5) * (1.0 / LENGTHS[i])
            column = iota((SIZES[i], 32), 1).astype(F32) - float(chunk * ITEMS)
            one = ((place >= column) & (place < column + 1.0)).astype(F32).astype(BF16)
            live[chunk, STARTS[i] : STARTS[i] + SIZES[i], :] = dot(one, item_live)

    for total in (d_sa, d_sb, d_ta, d_tb, d_win, d_wout, d_bias, d_gain, d_off, pack):
        total[...] = jnp.zeros(total.shape, F32)

    taps = 1.0 / KERNEL

    def matrix(ref, layer, c, rows, columns):
        return ref[layer, c - 1, :rows, :columns]

    def sides(scale, height, j):
        half = SIZES[scale] // 2
        return [STARTS[scale] + side * half + j * height for side in range(2)]

    def kept_of(chunk):
        return [
            ref.at[lax.rem(chunk, 2)]
            for ref in (
                unit_all,
                inverse_all,
                z_keep_all,
                hidden_all,
                slope_all,
                season_src_all,
                trend_src_all,
                season_hid_all,
                season_slope_all,
                trend_hid_all,
                trend_slope_all,
            )
        ]

    def forward(layer, chunk, found):
        (
            unit,
            inverse,
            z_keep,
            hidden,
            slope,
            season_src,
            trend_src,
            season_hid,
            season_slope,
            trend_hid,
            trend_slope,
        ) = kept_of(chunk)
        gain = ln_gain[layer : layer + 1, :]
        offset = ln_bias[layer : layer + 1, :]
        offset_pair = jnp.concatenate([offset, offset], 1)
        bias = ffn_bias[layer : layer + 1, :]

        def rows_of(start, height):
            if layer == 0:
                return tok_buf[chunk, start : start + height, :].astype(F32)
            return field[start : start + height, :]

        def norm(scale, height, j):
            while layer > 0 and ("y", layer - 1, scale, j) not in found:
                yield 1
            parts = []
            for start in sides(scale, height, j):
                x = rows_of(start, height)
                centered = x - jnp.mean(x, -1, keepdims=True)
                yield 1
                inv = lax.rsqrt(dot((centered * centered).astype(BF16), mean_lanes) + EPS)
                n = centered * inv
                unit[layer, start : start + height, :] = n
                inverse[layer, start : start + height, :] = inv
                parts.append(n * gain)
                yield 1
            both = jnp.concatenate(parts, 1)
            average = dot(moving[scale, :height, :height], both.astype(BF16)) * taps
            found["n", layer, scale, j] = both + offset_pair
            found["s", layer, scale, j] = both - average
            found["t", layer, scale, j] = average + offset_pair

        def mixed(source, first, second, kept, hid, slp, u, layer_at, c, fine_to_coarse):
            a = source.astype(BF16)
            rows_in = a.shape[0]
            rows_out = rows_in // 2 if fine_to_coarse else rows_in * 2
            kept[layer_at, u, :rows_in, :] = a
            p = dot(matrix(first, layer_at, c, rows_out, rows_in), a)
            yield None
            h, slope_value = gelu_parts(p)
            h = h.astype(BF16)
            hid[layer_at, u, :rows_out, :] = h
            slp[layer_at, u, :rows_out, :] = slope_value.astype(BF16)
            yield None
            yield dot(matrix(second, layer_at, c, rows_out, rows_out), h)

        def season(c):
            results = []
            for j, u in enumerate(UNITS[c]):
                while ("S", layer, c - 1, j) not in found and not (
                    c == 1 and ("s", layer, 0, j) in found
                ):
                    yield 1
                source = found["s", layer, 0, j] if c == 1 else found["S", layer, c - 1, j]
                for value in mixed(
                    source, sa, sb, season_src, season_hid, season_slope, u, layer, c, True
                ):
                    if value is None:
                        yield 1
                    else:
                        results.append(value)
            mix = results[0] if len(results) == 1 else jnp.concatenate(results, 0)
            found["sm", layer, c, 0] = mix
            while ("s", layer, c, 0) not in found:
                yield 1
            found["S", layer, c, 0] = found["s", layer, c, 0] + mix

        def trend(c):
            while ("t" if c == 3 else "T", layer, c, 0) not in found:
                yield 1
            source = found["t" if c == 3 else "T", layer, c, 0]
            for j, u in enumerate(UNITS[c]):
                part = source[96 * j : 96 * (j + 1)] if c == 1 else source
                for value in mixed(part, ta, tb, trend_src, trend_hid, trend_slope, u, layer, c, False):
                    if value is None:
                        yield 1
                    else:
                        found["tm", layer, c - 1, j] = value
            if c > 1:
                while ("t", layer, c - 1, 0) not in found:
                    yield 1
                found["T", layer, c - 1, 0] = found["t", layer, c - 1, 0] + found["tm", layer, c - 1, 0]

        def ffn(scale, height, j):
            needed = [("n", layer, scale, j)]
            if scale > 0:
                needed.append(("sm", layer, scale, j))
            if scale < 3:
                needed.append(("tm", layer, scale, j))
            while not all(key in found for key in needed):
                yield 1
            value = found[needed[0]]
            for key in needed[1:]:
                value = value + found[key]
            value = value.astype(BF16)
            starts = sides(scale, height, j)
            halves = [value[:, :LANES], value[:, LANES:]]
            for start, z in zip(starts, halves):
                z_keep[layer, start : start + height, :] = z
            a = dot(jnp.concatenate(halves, 0), ffn_in[layer]) + bias
            yield 1
            h, slope_value = gelu_parts(a)
            h = h.astype(BF16)
            slope_value = slope_value.astype(BF16)
            for k, start in enumerate(starts):
                hidden[layer, start : start + height, :] = h[k * height : (k + 1) * height]
                slope[layer, start : start + height, :] = slope_value[k * height : (k + 1) * height]
            yield 1
            f = dot(h, ffn_out[layer])
            yield 1
            for k, start in enumerate(starts):
                y = rows_of(start, height) + live[chunk, start : start + height, :] * f[
                    k * height : (k + 1) * height
                ]
                if layer == NL - 1:
                    out_buf[chunk, start : start + height, :] = y.astype(BF16)
                else:
                    field[start : start + height, :] = y
            found["y", layer, scale, j] = True

        for scale, height, number in reversed(SLABS):
            for j in range(number):
                yield norm(scale, height, j)
        for c in (3, 2, 1):
            yield trend(c)
        for c in (1, 2, 3):
            yield season(c)
        for scale, height, number in (SLABS[1], SLABS[2], SLABS[0], SLABS[3]):
            for j in range(number):
                yield ffn(scale, height, j)

    def backward(layer, chunk, found):
        (
            unit,
            inverse,
            z_keep,
            hidden,
            slope,
            season_src,
            trend_src,
            season_hid,
            season_slope,
            trend_hid,
            trend_slope,
        ) = kept_of(chunk)
        gain = ln_gain[layer : layer + 1, :]

        def rows_of(start, height):
            if layer == NL - 1:
                return cot_buf[chunk, start : start + height, :].astype(F32)
            return grad[start : start + height, :]

        def ffn(scale, height, j):
            while layer < NL - 1 and ("x", layer + 1, scale, j) not in found:
                yield 1
            starts = sides(scale, height, j)
            parts = []
            for start in starts:
                df = (live[chunk, start : start + height, :] * rows_of(start, height)).astype(BF16)
                df_keep[start : start + height, :] = df
                parts.append(df)
            dh = dot(jnp.concatenate(parts, 0), wout_t[layer])
            yield 1
            parts = []
            for k, start in enumerate(starts):
                da = dh[k * height : (k + 1) * height] * slope[layer, start : start + height, :].astype(F32)
                d_bias[layer] += fold_rows(da)
                da = da.astype(BF16)
                da_keep[start : start + height, :] = da
                parts.append(da)
            yield 1
            dz = dot(jnp.concatenate(parts, 0), win_t[layer])
            found["dz", layer, scale, j] = jnp.concatenate([dz[:height], dz[height:]], 1)

        def weight_grads():
            while not all(("dz", layer, scale, j) in found for scale, _, number in SLABS for j in range(number)):
                yield 1
            for t in range(0, CHUNK, TILE):
                d_win[layer] += dot_tn(z_keep[layer, t : t + TILE, :], da_keep[t : t + TILE, :])
                yield 1
                d_wout[layer] += dot_tn(df_keep[t : t + TILE, :], hidden[layer, t : t + TILE, :])
                yield 1

        def mixed(g, first_t, second_t, slp, u, c, fine_to_coarse):
            rows = g.shape[0]
            rows_out = rows * 2 if fine_to_coarse else rows // 2
            dh = dot(matrix(second_t, layer, c, rows, rows), g)
            yield None
            dp = (dh * slp[layer, u, :rows, :].astype(F32)).astype(BF16)
            yield dp
            yield dot(matrix(first_t, layer, c, rows_out, rows), dp)

        def trend(c):
            results, gs, dps = [], [], []
            for j, u in enumerate(UNITS[c]):
                key = ("dz", layer, 0, j) if c == 1 else ("dT", layer, c - 1, 0)
                while key not in found:
                    yield 1
                g = found[key].astype(BF16)
                gs.append(beside(g, 96))
                steps = []
                for value in mixed(g, ta_t, tb_t, trend_slope, u, c, False):
                    if value is not None:
                        steps.append(value)
                    yield 1
                dps.append(beside(steps[0], 96))
                results.append(steps[1])
            total = results[0] if len(results) == 1 else jnp.concatenate(results, 0)
            found["gT", layer, c, 0] = total
            while ("dz", layer, c, 0) not in found:
                yield 1
            found["dT", layer, c, 0] = found["dz", layer, c, 0] + total
            rows = 48 if c == 3 else 96
            kept = [beside(trend_hid[layer, u, : 2 * rows, :], 96) for u in UNITS[c]]
            d_tb[layer, c - 1] += dot_nt(jnp.concatenate(gs, 1), jnp.concatenate(kept, 1))
            yield 1
            kept = [beside(trend_src[layer, u, :rows, :], 48) for u in UNITS[c]]
            d_ta[layer, c - 1] += dot_nt(jnp.concatenate(kept, 1), jnp.concatenate(dps, 1))

        def season(c):
            key = ("dz", layer, 3, 0) if c == 3 else ("dS", layer, c, 0)
            while key not in found:
                yield 1
            gs, dps = [], []
            for j, u in enumerate(UNITS[c]):
                g = found[key].astype(BF16)
                if c == 1:
                    g = g[96 * j : 96 * (j + 1)]
                gs.append(beside(g, 48))
                steps = []
                for value in mixed(g, sa_t, sb_t, season_slope, u, c, True):
                    if value is not None:
                        steps.append(value)
                    yield 1
                dps.append(beside(steps[0], 48))
                found["gS", layer, c - 1, j] = steps[1]
            if c > 1:
                while ("dz", layer, c - 1, 0) not in found:
                    yield 1
                found["dS", layer, c - 1, 0] = found["dz", layer, c - 1, 0] + found["gS", layer, c - 1, 0]
            rows = 48 if c == 3 else 96
            kept = [beside(season_hid[layer, u, :rows, :], 48) for u in UNITS[c]]
            d_sb[layer, c - 1] += dot_nt(jnp.concatenate(kept, 1), jnp.concatenate(gs, 1))
            yield 1
            kept = [beside(season_src[layer, u, : 2 * rows, :], 96) for u in UNITS[c]]
            d_sa[layer, c - 1] += dot_nt(jnp.concatenate(dps, 1), jnp.concatenate(kept, 1))

        def norm(scale, height, j):
            needed = [("dz", layer, scale, j)]
            if scale < 3:
                needed.append(("gS", layer, scale, j))
            if scale > 0:
                needed.append(("gT", layer, scale, j))
            while not all(key in found for key in needed):
                yield 1
            value = found[needed[0]]
            if scale == 0:
                moved = -found[needed[1]]
                value = value + found[needed[1]]
            elif scale == 3:
                moved = found[needed[1]]
            else:
                moved = found[needed[2]] - found[needed[1]]
                value = value + found[needed[1]]
            value = value + dot(moving_t[scale, :height, :height], moved.astype(BF16)) * taps
            yield 1
            for side, start in enumerate(sides(scale, height, j)):
                d = value[:, side * LANES : (side + 1) * LANES]
                n = unit[layer, start : start + height, :]
                dn = d * n
                d_gain[layer] += fold_rows(dn)
                d_off[layer] += fold_rows(d)
                q = d * gain
                qn = dn * gain
                mean_q = dot(q.astype(BF16), mean_lanes)
                mean_qn = dot(qn.astype(BF16), mean_lanes)
                yield 1
                x = rows_of(start, height) + inverse[layer, start : start + height, :] * (
                    q - mean_q - n * mean_qn
                )
                if layer == 0:
                    grad_buf[chunk, start : start + height, :] = x.astype(BF16)
                else:
                    grad[start : start + height, :] = x
                yield 1
            found["x", layer, scale, j] = True

        for scale, height, number in (SLABS[0], SLABS[3], SLABS[1], SLABS[2]):
            for j in range(number):
                yield ffn(scale, height, j)
        for c in (1, 2, 3):
            yield trend(c)
        for c in (3, 2, 1):
            yield season(c)
        for scale, height, number in reversed(SLABS):
            for j in range(number):
                yield norm(scale, height, j)
        yield weight_grads()

    def one_step(step, carry):
        @pl.when(step < chunks)
        def _():
            inbound_wait(0, step)
            found = {}
            drive([thread for layer in range(NL) for thread in forward(layer, step, found)])
            later = step + FIRST_STEPS
            inbound_start(later, jnp.where(far & (later <= lower_chunks), later + 1, later))
            results_out("forward", step)

        @pl.when(step > 0)
        def _():
            chunk = step - 1
            inbound_wait(1, chunk)

            @pl.when(jnp.logical_not(upper | far) & (chunk == lower_chunks - 1))
            def _():
                pl.semaphore_signal(
                    come_down,
                    inc=1,
                    device_id=(scale_index, position + groups // 2),
                    device_id_type=MESH,
                )

            found = {}
            drive([thread for layer in reversed(range(NL)) for thread in backward(layer, chunk, found)])
            results_out("backward", chunk)

        return carry

    lax.fori_loop(0, chunks + 1, one_step, 0)
    rest = chunks + FIRST_STEPS
    inbound_start(rest, jnp.where(far & upper, lower_chunks + 1, rest))

    for layer in range(NL):
        parts = [None] * 4
        for c in (1, 2, 3):
            for k, value in enumerate((d_sa, d_sb, d_ta, d_tb)):
                masked = (value[layer, c - 1] * masks[k][c - 1]).astype(BF16)
                found = dot(dot(places[k][layer, c - 1], masked).astype(BF16), lays[k][c - 1])
                parts[k] = found if parts[k] is None else parts[k] + found
        pack[layer : layer + 1, :] = jnp.sum(d_gain[layer], 0, keepdims=True)
        pack[NL + layer : NL + layer + 1, :] = jnp.sum(d_off[layer], 0, keepdims=True)
        bias_sum = jnp.sum(d_bias[layer], 0, keepdims=True)
        pack[AT_SEASON_IN : AT_SEASON_IN + NL * SEASON_ROWS, :] += parts[0]
        row = AT_SEASON_OUT + layer * L0 // 2
        pack[row : row + L0 // 2, :] = parts[1]
        row = AT_TREND_OUT + layer * TREND_STEP
        pack[row : row + TREND_ROWS, :] = parts[3]
        for side in range(2):
            lanes = slice(side * LANES, (side + 1) * LANES)
            row = 2 * NL + 2 * layer + side
            pack[row : row + 1, :] = bias_sum[:, lanes]
            row = AT_TREND_IN + layer * L0 + side * L0 // 2
            pack[row : row + L0 // 2, :] = parts[2][:, lanes]
            row = AT_FFN_IN + (2 * layer + side) * LANES
            pack[row : row + LANES, :] = d_win[layer, :, lanes]
            row = AT_FFN_OUT + (2 * layer + side) * LANES
            pack[row : row + LANES, :] = d_wout[layer, :, lanes].T

    plane_index = scale_index * plane_dp + place_dp
    half_rows = pack_rows // 2
    plane_rows = half_rows // plane_size

    def core_id():
        return (scale_index, position + 1 - 2 * core)

    def plane_id(index):
        return (
            lax.div(index, plane_dp),
            depth_index * (2 * plane_dp) + lax.rem(index, plane_dp) * 2 + core,
        )

    def depth_id(index):
        return (scale_index, index * (2 * plane_dp) + place_dp * 2 + core)

    def remote(src, dst, stage, slot_out, slot_in, device):
        return pltpu.make_async_remote_copy(
            src_ref=src,
            dst_ref=dst,
            send_sem=ar_send.at[stage, slot_out],
            recv_sem=ar_recv.at[stage, slot_in],
            device_id=device,
            device_id_type=MESH,
        )

    def arrived(ref, stage, slot):
        pltpu.make_async_copy(ref, ref, ar_recv.at[stage, slot]).wait()

    mine = pl.multiple_of(core * half_rows, 16)
    theirs = pl.multiple_of((1 - core) * half_rows, 16)
    first_copy = remote(pack.at[pl.ds(theirs, half_rows)], half_in, 0, 0, 0, core_id())
    first_copy.start()
    results_out("packed", 0)
    first_copy.wait_send()
    arrived(half_in, 0, 0)
    half_bf[pl.ds(mine, half_rows)] = (pack[pl.ds(mine, half_rows)] + half_in[...]).astype(BF16)

    def plane_piece(index):
        return pl.ds(pl.multiple_of(mine + index * plane_rows, 16), plane_rows)

    def plane_round(act):
        def one(k, carry):
            other = lax.rem(plane_index + k, plane_size)
            back = lax.rem(plane_index + plane_size - k, plane_size)
            act(other, back, k)
            return carry

        lax.fori_loop(1, plane_size, one, 0)

    def plane_scatter(other, back, k):
        remote(half_bf.at[plane_piece(other)], plane_in.at[k], 1, k, k, plane_id(other)).start()

    plane_round(plane_scatter)
    results_out("planed", 0)
    plane_sum = pack[plane_piece(plane_index)] + half_in[
        pl.ds(pl.multiple_of(plane_index * plane_rows, 16), plane_rows)
    ]

    def plane_wait(k, carry):
        remote(half_bf.at[plane_piece(0)], plane_in.at[k], 1, k, k, core_id()).wait_send()
        arrived(plane_in.at[k], 1, k)
        return carry

    lax.fori_loop(1, plane_size, plane_wait, 0)
    for k in range(1, plane_size):
        plane_sum = plane_sum + plane_in[k].astype(F32)
    plane_bf[...] = plane_sum.astype(BF16)

    outer = jnp.where(depth_index < 2, 0, 3)
    inner = jnp.where(depth_index < 2, 1, 2)
    own_plane = plane_piece(plane_index)
    give = remote(plane_bf, pair_in, 2, 0, 0, depth_id(outer))
    across = remote(across_out, across_in, 3, 0, 0, depth_id(3 - outer))
    back = remote(packed_out.at[own_plane], packed_out.at[own_plane], 4, 0, 0, depth_id(inner))

    @pl.when(depth_index == inner)
    def _():
        give.start()

    results_out("paired", 0)

    @pl.when(depth_index == inner)
    def _():
        give.wait_send()
        arrived(packed_out.at[own_plane], 4, 0)

    @pl.when(depth_index == outer)
    def _():
        arrived(pair_in, 2, 0)
        across_out[...] = (plane_bf[...].astype(F32) + pair_in[...].astype(F32)).astype(BF16)
        across.start()

    @pl.when(far & upper)
    def _():
        pl.semaphore_wait(come_down, 1)

    results_out("crossed", 0)

    @pl.when(depth_index == outer)
    def _():
        across.wait_send()
        arrived(across_in, 3, 0)
        packed_out[own_plane] = (across_out[...].astype(F32) + across_in[...].astype(F32)).astype(BF16)
        back.start()

    results_out("gathered", 0)

    @pl.when(depth_index == outer)
    def _():
        back.wait_send()


    def plane_gather(other, back, k):
        remote(packed_out.at[own_plane], packed_out.at[own_plane], 5, k, k, plane_id(other)).start()

    plane_round(plane_gather)

    def plane_gathered(other, back, k):
        remote(packed_out.at[own_plane], packed_out.at[own_plane], 5, k, k, core_id()).wait_send()
        arrived(packed_out.at[plane_piece(back)], 5, k)

    plane_round(plane_gathered)
    own_half = pl.ds(mine, half_rows)
    last_copy = remote(packed_out.at[own_half], packed_out.at[own_half], 6, 0, 0, core_id())
    last_copy.start()
    last_copy.wait_send()
    arrived(packed_out.at[pl.ds(theirs, half_rows)], 6, 0)

    @pl.when(position >= bounds[3])
    def _():
        for copy in padding():
            copy.wait()

    def sent(copy, remote_copy):
        if remote_copy:
            copy.wait_send()

    each_inbound(sent, lambda copy, kind, slot, chunk: copy.wait_send(), 0, lower_chunks + 1)

    def finish(chunk, carry):
        for kind in range(2):
            for scale in range(4):
                home, local, remote_copy = outbound(kind, scale, chunk)

                @pl.when((home != position) & (chunk < chunks))
                def _():
                    remote_copy.wait_send()

            for scale in range(4):

                @pl.when((position >= bounds[scale]) & (position < bounds[scale + 1]))
                def _():
                    for slot in range(SLOTS[scale]):
                        for half in range(2):

                            @pl.when(chunk < (upper_chunks if half else lower_chunks))
                            def _():
                                place = half * lower_chunks + chunk
                                first = (slot * per_device + place * ITEMS) * LENGTHS[scale]
                                ref = (mixed_out, input_grad)[kind].at[
                                    pl.ds(pl.multiple_of(first, 16), SIZES[scale])
                                ]
                                sem = out_recv.at[kind, chunk, slot * 2 + half]
                                pltpu.make_async_copy(ref, ref, sem).wait()

        return carry

    lax.fori_loop(0, lower_chunks, finish, 0)


def unpack_body(mixed, grad, packed, mixed_out, input_grad, *refs):
    finals, small_sem, big_sem = refs[:9], refs[18], refs[19]
    (
        gain_grad,
        bias_grad,
        season_in_grad,
        season_out_grad,
        trend_in_grad,
        trend_out_grad,
        ffn_in_grad,
        ffn_bias_grad,
        ffn_out_grad,
    ) = refs[9:18]
    size = mixed.shape[0] // PIECES
    big = []
    for kind, (source, target) in enumerate(((mixed, mixed_out), (grad, input_grad))):
        for k in range(PIECES):
            rows = pl.ds(k * size, size)
            big.append(pltpu.make_async_copy(source.at[rows], target.at[rows], big_sem.at[kind, k]))
    for copy in big:
        copy.start()
    top = packed[0:16, :].astype(F32)
    gain_grad[...] = top[0:NL]
    bias_grad[...] = top[NL : 2 * NL]
    for layer in range(NL):
        for side in range(2):
            lanes = slice(side * LANES, (side + 1) * LANES)
            row = 2 * NL + 2 * layer + side
            ffn_bias_grad[layer : layer + 1, lanes] = top[row : row + 1]
            row = AT_FFN_IN + (2 * layer + side) * LANES
            ffn_in_grad[layer, :, lanes] = packed[row : row + LANES, :].astype(F32)
            row = AT_FFN_OUT + (2 * layer + side) * LANES
            ffn_out_grad[layer, side * LANES : (side + 1) * LANES, :] = packed[row : row + LANES, :].astype(F32)
        row = AT_SEASON_OUT + layer * L0 // 2
        season_out_grad[layer] = packed[row : row + L0 // 2, :SEASON_ROWS].astype(F32)
        row = AT_TREND_IN + layer * L0
        trend_in_grad[layer, :, :LANES] = packed[row : row + L0 // 2, :].astype(F32)
        trend_in_grad[layer, :, LANES:] = packed[
            row + L0 // 2 : row + L0, : TREND_ROWS - LANES
        ].astype(F32)
        row = AT_TREND_OUT + layer * TREND_STEP
        trend_out_grad[layer] = packed[row : row + TREND_ROWS, :L0].astype(F32)
    season_in_grad[...] = packed[AT_SEASON_IN : AT_SEASON_IN + NL * SEASON_ROWS, :L0].astype(F32)
    small = [
        pltpu.make_async_copy(source, target, small_sem.at[k])
        for k, (source, target) in enumerate(zip(refs[9:18], finals))
    ]
    for copy in small:
        copy.start()
    for copy in small + big:
        copy.wait()


def body(groups, n_scale, *args):
    tokens = args[0]
    hidden = args[9].shape[2]
    per_device = tokens.shape[0] // L0
    chunks = max(chunk_counts(per_device))
    unit_rows = 16 * 2 * (groups // 8) * n_scale
    pack_rows = -(-USED_ROWS // unit_rows) * unit_rows
    plane_size = groups // 8 * n_scale
    plane_rows = pack_rows // 2 // plane_size
    anywhere = pl.BlockSpec(memory_space=pl.ANY)
    vmem = pl.BlockSpec(memory_space=pltpu.VMEM)
    dma = pltpu.SemaphoreType.DMA
    turned = (
        args[:5]
        + (jnp.swapaxes(args[5], 0, 1).reshape(NL * SEASON_ROWS, L0),)
        + tuple(jnp.swapaxes(member, 1, 2) for member in args[6:8])
        + (args[8].reshape(NL * TREND_ROWS, L0),)
        + args[9:]
    )
    scratch = [pltpu.VMEM(member.shape, member.dtype) for k, member in enumerate(turned) if k not in (0, 1, 5)]
    scratch += [
        dma((len(turned) - 3,)),
        pltpu.VMEM((chunks, CHUNK, LANES), BF16),
        pltpu.VMEM((chunks, CHUNK, LANES), BF16),
        pltpu.VMEM((chunks, CHUNK, LANES), BF16),
        pltpu.VMEM((chunks, CHUNK, LANES), BF16),
        pltpu.VMEM((chunks, CHUNK, LANES), F32),
        pltpu.VMEM((CHUNK, LANES), F32),
        pltpu.VMEM((CHUNK, LANES), F32),
        pltpu.VMEM((CHUNK, LANES), BF16),
        pltpu.VMEM((CHUNK, hidden), BF16),
        pltpu.VMEM((2, NL, CHUNK, LANES), F32),
        pltpu.VMEM((2, NL, CHUNK, LANES), F32),
        pltpu.VMEM((2, NL, CHUNK, LANES), BF16),
        pltpu.VMEM((2, NL, CHUNK, hidden), BF16),
        pltpu.VMEM((2, NL, CHUNK, hidden), BF16),
        pltpu.VMEM((2, NL, 4, 192, 2 * LANES), BF16),
        pltpu.VMEM((2, NL, 4, 96, 2 * LANES), BF16),
        pltpu.VMEM((2, NL, 4, 96, 2 * LANES), BF16),
        pltpu.VMEM((2, NL, 4, 96, 2 * LANES), BF16),
        pltpu.VMEM((2, NL, 4, 192, 2 * LANES), BF16),
        pltpu.VMEM((2, NL, 4, 192, 2 * LANES), BF16),
        pltpu.VMEM((NL, 3, 96, 192), BF16),
        pltpu.VMEM((NL, 3, 96, 96), BF16),
        pltpu.VMEM((NL, 3, 192, 96), BF16),
        pltpu.VMEM((NL, 3, 192, 192), BF16),
        pltpu.VMEM((NL, 3, 192, 96), BF16),
        pltpu.VMEM((NL, 3, 96, 96), BF16),
        pltpu.VMEM((NL, 3, 96, 192), BF16),
        pltpu.VMEM((NL, 3, 192, 192), BF16),
        pltpu.VMEM((4, 192, 192), BF16),
        pltpu.VMEM((4, 192, 192), BF16),
        pltpu.VMEM((NL, hidden, LANES), BF16),
        pltpu.VMEM((NL, LANES, hidden), BF16),
        pltpu.VMEM((NL, 3, 48, 96), F32),
        pltpu.VMEM((NL, 3, 48, 48), F32),
        pltpu.VMEM((NL, 3, 48, 96), F32),
        pltpu.VMEM((NL, 3, 96, 96), F32),
        pltpu.VMEM((NL, LANES, hidden), F32),
        pltpu.VMEM((NL, LANES, hidden), F32),
        pltpu.VMEM((NL, 8, hidden), F32),
        pltpu.VMEM((NL, 8, LANES), F32),
        pltpu.VMEM((NL, 8, LANES), F32),
        pltpu.VMEM((pack_rows, LANES), F32),
        pltpu.VMEM((pack_rows // 2, LANES), F32),
        pltpu.VMEM((pack_rows, LANES), BF16),
        pltpu.VMEM((plane_size, plane_rows, LANES), BF16),
        pltpu.VMEM((plane_rows, LANES), BF16),
        pltpu.VMEM((plane_rows, LANES), BF16),
        pltpu.VMEM((plane_rows, LANES), BF16),
        pltpu.VMEM((plane_rows, LANES), BF16),
        dma((2,)),
        pltpu.SemaphoreType.REGULAR,
        pltpu.VMEM((2, chunks, 2, SIZES[2], LANES), BF16),
        dma((2, chunks, 2)),
        dma((2, chunks, 2)),
        dma((2, chunks, 8)),
        dma((2, chunks, 4)),
        dma((2, chunks, 4)),
        dma((2, chunks, 8)),
        dma((7, plane_size)),
        dma((7, plane_size)),
        pltpu.VMEM((3, 48, 96), F32),
        pltpu.VMEM((3, 48, 48), F32),
        pltpu.VMEM((3, 48, 96), F32),
        pltpu.VMEM((3, 96, 96), F32),
        pltpu.VMEM((NL, 3, NL * SEASON_ROWS, 48), BF16),
        pltpu.VMEM((NL, 3, L0 // 2, 48), BF16),
        pltpu.VMEM((NL, 3, L0 // 2, 48), BF16),
        pltpu.VMEM((NL, 3, TREND_ROWS, 96), BF16),
        pltpu.VMEM((3, 96, LANES), BF16),
        pltpu.VMEM((3, 48, LANES), BF16),
        pltpu.VMEM((3, 96, 2 * LANES), BF16),
        pltpu.VMEM((3, 96, LANES), BF16),
    ]
    mixed_out, input_grad, packed = pl.pallas_call(
        functools.partial(kernel_body, groups, n_scale, per_device, pack_rows),
        out_shape=[
            pltpu.VMEM(tokens.shape, BF16),
            pltpu.VMEM(tokens.shape, BF16),
            pltpu.VMEM((pack_rows, LANES), BF16),
        ],
        in_specs=[vmem if k == 5 else anywhere for k in range(len(turned))],
        out_specs=[vmem, vmem, vmem],
        scratch_shapes=scratch,
        compiler_params=pltpu.CompilerParams(
            collective_id=0, has_side_effects=True, vmem_limit_bytes=58 << 20
        ),
    )(*turned)
    finals = [
        jax.ShapeDtypeStruct(shape, F32)
        for shape in (
            (NL, LANES),
            (NL, LANES),
            (NL * SEASON_ROWS, L0),
            (NL, L0 // 2, SEASON_ROWS),
            (NL, L0 // 2, TREND_ROWS),
            (NL, TREND_ROWS, L0),
            (NL, LANES, hidden),
            (NL, hidden),
            (NL, hidden, LANES),
        )
    ]
    outs = pl.pallas_call(
        unpack_body,
        out_shape=[
            jax.ShapeDtypeStruct(tokens.shape, BF16),
            jax.ShapeDtypeStruct(tokens.shape, BF16),
            *finals,
        ],
        in_specs=[vmem] * 3,
        out_specs=[anywhere] * 11,
        scratch_shapes=[pltpu.VMEM(member.shape, F32) for member in finals]
        + [dma((len(finals),)), dma((2, PIECES))],
        compiler_params=pltpu.CompilerParams(vmem_limit_bytes=16 << 20),
    )(*(pltpu.with_memory_space_constraint(member, pltpu.VMEM) for member in (mixed_out, input_grad, packed)))
    return (
        *outs[:4],
        jnp.swapaxes(outs[4].reshape(SEASON_ROWS, NL, L0), 0, 1),
        jnp.swapaxes(outs[5], 1, 2),
        jnp.swapaxes(outs[6], 1, 2),
        *outs[7:],
    )


def solution(mesh):
    rows = P(("scale", "dp"), None)
    return jax.shard_map(
        functools.partial(body, mesh.shape["dp"], mesh.shape["scale"]),
        mesh=mesh,
        in_specs=(rows, rows, P("scale", None)) + (P(),) * 9,
        out_specs=(rows, rows) + (P(),) * 9,
        check_vma=False,
    )
```

```python
import functools

import jax
import jax.numpy as jnp
from jax import lax
from jax.experimental import pallas as pl
from jax.experimental.pallas import tpu as pltpu
from jax.sharding import PartitionSpec as P

L0 = 96
KERNEL = 25
NL = 2
SEASON_ROWS = 84
TREND_ROWS = 168
EPS = 1e-05
LANES = 128
ITEMS = 8
PAIR = 4
MESH = pl.DeviceIdType.MESH
F32 = jnp.float32
BF16 = jnp.bfloat16

LENGTHS = [L0 >> i for i in range(4)]
SIZES = [ITEMS * n for n in LENGTHS]
STARTS = [sum(SIZES[:i]) for i in range(4)]
CHUNK = sum(SIZES)
SLOTS = [1, 2, 4, 4]
SELF = [(0, 0), (0, 1), (1, 1), (3, 1)]
TILE = 480
SLABS = [(0, 192, 2), (1, 192, 1), (2, 96, 1), (3, 48, 1)]
UNITS = {1: (0, 1), 2: (2,), 3: (3,)}
WEIGHT_COUNT = {1: 2, 2: 4, 3: 4}
GRAD_COUNT = {1: 1, 2: 2, 3: 4}
AT_SEASON_IN = 16
AT_TREND_IN = AT_SEASON_IN + 176
AT_SEASON_OUT = AT_TREND_IN + NL * L0
AT_TREND_OUT = AT_SEASON_OUT + NL * L0 // 2
TREND_STEP = 176
AT_FFN_IN = AT_TREND_OUT + NL * TREND_STEP
AT_FFN_OUT = AT_FFN_IN + NL * 2 * LANES
USED_ROWS = AT_FFN_OUT + NL * 2 * LANES
PIECES = 4
FIRST_STEPS = 3


def dot(a, b):
    return jnp.dot(a, b, preferred_element_type=F32)


def dot_nt(a, b):
    return lax.dot_general(a, b, (((1,), (1,)), ((), ())), preferred_element_type=F32)


def dot_tn(a, b):
    return lax.dot_general(a, b, (((0,), (0,)), ((), ())), preferred_element_type=F32)


def gelu_parts(v):
    cumulative = 0.5 * (1.0 + lax.erf(v * 0.7071067811865476))
    density = jnp.exp(-0.5 * (v * v)) * 0.3989422804014327
    return v * cumulative, cumulative + v * density


def iota(shape, dim):
    return lax.broadcasted_iota(jnp.int32, shape, dim)


def selection(rows, columns, count, length, base, turned=False, stride=1):
    shape = (columns, rows) if turned else (rows, columns)
    r = iota(shape, 1 if turned else 0)
    c = iota(shape, 0 if turned else 1)
    found = jnp.zeros(shape, jnp.bool_)
    for k in range(count):
        near = c == (r - k * length) * stride + base
        found = found | (near & (r >= k * length) & (r < (k + 1) * length))
    return found.astype(F32)


def block_mask(count, height, width, turned=False):
    shape = (count * width, count * height) if turned else (count * height, count * width)
    r = iota(shape, 1 if turned else 0)
    c = iota(shape, 0 if turned else 1)
    found = jnp.zeros(shape, jnp.bool_)
    for k in range(count):
        found = found | (
            (r >= k * height) & (r < (k + 1) * height) & (c >= k * width) & (c < (k + 1) * width)
        )
    return found.astype(F32)


def moving_counts(count, length, turned):
    size = count * length
    t = iota((size, size), 1 if turned else 0)
    u = iota((size, size), 0 if turned else 1)
    total = jnp.zeros((size, size), F32)
    half = (KERNEL - 1) // 2
    for k in range(count):
        low, high = k * length, (k + 1) * length - 1
        inside = (t >= low) & (t <= high) & (u >= low) & (u <= high)
        near = (jnp.abs(t - u) <= half).astype(F32)
        first = jnp.where(u == low, jnp.maximum(half - (t - low), 0), 0).astype(F32)
        last = jnp.where(u == high, jnp.maximum(half - (high - t), 0), 0).astype(F32)
        total = total + jnp.where(inside, near + first + last, 0.0)
    return total


def beside(value, height):
    return jnp.concatenate([value[k : k + height] for k in range(0, value.shape[0], height)], 1)


def drive(threads):
    active = list(threads)
    while active:
        rest = []
        for thread in active:
            if next(thread, None) is not None:
                rest.append(thread)
        active = rest


def fold_rows(value):
    return jnp.sum(value.reshape(-1, 8, value.shape[-1]), 0)


def group_of(groups, scale, slot, position):
    bounds = [0, groups // 2, 3 * groups // 4, 7 * groups // 8]
    offsets = [0, groups // 4, groups // 8, 3 * groups // 8]
    return position - bounds[scale] + offsets[slot]


def home_of(groups, scale, group):
    if scale == 0:
        return group, 0
    if scale == 1:
        return groups // 2 + lax.rem(group, groups // 4), lax.div(group, groups // 4)
    part = lax.div(group, groups // 8)
    slot = jnp.where(part == 1, 2, jnp.where(part == 2, 1, part))
    first = 3 * groups // 4 if scale == 2 else 7 * groups // 8
    return first + lax.rem(group, groups // 8), slot


def chunk_counts(per_device):
    total = per_device // ITEMS
    return total - total // 3, total // 3


def due_results(per_device):
    lower_chunks, upper_chunks = chunk_counts(per_device)

    def at_once(count):
        return {("forward", c): [(0, c)] for c in range(count)} | {("backward", c): [(1, c)] for c in range(count)}

    last, top = lower_chunks - 1, upper_chunks - 1
    return {
        (True, False): {("forward", c + 1): [(0, c)] for c in range(last)}
        | {("backward", c): [(1, c)] for c in range(last)}
        | {("forward", last): [(0, last - 1), (0, last)], ("gathered", 0): [(1, last)]},
        (False, False): at_once(lower_chunks) | {("backward", last): [], ("paired", 0): [(1, last)]},
        (False, True): at_once(upper_chunks) | {("backward", top): [], ("paired", 0): [(1, top)]},
        (True, True): {
            ("crossed", 0): [(kind, c) for c in range(upper_chunks) for kind in range(2)][:-1],
            ("gathered", 0): [(1, top)],
        },
    }


def kernel_body(
    groups,
    n_scale,
    per_device,
    pack_rows,
    tokens,
    cotangent,
    item_mask_hbm,
    ln_gain_hbm,
    ln_bias_hbm,
    season_in,
    season_out_hbm,
    trend_in_hbm,
    trend_out_hbm,
    ffn_in_hbm,
    ffn_bias_hbm,
    ffn_out_hbm,
    mixed_out,
    input_grad,
    packed_out,
    item_mask,
    ln_gain,
    ln_bias,
    season_out,
    trend_in,
    trend_out,
    ffn_in,
    ffn_bias,
    ffn_out,
    param_sem,
    tok_buf,
    cot_buf,
    out_buf,
    grad_buf,
    live,
    field,
    grad,
    df_keep,
    da_keep,
    unit_all,
    inverse_all,
    z_keep_all,
    hidden_all,
    slope_all,
    season_src_all,
    trend_src_all,
    season_hid_all,
    season_slope_all,
    trend_hid_all,
    trend_slope_all,
    sa,
    sb,
    ta,
    tb,
    sa_t,
    sb_t,
    ta_t,
    tb_t,
    moving,
    moving_t,
    win_t,
    wout_t,
    d_sa,
    d_sb,
    d_ta,
    d_tb,
    d_win,
    d_wout,
    d_bias,
    d_gain,
    d_off,
    pack,
    half_in,
    half_bf,
    plane_in,
    plane_bf,
    pair_in,
    across_out,
    across_in,
    pad_sem,
    come_down,
    relay_buf,
    relay_send,
    relay_recv,
    in_send,
    in_recv,
    out_send,
    out_recv,
    ar_send,
    ar_recv,
    *pack_refs,
):
    scale_index = lax.axis_index("scale")
    position = lax.axis_index("dp")
    worker_group = lax.rem(position, groups // 2)
    worker_half = lax.div(position, groups // 2)
    upper = position >= groups // 2
    lower_chunks, upper_chunks = chunk_counts(per_device)
    chunks = jnp.where(upper, upper_chunks, lower_chunks)
    bounds = [0, groups // 2, 3 * groups // 4, 7 * groups // 8, groups]

    masks, places, lays = pack_refs[0:4], pack_refs[4:8], pack_refs[8:12]
    params = [
        pltpu.make_async_copy(source, target, param_sem.at[k])
        for k, (source, target) in enumerate(
            (
                (item_mask_hbm, item_mask),
                (ln_gain_hbm, ln_gain),
                (ln_bias_hbm, ln_bias),
                (season_out_hbm, season_out),
                (trend_in_hbm, trend_in),
                (trend_out_hbm, trend_out),
                (ffn_in_hbm, ffn_in),
                (ffn_bias_hbm, ffn_bias),
                (ffn_out_hbm, ffn_out),
            )
        )
    ]

    barrier = pltpu.get_barrier_semaphore()

    plane_dp = groups // 8
    plane_size = plane_dp * n_scale
    core = lax.rem(position, 2)
    place_dp = lax.rem(lax.div(position, 2), plane_dp)
    depth_index = lax.div(position, 2 * plane_dp)

    def greet(device):
        pl.semaphore_signal(barrier, inc=1, device_id=device, device_id_type=MESH)

    for k in range(1, groups):
        greet((scale_index, lax.rem(position + k, groups)))
    for k in range((n_scale - 1) * plane_dp):
        other = lax.rem(scale_index + 1 + k // plane_dp, n_scale)
        greet((other, (depth_index * plane_dp + k % plane_dp) * 2 + core))
    pl.semaphore_wait(barrier, groups - 1 + (n_scale - 1) * plane_dp)

    def relayed(scale, slot, half):
        return half == 0 and ((scale == 2 and slot >= 2) or (scale == 3 and slot < 2))

    def inbound(kind, scale, slot, half, chunk):
        source = (tokens, cotangent)[kind]
        target = (tok_buf, cot_buf)[kind]
        length, size = LENGTHS[scale], SIZES[scale]
        first = (slot * per_device + (half * lower_chunks + chunk) * ITEMS) * length
        src = source.at[pl.ds(pl.multiple_of(first, 16), size)]
        dst = target.at[chunk, pl.ds(STARTS[scale], size)]
        recv = in_recv.at[kind, chunk, scale]
        if (slot, half) == SELF[scale]:
            return pltpu.make_async_copy(src, dst, recv), False
        owner = half * (groups // 2) + group_of(groups, scale, slot, position)
        if relayed(scale, slot, half):
            owner = position + (groups // 8 if scale == 2 else -(groups // 8))
            dst = relay_buf.at[kind, chunk, slot % 2, pl.ds(0, size)]
            recv = relay_recv.at[kind, chunk, slot % 2]
        return (
            pltpu.make_async_remote_copy(
                src_ref=src,
                dst_ref=dst,
                send_sem=in_send.at[kind, chunk, slot * 2 + half],
                recv_sem=recv,
                device_id=(scale_index, owner),
                device_id_type=MESH,
            ),
            True,
        )

    def relay(kind, scale, slot, chunk):
        length, size = LENGTHS[scale], SIZES[scale]
        src = relay_buf.at[kind, chunk, slot % 2, pl.ds(0, size)]
        target = (tok_buf, cot_buf)[kind]
        partner = position + (groups // 8 if scale == 3 else -(groups // 8))
        return pltpu.make_async_remote_copy(
            src_ref=src,
            dst_ref=target.at[chunk, pl.ds(STARTS[scale], size)],
            send_sem=relay_send.at[kind, chunk, slot % 2],
            recv_sem=in_recv.at[kind, chunk, scale],
            device_id=(scale_index, group_of(groups, scale, slot, partner)),
            device_id_type=MESH,
        )

    def order(scale):
        moves = [(kind, slot, half) for kind in range(2) for slot in range(SLOTS[scale]) for half in (1, 0)]
        return sorted(moves, key=lambda move: (move[0], not relayed(scale, move[1], move[2])))

    def each_inbound(act, act_relay, low, high):
        for scale in range(4):

            @pl.when((position >= bounds[scale]) & (position < bounds[scale + 1]))
            def _():
                def one_step(step, carry):
                    for kind, slot, half in order(scale):
                        chunk = step - kind

                        @pl.when((chunk >= 0) & (chunk < (upper_chunks if half else lower_chunks)))
                        def _():
                            act(*inbound(kind, scale, slot, half, chunk))

                    if scale >= 2:
                        other = 5 - scale
                        for kind in range(2):
                            chunk = step - kind

                            @pl.when((chunk >= 0) & (chunk < lower_chunks))
                            def _():
                                for slot in range(4):
                                    if relayed(other, slot, 0):
                                        act_relay(relay(kind, other, slot, chunk), kind, slot, chunk)

                    return carry

                lax.fori_loop(low, high, one_step, 0)

    def pass_on(copy, kind, slot, chunk):
        size = SIZES[2 if slot >= 2 else 3]
        ref = relay_buf.at[kind, chunk, slot % 2, pl.ds(0, size)]
        pltpu.make_async_copy(ref, ref, relay_recv.at[kind, chunk, slot % 2]).wait()
        copy.start()

    def inbound_start(low, high):
        each_inbound(lambda copy, remote: copy.start(), pass_on, low, high)

    far = (position < groups // 4) | (position >= bounds[2])
    inbound_start(0, jnp.where(far, FIRST_STEPS, lower_chunks + 1))
    for copy in params:
        copy.start()
    for copy in params:
        copy.wait()

    def inbound_wait(kind, chunk):
        target = (tok_buf, cot_buf)[kind]
        for scale in range(4):
            ref = target.at[chunk, pl.ds(STARTS[scale], SIZES[scale])]
            pltpu.make_async_copy(ref, ref, in_recv.at[kind, chunk, scale]).wait()

    pad_rows = SLOTS[3] * per_device * LENGTHS[3]

    def padding():
        rows = pl.ds(pad_rows, tokens.shape[0] - pad_rows)
        return [
            pltpu.make_async_copy(tokens.at[rows], mixed_out.at[rows], pad_sem.at[0]),
            pltpu.make_async_copy(cotangent.at[rows], input_grad.at[rows], pad_sem.at[1]),
        ]

    @pl.when(position >= bounds[3])
    def _():
        for copy in padding():
            copy.start()

    def outbound(kind, scale, chunk):
        source = (out_buf, grad_buf)[kind]
        target = (mixed_out, input_grad)[kind]
        home, slot = home_of(groups, scale, worker_group)
        length, size = LENGTHS[scale], SIZES[scale]
        first = (slot * per_device + (worker_half * lower_chunks + chunk) * ITEMS) * length
        src = source.at[chunk, pl.ds(STARTS[scale], size)]
        dst = target.at[pl.ds(pl.multiple_of(first, 16), size)]
        recv = out_recv.at[kind, chunk, slot * 2 + worker_half]
        local = pltpu.make_async_copy(src, dst, recv)
        remote = pltpu.make_async_remote_copy(
            src_ref=src,
            dst_ref=dst,
            send_sem=out_send.at[kind, chunk, scale],
            recv_sem=recv,
            device_id=(scale_index, home),
            device_id_type=MESH,
        )
        return home, local, remote

    def outbound_start(kind, chunk):
        for scale in range(4):
            home, local, remote = outbound(kind, scale, chunk)

            @pl.when(home == position)
            def _():
                local.start()

            @pl.when(home != position)
            def _():
                remote.start()

    def results_out(event, chunk):
        for (is_far, is_upper), due in due_results(per_device).items():
            for at, sends in due.items():
                if at[0] == event and sends:

                    @pl.when((far == is_far) & (upper == is_upper) & (chunk == at[1]))
                    def _():
                        for kind, done in sends:
                            outbound_start(kind, done)

    for layer in range(NL):
        for c in (1, 2, 3):
            count = WEIGHT_COUNT[c]
            fine, coarse = LENGTHS[c - 1], LENGTHS[c]
            at_season = L0 - fine
            at_trend = 2 * L0 - 2 * fine
            for whole, normal, turned, height, width, row, column, stride in (
                (season_in[...], sa, sa_t, coarse, fine, NL * at_season + layer, 0, NL),
                (season_out[layer], sb_t, sb, coarse, coarse, 0, at_season, 1),
                (trend_in[layer], ta_t, ta, coarse, fine, 0, at_trend, 1),
                (trend_out[...], tb, tb_t, fine, fine, TREND_ROWS * layer + at_trend, 0, 1),
            ):
                rows = selection(count * height, whole.shape[0], count, height, row, stride=stride)
                columns = selection(count * width, whole.shape[1], count, width, column).astype(BF16)
                tall = dot(rows.astype(BF16), whole).astype(BF16)
                normal[layer, c - 1, : count * height, : count * width] = (
                    dot_nt(tall, columns) * block_mask(count, height, width)
                ).astype(BF16)
                turned[layer, c - 1, : count * width, : count * height] = (
                    dot_nt(columns, tall) * block_mask(count, height, width, True)
                ).astype(BF16)
        eye_in = selection(ffn_in.shape[2], ffn_in.shape[2], 1, ffn_in.shape[2], 0).astype(BF16)
        eye_out = selection(LANES, LANES, 1, LANES, 0).astype(BF16)
        win_t[layer] = dot_nt(eye_in, ffn_in[layer]).astype(BF16)
        wout_t[layer] = dot_nt(eye_out, ffn_out[layer]).astype(BF16)
    for c in (1, 2, 3):
        count = GRAD_COUNT[c]
        fine, coarse = LENGTHS[c - 1], LENGTHS[c]
        at_season = L0 - fine
        at_trend = 2 * L0 - 2 * fine
        for k, (height, width, row, lane, stride) in enumerate(
            (
                (coarse, fine, NL * at_season, 0, NL),
                (coarse, coarse, 0, at_season, 1),
                (coarse, fine, 0, at_trend, 1),
                (fine, fine, at_trend, 0, 1),
            )
        ):
            masks[k][c - 1] = block_mask(count, height, width)
            rows, lanes = places[k].shape[2], lays[k].shape[2]
            for layer in range(NL):
                start = row + layer if stride > 1 else row
                place = selection(count * height, rows, count, height, start, True, stride)
                places[k][layer, c - 1] = place.astype(BF16)
            lays[k][c - 1] = selection(count * width, lanes, count, width, lane).astype(BF16)
    for scale, height, number in SLABS:
        for ref, is_turned in ((moving, False), (moving_t, True)):
            counts = moving_counts(height // LENGTHS[scale], LENGTHS[scale], is_turned)
            ref[scale, :height, :height] = counts.astype(BF16)
    mean_lanes = jnp.full((LANES, LANES), 1.0 / LANES, BF16)

    mask_rows = jnp.broadcast_to(item_mask[...].astype(F32), (LANES, item_mask.shape[1])).astype(BF16)
    first_item = worker_group * per_device + worker_half * lower_chunks * ITEMS
    chosen = iota((32, item_mask.shape[1]), 1) == iota((32, item_mask.shape[1]), 0) + first_item
    item_live = dot_nt(chosen.astype(F32).astype(BF16), mask_rows).astype(BF16)
    for chunk in range(lower_chunks):
        for i in range(4):
            place = (iota((SIZES[i], 32), 0).astype(F32) + 0.5) * (1.0 / LENGTHS[i])
            column = iota((SIZES[i], 32), 1).astype(F32) - float(chunk * ITEMS)
            one = ((place >= column) & (place < column + 1.0)).astype(F32).astype(BF16)
            live[chunk, STARTS[i] : STARTS[i] + SIZES[i], :] = dot(one, item_live)

    for total in (d_sa, d_sb, d_ta, d_tb, d_win, d_wout, d_bias, d_gain, d_off, pack):
        total[...] = jnp.zeros(total.shape, F32)

    taps = 1.0 / KERNEL

    def matrix(ref, layer, c, rows, columns):
        return ref[layer, c - 1, :rows, :columns]

    def sides(scale, height, j):
        half = SIZES[scale] // 2
        return [STARTS[scale] + side * half + j * height for side in range(2)]

    def kept_of(chunk):
        return [
            ref.at[lax.rem(chunk, 2)]
            for ref in (
                unit_all,
                inverse_all,
                z_keep_all,
                hidden_all,
                slope_all,
                season_src_all,
                trend_src_all,
                season_hid_all,
                season_slope_all,
                trend_hid_all,
                trend_slope_all,
            )
        ]

    def forward(layer, chunk, found):
        (
            unit,
            inverse,
            z_keep,
            hidden,
            slope,
            season_src,
            trend_src,
            season_hid,
            season_slope,
            trend_hid,
            trend_slope,
        ) = kept_of(chunk)
        gain = ln_gain[layer : layer + 1, :]
        offset = ln_bias[layer : layer + 1, :]
        offset_pair = jnp.concatenate([offset, offset], 1)
        bias = ffn_bias[layer : layer + 1, :]

        def rows_of(start, height):
            if layer == 0:
                return tok_buf[chunk, start : start + height, :].astype(F32)
            return field[start : start + height, :]

        def norm(scale, height, j):
            while layer > 0 and ("y", layer - 1, scale, j) not in found:
                yield 1
            parts = []
            for start in sides(scale, height, j):
                x = rows_of(start, height)
                centered = x - jnp.mean(x, -1, keepdims=True)
                yield 1
                inv = lax.rsqrt(dot((centered * centered).astype(BF16), mean_lanes) + EPS)
                n = centered * inv
                unit[layer, start : start + height, :] = n
                inverse[layer, start : start + height, :] = inv
                parts.append(n * gain)
                yield 1
            both = jnp.concatenate(parts, 1)
            average = dot(moving[scale, :height, :height], both.astype(BF16)) * taps
            found["n", layer, scale, j] = both + offset_pair
            found["s", layer, scale, j] = both - average
            found["t", layer, scale, j] = average + offset_pair

        def mixed(source, first, second, kept, hid, slp, u, layer_at, c, fine_to_coarse):
            a = source.astype(BF16)
            rows_in = a.shape[0]
            rows_out = rows_in // 2 if fine_to_coarse else rows_in * 2
            kept[layer_at, u, :rows_in, :] = a
            p = dot(matrix(first, layer_at, c, rows_out, rows_in), a)
            yield None
            h, slope_value = gelu_parts(p)
            h = h.astype(BF16)
            hid[layer_at, u, :rows_out, :] = h
            slp[layer_at, u, :rows_out, :] = slope_value.astype(BF16)
            yield None
            yield dot(matrix(second, layer_at, c, rows_out, rows_out), h)

        def season(c):
            results = []
            for j, u in enumerate(UNITS[c]):
                while ("S", layer, c - 1, j) not in found and not (
                    c == 1 and ("s", layer, 0, j) in found
                ):
                    yield 1
                source = found["s", layer, 0, j] if c == 1 else found["S", layer, c - 1, j]
                for value in mixed(
                    source, sa, sb, season_src, season_hid, season_slope, u, layer, c, True
                ):
                    if value is None:
                        yield 1
                    else:
                        results.append(value)
            mix = results[0] if len(results) == 1 else jnp.concatenate(results, 0)
            found["sm", layer, c, 0] = mix
            while ("s", layer, c, 0) not in found:
                yield 1
            found["S", layer, c, 0] = found["s", layer, c, 0] + mix

        def trend(c):
            while ("t" if c == 3 else "T", layer, c, 0) not in found:
                yield 1
            source = found["t" if c == 3 else "T", layer, c, 0]
            for j, u in enumerate(UNITS[c]):
                part = source[96 * j : 96 * (j + 1)] if c == 1 else source
                for value in mixed(part, ta, tb, trend_src, trend_hid, trend_slope, u, layer, c, False):
                    if value is None:
                        yield 1
                    else:
                        found["tm", layer, c - 1, j] = value
            if c > 1:
                while ("t", layer, c - 1, 0) not in found:
                    yield 1
                found["T", layer, c - 1, 0] = found["t", layer, c - 1, 0] + found["tm", layer, c - 1, 0]

        def ffn(scale, height, j):
            needed = [("n", layer, scale, j)]
            if scale > 0:
                needed.append(("sm", layer, scale, j))
            if scale < 3:
                needed.append(("tm", layer, scale, j))
            while not all(key in found for key in needed):
                yield 1
            value = found[needed[0]]
            for key in needed[1:]:
                value = value + found[key]
            value = value.astype(BF16)
            starts = sides(scale, height, j)
            halves = [value[:, :LANES], value[:, LANES:]]
            for start, z in zip(starts, halves):
                z_keep[layer, start : start + height, :] = z
            a = dot(jnp.concatenate(halves, 0), ffn_in[layer]) + bias
            yield 1
            h, slope_value = gelu_parts(a)
            h = h.astype(BF16)
            slope_value = slope_value.astype(BF16)
            for k, start in enumerate(starts):
                hidden[layer, start : start + height, :] = h[k * height : (k + 1) * height]
                slope[layer, start : start + height, :] = slope_value[k * height : (k + 1) * height]
            yield 1
            f = dot(h, ffn_out[layer])
            yield 1
            for k, start in enumerate(starts):
                y = rows_of(start, height) + live[chunk, start : start + height, :] * f[
                    k * height : (k + 1) * height
                ]
                if layer == NL - 1:
                    out_buf[chunk, start : start + height, :] = y.astype(BF16)
                else:
                    field[start : start + height, :] = y
            found["y", layer, scale, j] = True

        for scale, height, number in reversed(SLABS):
            for j in range(number):
                yield norm(scale, height, j)
        for c in (3, 2, 1):
            yield trend(c)
        for c in (1, 2, 3):
            yield season(c)
        for scale, height, number in (SLABS[1], SLABS[2], SLABS[0], SLABS[3]):
            for j in range(number):
                yield ffn(scale, height, j)

    def backward(layer, chunk, found):
        (
            unit,
            inverse,
            z_keep,
            hidden,
            slope,
            season_src,
            trend_src,
            season_hid,
            season_slope,
            trend_hid,
            trend_slope,
        ) = kept_of(chunk)
        gain = ln_gain[layer : layer + 1, :]

        def rows_of(start, height):
            if layer == NL - 1:
                return cot_buf[chunk, start : start + height, :].astype(F32)
            return grad[start : start + height, :]

        def ffn(scale, height, j):
            while layer < NL - 1 and ("x", layer + 1, scale, j) not in found:
                yield 1
            starts = sides(scale, height, j)
            parts = []
            for start in starts:
                df = (live[chunk, start : start + height, :] * rows_of(start, height)).astype(BF16)
                df_keep[start : start + height, :] = df
                parts.append(df)
            dh = dot(jnp.concatenate(parts, 0), wout_t[layer])
            yield 1
            parts = []
            for k, start in enumerate(starts):
                da = dh[k * height : (k + 1) * height] * slope[layer, start : start + height, :].astype(F32)
                d_bias[layer] += fold_rows(da)
                da = da.astype(BF16)
                da_keep[start : start + height, :] = da
                parts.append(da)
            yield 1
            dz = dot(jnp.concatenate(parts, 0), win_t[layer])
            found["dz", layer, scale, j] = jnp.concatenate([dz[:height], dz[height:]], 1)

        def weight_grads():
            while not all(("dz", layer, scale, j) in found for scale, _, number in SLABS for j in range(number)):
                yield 1
            for t in range(0, CHUNK, TILE):
                d_win[layer] += dot_tn(z_keep[layer, t : t + TILE, :], da_keep[t : t + TILE, :])
                yield 1
                d_wout[layer] += dot_tn(df_keep[t : t + TILE, :], hidden[layer, t : t + TILE, :])
                yield 1

        def mixed(g, first_t, second_t, slp, u, c, fine_to_coarse):
            rows = g.shape[0]
            rows_out = rows * 2 if fine_to_coarse else rows // 2
            dh = dot(matrix(second_t, layer, c, rows, rows), g)
            yield None
            dp = (dh * slp[layer, u, :rows, :].astype(F32)).astype(BF16)
            yield dp
            yield dot(matrix(first_t, layer, c, rows_out, rows), dp)

        def trend(c):
            results, gs, dps = [], [], []
            for j, u in enumerate(UNITS[c]):
                key = ("dz", layer, 0, j) if c == 1 else ("dT", layer, c - 1, 0)
                while key not in found:
                    yield 1
                g = found[key].astype(BF16)
                gs.append(beside(g, 96))
                steps = []
                for value in mixed(g, ta_t, tb_t, trend_slope, u, c, False):
                    if value is not None:
                        steps.append(value)
                    yield 1
                dps.append(beside(steps[0], 96))
                results.append(steps[1])
            total = results[0] if len(results) == 1 else jnp.concatenate(results, 0)
            found["gT", layer, c, 0] = total
            while ("dz", layer, c, 0) not in found:
                yield 1
            found["dT", layer, c, 0] = found["dz", layer, c, 0] + total
            rows = 48 if c == 3 else 96
            kept = [beside(trend_hid[layer, u, : 2 * rows, :], 96) for u in UNITS[c]]
            d_tb[layer, c - 1] += dot_nt(jnp.concatenate(gs, 1), jnp.concatenate(kept, 1))
            yield 1
            kept = [beside(trend_src[layer, u, :rows, :], 48) for u in UNITS[c]]
            d_ta[layer, c - 1] += dot_nt(jnp.concatenate(kept, 1), jnp.concatenate(dps, 1))

        def season(c):
            key = ("dz", layer, 3, 0) if c == 3 else ("dS", layer, c, 0)
            while key not in found:
                yield 1
            gs, dps = [], []
            for j, u in enumerate(UNITS[c]):
                g = found[key].astype(BF16)
                if c == 1:
                    g = g[96 * j : 96 * (j + 1)]
                gs.append(beside(g, 48))
                steps = []
                for value in mixed(g, sa_t, sb_t, season_slope, u, c, True):
                    if value is not None:
                        steps.append(value)
                    yield 1
                dps.append(beside(steps[0], 48))
                found["gS", layer, c - 1, j] = steps[1]
            if c > 1:
                while ("dz", layer, c - 1, 0) not in found:
                    yield 1
                found["dS", layer, c - 1, 0] = found["dz", layer, c - 1, 0] + found["gS", layer, c - 1, 0]
            rows = 48 if c == 3 else 96
            kept = [beside(season_hid[layer, u, :rows, :], 48) for u in UNITS[c]]
            d_sb[layer, c - 1] += dot_nt(jnp.concatenate(kept, 1), jnp.concatenate(gs, 1))
            yield 1
            kept = [beside(season_src[layer, u, : 2 * rows, :], 96) for u in UNITS[c]]
            d_sa[layer, c - 1] += dot_nt(jnp.concatenate(dps, 1), jnp.concatenate(kept, 1))

        def norm(scale, height, j):
            needed = [("dz", layer, scale, j)]
            if scale < 3:
                needed.append(("gS", layer, scale, j))
            if scale > 0:
                needed.append(("gT", layer, scale, j))
            while not all(key in found for key in needed):
                yield 1
            value = found[needed[0]]
            if scale == 0:
                moved = -found[needed[1]]
                value = value + found[needed[1]]
            elif scale == 3:
                moved = found[needed[1]]
            else:
                moved = found[needed[2]] - found[needed[1]]
                value = value + found[needed[1]]
            value = value + dot(moving_t[scale, :height, :height], moved.astype(BF16)) * taps
            yield 1
            for side, start in enumerate(sides(scale, height, j)):
                d = value[:, side * LANES : (side + 1) * LANES]
                n = unit[layer, start : start + height, :]
                dn = d * n
                d_gain[layer] += fold_rows(dn)
                d_off[layer] += fold_rows(d)
                q = d * gain
                qn = dn * gain
                mean_q = dot(q.astype(BF16), mean_lanes)
                mean_qn = dot(qn.astype(BF16), mean_lanes)
                yield 1
                x = rows_of(start, height) + inverse[layer, start : start + height, :] * (
                    q - mean_q - n * mean_qn
                )
                if layer == 0:
                    grad_buf[chunk, start : start + height, :] = x.astype(BF16)
                else:
                    grad[start : start + height, :] = x
                yield 1
            found["x", layer, scale, j] = True

        for scale, height, number in (SLABS[0], SLABS[3], SLABS[1], SLABS[2]):
            for j in range(number):
                yield ffn(scale, height, j)
        for c in (1, 2, 3):
            yield trend(c)
        for c in (3, 2, 1):
            yield season(c)
        for scale, height, number in reversed(SLABS):
            for j in range(number):
                yield norm(scale, height, j)
        yield weight_grads()

    def one_step(step, carry):
        @pl.when(step < chunks)
        def _():
            inbound_wait(0, step)
            found = {}
            drive([thread for layer in range(NL) for thread in forward(layer, step, found)])
            later = step + FIRST_STEPS
            inbound_start(later, jnp.where(far & (later <= lower_chunks), later + 1, later))
            results_out("forward", step)

        @pl.when(step > 0)
        def _():
            chunk = step - 1
            inbound_wait(1, chunk)

            @pl.when(jnp.logical_not(upper | far) & (chunk == lower_chunks - 1))
            def _():
                pl.semaphore_signal(
                    come_down,
                    inc=1,
                    device_id=(scale_index, position + groups // 2),
                    device_id_type=MESH,
                )

            found = {}
            drive([thread for layer in reversed(range(NL)) for thread in backward(layer, chunk, found)])
            results_out("backward", chunk)

        return carry

    lax.fori_loop(0, chunks + 1, one_step, 0)
    rest = chunks + FIRST_STEPS
    inbound_start(rest, jnp.where(far & upper, lower_chunks + 1, rest))

    for layer in range(NL):
        parts = [None] * 4
        for c in (1, 2, 3):
            for k, value in enumerate((d_sa, d_sb, d_ta, d_tb)):
                masked = (value[layer, c - 1] * masks[k][c - 1]).astype(BF16)
                found = dot(dot(places[k][layer, c - 1], masked).astype(BF16), lays[k][c - 1])
                parts[k] = found if parts[k] is None else parts[k] + found
        pack[layer : layer + 1, :] = jnp.sum(d_gain[layer], 0, keepdims=True)
        pack[NL + layer : NL + layer + 1, :] = jnp.sum(d_off[layer], 0, keepdims=True)
        bias_sum = jnp.sum(d_bias[layer], 0, keepdims=True)
        pack[AT_SEASON_IN : AT_SEASON_IN + NL * SEASON_ROWS, :] += parts[0]
        row = AT_SEASON_OUT + layer * L0 // 2
        pack[row : row + L0 // 2, :] = parts[1]
        row = AT_TREND_OUT + layer * TREND_STEP
        pack[row : row + TREND_ROWS, :] = parts[3]
        for side in range(2):
            lanes = slice(side * LANES, (side + 1) * LANES)
            row = 2 * NL + 2 * layer + side
            pack[row : row + 1, :] = bias_sum[:, lanes]
            row = AT_TREND_IN + layer * L0 + side * L0 // 2
            pack[row : row + L0 // 2, :] = parts[2][:, lanes]
            row = AT_FFN_IN + (2 * layer + side) * LANES
            pack[row : row + LANES, :] = d_win[layer, :, lanes]
            row = AT_FFN_OUT + (2 * layer + side) * LANES
            pack[row : row + LANES, :] = d_wout[layer, :, lanes].T

    plane_index = scale_index * plane_dp + place_dp
    half_rows = pack_rows // 2
    plane_rows = half_rows // plane_size

    def core_id():
        return (scale_index, position + 1 - 2 * core)

    def plane_id(index):
        return (
            lax.div(index, plane_dp),
            depth_index * (2 * plane_dp) + lax.rem(index, plane_dp) * 2 + core,
        )

    def depth_id(index):
        return (scale_index, index * (2 * plane_dp) + place_dp * 2 + core)

    def remote(src, dst, stage, slot_out, slot_in, device):
        return pltpu.make_async_remote_copy(
            src_ref=src,
            dst_ref=dst,
            send_sem=ar_send.at[stage, slot_out],
            recv_sem=ar_recv.at[stage, slot_in],
            device_id=device,
            device_id_type=MESH,
        )

    def arrived(ref, stage, slot):
        pltpu.make_async_copy(ref, ref, ar_recv.at[stage, slot]).wait()

    mine = pl.multiple_of(core * half_rows, 16)
    theirs = pl.multiple_of((1 - core) * half_rows, 16)
    first_copy = remote(pack.at[pl.ds(theirs, half_rows)], half_in, 0, 0, 0, core_id())
    first_copy.start()
    results_out("packed", 0)
    first_copy.wait_send()
    arrived(half_in, 0, 0)
    half_bf[pl.ds(mine, half_rows)] = (pack[pl.ds(mine, half_rows)] + half_in[...]).astype(BF16)

    def plane_piece(index):
        return pl.ds(pl.multiple_of(mine + index * plane_rows, 16), plane_rows)

    def plane_round(act):
        def one(k, carry):
            other = lax.rem(plane_index + k, plane_size)
            back = lax.rem(plane_index + plane_size - k, plane_size)
            act(other, back, k)
            return carry

        lax.fori_loop(1, plane_size, one, 0)

    def plane_scatter(other, back, k):
        remote(half_bf.at[plane_piece(other)], plane_in.at[k], 1, k, k, plane_id(other)).start()

    plane_round(plane_scatter)
    results_out("planed", 0)
    plane_sum = pack[plane_piece(plane_index)] + half_in[
        pl.ds(pl.multiple_of(plane_index * plane_rows, 16), plane_rows)
    ]

    def plane_wait(k, carry):
        remote(half_bf.at[plane_piece(0)], plane_in.at[k], 1, k, k, core_id()).wait_send()
        arrived(plane_in.at[k], 1, k)
        return carry

    lax.fori_loop(1, plane_size, plane_wait, 0)
    for k in range(1, plane_size):
        plane_sum = plane_sum + plane_in[k].astype(F32)
    plane_bf[...] = plane_sum.astype(BF16)

    outer = jnp.where(depth_index < 2, 0, 3)
    inner = jnp.where(depth_index < 2, 1, 2)
    own_plane = plane_piece(plane_index)
    give = remote(plane_bf, pair_in, 2, 0, 0, depth_id(outer))
    across = remote(across_out, across_in, 3, 0, 0, depth_id(3 - outer))
    back = remote(packed_out.at[own_plane], packed_out.at[own_plane], 4, 0, 0, depth_id(inner))

    @pl.when(depth_index == inner)
    def _():
        give.start()

    results_out("paired", 0)

    @pl.when(depth_index == inner)
    def _():
        give.wait_send()
        arrived(packed_out.at[own_plane], 4, 0)

    @pl.when(depth_index == outer)
    def _():
        arrived(pair_in, 2, 0)
        across_out[...] = (plane_bf[...].astype(F32) + pair_in[...].astype(F32)).astype(BF16)
        across.start()

    @pl.when(far & upper)
    def _():
        pl.semaphore_wait(come_down, 1)

    results_out("crossed", 0)

    @pl.when(depth_index == outer)
    def _():
        across.wait_send()
        arrived(across_in, 3, 0)
        packed_out[own_plane] = (across_out[...].astype(F32) + across_in[...].astype(F32)).astype(BF16)
        back.start()

    results_out("gathered", 0)

    @pl.when(depth_index == outer)
    def _():
        back.wait_send()


    def plane_gather(other, back, k):
        remote(packed_out.at[own_plane], packed_out.at[own_plane], 5, k, k, plane_id(other)).start()

    plane_round(plane_gather)

    def plane_gathered(other, back, k):
        remote(packed_out.at[own_plane], packed_out.at[own_plane], 5, k, k, core_id()).wait_send()
        arrived(packed_out.at[plane_piece(back)], 5, k)

    plane_round(plane_gathered)
    own_half = pl.ds(mine, half_rows)
    last_copy = remote(packed_out.at[own_half], packed_out.at[own_half], 6, 0, 0, core_id())
    last_copy.start()
    last_copy.wait_send()
    arrived(packed_out.at[pl.ds(theirs, half_rows)], 6, 0)

    @pl.when(position >= bounds[3])
    def _():
        for copy in padding():
            copy.wait()

    def sent(copy, remote_copy):
        if remote_copy:
            copy.wait_send()

    each_inbound(sent, lambda copy, kind, slot, chunk: copy.wait_send(), 0, lower_chunks + 1)

    def finish(chunk, carry):
        for kind in range(2):
            for scale in range(4):
                home, local, remote_copy = outbound(kind, scale, chunk)

                @pl.when((home != position) & (chunk < chunks))
                def _():
                    remote_copy.wait_send()

            for scale in range(4):

                @pl.when((position >= bounds[scale]) & (position < bounds[scale + 1]))
                def _():
                    for slot in range(SLOTS[scale]):
                        for half in range(2):

                            @pl.when(chunk < (upper_chunks if half else lower_chunks))
                            def _():
                                place = half * lower_chunks + chunk
                                first = (slot * per_device + place * ITEMS) * LENGTHS[scale]
                                ref = (mixed_out, input_grad)[kind].at[
                                    pl.ds(pl.multiple_of(first, 16), SIZES[scale])
                                ]
                                sem = out_recv.at[kind, chunk, slot * 2 + half]
                                pltpu.make_async_copy(ref, ref, sem).wait()

        return carry

    lax.fori_loop(0, lower_chunks, finish, 0)


def unpack_body(mixed, grad, packed, mixed_out, input_grad, *refs):
    finals, small_sem, big_sem = refs[:9], refs[18], refs[19]
    (
        gain_grad,
        bias_grad,
        season_in_grad,
        season_out_grad,
        trend_in_grad,
        trend_out_grad,
        ffn_in_grad,
        ffn_bias_grad,
        ffn_out_grad,
    ) = refs[9:18]
    size = mixed.shape[0] // PIECES
    big = []
    for kind, (source, target) in enumerate(((mixed, mixed_out), (grad, input_grad))):
        for k in range(PIECES):
            rows = pl.ds(k * size, size)
            big.append(pltpu.make_async_copy(source.at[rows], target.at[rows], big_sem.at[kind, k]))
    for copy in big:
        copy.start()
    top = packed[0:16, :].astype(F32)
    gain_grad[...] = top[0:NL]
    bias_grad[...] = top[NL : 2 * NL]
    for layer in range(NL):
        for side in range(2):
            lanes = slice(side * LANES, (side + 1) * LANES)
            row = 2 * NL + 2 * layer + side
            ffn_bias_grad[layer : layer + 1, lanes] = top[row : row + 1]
            row = AT_FFN_IN + (2 * layer + side) * LANES
            ffn_in_grad[layer, :, lanes] = packed[row : row + LANES, :].astype(F32)
            row = AT_FFN_OUT + (2 * layer + side) * LANES
            ffn_out_grad[layer, side * LANES : (side + 1) * LANES, :] = packed[row : row + LANES, :].astype(F32)
        row = AT_SEASON_OUT + layer * L0 // 2
        season_out_grad[layer] = packed[row : row + L0 // 2, :SEASON_ROWS].astype(F32)
        row = AT_TREND_IN + layer * L0
        trend_in_grad[layer, :, :LANES] = packed[row : row + L0 // 2, :].astype(F32)
        trend_in_grad[layer, :, LANES:] = packed[
            row + L0 // 2 : row + L0, : TREND_ROWS - LANES
        ].astype(F32)
        row = AT_TREND_OUT + layer * TREND_STEP
        trend_out_grad[layer] = packed[row : row + TREND_ROWS, :L0].astype(F32)
    season_in_grad[...] = packed[AT_SEASON_IN : AT_SEASON_IN + NL * SEASON_ROWS, :L0].astype(F32)
    small = [
        pltpu.make_async_copy(source, target, small_sem.at[k])
        for k, (source, target) in enumerate(zip(refs[9:18], finals))
    ]
    for copy in small:
        copy.start()
    for copy in small + big:
        copy.wait()


def body(groups, n_scale, *args):
    tokens = args[0]
    hidden = args[9].shape[2]
    per_device = tokens.shape[0] // L0
    chunks = max(chunk_counts(per_device))
    unit_rows = 16 * 2 * (groups // 8) * n_scale
    pack_rows = -(-USED_ROWS // unit_rows) * unit_rows
    plane_size = groups // 8 * n_scale
    plane_rows = pack_rows // 2 // plane_size
    anywhere = pl.BlockSpec(memory_space=pl.ANY)
    vmem = pl.BlockSpec(memory_space=pltpu.VMEM)
    dma = pltpu.SemaphoreType.DMA
    turned = (
        args[:5]
        + (jnp.swapaxes(args[5], 0, 1).reshape(NL * SEASON_ROWS, L0),)
        + tuple(jnp.swapaxes(member, 1, 2) for member in args[6:8])
        + (args[8].reshape(NL * TREND_ROWS, L0),)
        + args[9:]
    )
    scratch = [pltpu.VMEM(member.shape, member.dtype) for k, member in enumerate(turned) if k not in (0, 1, 5)]
    scratch += [
        dma((len(turned) - 3,)),
        pltpu.VMEM((chunks, CHUNK, LANES), BF16),
        pltpu.VMEM((chunks, CHUNK, LANES), BF16),
        pltpu.VMEM((chunks, CHUNK, LANES), BF16),
        pltpu.VMEM((chunks, CHUNK, LANES), BF16),
        pltpu.VMEM((chunks, CHUNK, LANES), F32),
        pltpu.VMEM((CHUNK, LANES), F32),
        pltpu.VMEM((CHUNK, LANES), F32),
        pltpu.VMEM((CHUNK, LANES), BF16),
        pltpu.VMEM((CHUNK, hidden), BF16),
        pltpu.VMEM((2, NL, CHUNK, LANES), F32),
        pltpu.VMEM((2, NL, CHUNK, LANES), F32),
        pltpu.VMEM((2, NL, CHUNK, LANES), BF16),
        pltpu.VMEM((2, NL, CHUNK, hidden), BF16),
        pltpu.VMEM((2, NL, CHUNK, hidden), BF16),
        pltpu.VMEM((2, NL, 4, 192, 2 * LANES), BF16),
        pltpu.VMEM((2, NL, 4, 96, 2 * LANES), BF16),
        pltpu.VMEM((2, NL, 4, 96, 2 * LANES), BF16),
        pltpu.VMEM((2, NL, 4, 96, 2 * LANES), BF16),
        pltpu.VMEM((2, NL, 4, 192, 2 * LANES), BF16),
        pltpu.VMEM((2, NL, 4, 192, 2 * LANES), BF16),
        pltpu.VMEM((NL, 3, 96, 192), BF16),
        pltpu.VMEM((NL, 3, 96, 96), BF16),
        pltpu.VMEM((NL, 3, 192, 96), BF16),
        pltpu.VMEM((NL, 3, 192, 192), BF16),
        pltpu.VMEM((NL, 3, 192, 96), BF16),
        pltpu.VMEM((NL, 3, 96, 96), BF16),
        pltpu.VMEM((NL, 3, 96, 192), BF16),
        pltpu.VMEM((NL, 3, 192, 192), BF16),
        pltpu.VMEM((4, 192, 192), BF16),
        pltpu.VMEM((4, 192, 192), BF16),
        pltpu.VMEM((NL, hidden, LANES), BF16),
        pltpu.VMEM((NL, LANES, hidden), BF16),
        pltpu.VMEM((NL, 3, 48, 96), F32),
        pltpu.VMEM((NL, 3, 48, 48), F32),
        pltpu.VMEM((NL, 3, 48, 96), F32),
        pltpu.VMEM((NL, 3, 96, 96), F32),
        pltpu.VMEM((NL, LANES, hidden), F32),
        pltpu.VMEM((NL, LANES, hidden), F32),
        pltpu.VMEM((NL, 8, hidden), F32),
        pltpu.VMEM((NL, 8, LANES), F32),
        pltpu.VMEM((NL, 8, LANES), F32),
        pltpu.VMEM((pack_rows, LANES), F32),
        pltpu.VMEM((pack_rows // 2, LANES), F32),
        pltpu.VMEM((pack_rows, LANES), BF16),
        pltpu.VMEM((plane_size, plane_rows, LANES), BF16),
        pltpu.VMEM((plane_rows, LANES), BF16),
        pltpu.VMEM((plane_rows, LANES), BF16),
        pltpu.VMEM((plane_rows, LANES), BF16),
        pltpu.VMEM((plane_rows, LANES), BF16),
        dma((2,)),
        pltpu.SemaphoreType.REGULAR,
        pltpu.VMEM((2, chunks, 2, SIZES[2], LANES), BF16),
        dma((2, chunks, 2)),
        dma((2, chunks, 2)),
        dma((2, chunks, 8)),
        dma((2, chunks, 4)),
        dma((2, chunks, 4)),
        dma((2, chunks, 8)),
        dma((7, plane_size)),
        dma((7, plane_size)),
        pltpu.VMEM((3, 48, 96), F32),
        pltpu.VMEM((3, 48, 48), F32),
        pltpu.VMEM((3, 48, 96), F32),
        pltpu.VMEM((3, 96, 96), F32),
        pltpu.VMEM((NL, 3, NL * SEASON_ROWS, 48), BF16),
        pltpu.VMEM((NL, 3, L0 // 2, 48), BF16),
        pltpu.VMEM((NL, 3, L0 // 2, 48), BF16),
        pltpu.VMEM((NL, 3, TREND_ROWS, 96), BF16),
        pltpu.VMEM((3, 96, LANES), BF16),
        pltpu.VMEM((3, 48, LANES), BF16),
        pltpu.VMEM((3, 96, 2 * LANES), BF16),
        pltpu.VMEM((3, 96, LANES), BF16),
    ]
    mixed_out, input_grad, packed = pl.pallas_call(
        functools.partial(kernel_body, groups, n_scale, per_device, pack_rows),
        out_shape=[
            pltpu.VMEM(tokens.shape, BF16),
            pltpu.VMEM(tokens.shape, BF16),
            pltpu.VMEM((pack_rows, LANES), BF16),
        ],
        in_specs=[vmem if k == 5 else anywhere for k in range(len(turned))],
        out_specs=[vmem, vmem, vmem],
        scratch_shapes=scratch,
        compiler_params=pltpu.CompilerParams(
            collective_id=0, has_side_effects=True, vmem_limit_bytes=58 << 20
        ),
    )(*turned)
    finals = [
        jax.ShapeDtypeStruct(shape, F32)
        for shape in (
            (NL, LANES),
            (NL, LANES),
            (NL * SEASON_ROWS, L0),
            (NL, L0 // 2, SEASON_ROWS),
            (NL, L0 // 2, TREND_ROWS),
            (NL, TREND_ROWS, L0),
            (NL, LANES, hidden),
            (NL, hidden),
            (NL, hidden, LANES),
        )
    ]
    outs = pl.pallas_call(
        unpack_body,
        out_shape=[
            jax.ShapeDtypeStruct(tokens.shape, BF16),
            jax.ShapeDtypeStruct(tokens.shape, BF16),
            *finals,
        ],
        in_specs=[vmem] * 3,
        out_specs=[anywhere] * 11,
        scratch_shapes=[pltpu.VMEM(member.shape, F32) for member in finals]
        + [dma((len(finals),)), dma((2, PIECES))],
        compiler_params=pltpu.CompilerParams(vmem_limit_bytes=16 << 20),
    )(*(pltpu.with_memory_space_constraint(member, pltpu.VMEM) for member in (mixed_out, input_grad, packed)))
    return (
        *outs[:4],
        jnp.swapaxes(outs[4].reshape(SEASON_ROWS, NL, L0), 0, 1),
        jnp.swapaxes(outs[5], 1, 2),
        jnp.swapaxes(outs[6], 1, 2),
        *outs[7:],
    )


def solution(mesh):
    rows = P(("scale", "dp"), None)
    return jax.shard_map(
        functools.partial(body, mesh.shape["dp"], mesh.shape["scale"]),
        mesh=mesh,
        in_specs=(rows, rows, P("scale", None)) + (P(),) * 9,
        out_specs=(rows, rows) + (P(),) * 9,
        check_vma=False,
    )
```

```python
import functools

import jax
import jax.numpy as jnp
from jax import lax
from jax.experimental import pallas as pl
from jax.experimental.pallas import tpu as pltpu
from jax.sharding import PartitionSpec as P

L0 = 96
KERNEL = 25
NL = 2
SEASON_ROWS = 84
TREND_ROWS = 168
EPS = 1e-05
LANES = 128
ITEMS = 8
PAIR = 4
MESH = pl.DeviceIdType.MESH
F32 = jnp.float32
BF16 = jnp.bfloat16

LENGTHS = [L0 >> i for i in range(4)]
SIZES = [ITEMS * n for n in LENGTHS]
STARTS = [sum(SIZES[:i]) for i in range(4)]
CHUNK = sum(SIZES)
SLOTS = [1, 2, 4, 4]
SELF = [(0, 0), (0, 1), (1, 1), (3, 1)]
TILE = 480
SLABS = [(0, 192, 2), (1, 192, 1), (2, 96, 1), (3, 48, 1)]
UNITS = {1: (0, 1), 2: (2,), 3: (3,)}
WEIGHT_COUNT = {1: 2, 2: 4, 3: 4}
GRAD_COUNT = {1: 1, 2: 2, 3: 4}
AT_SEASON_IN = 16
AT_TREND_IN = AT_SEASON_IN + 176
AT_SEASON_OUT = AT_TREND_IN + NL * L0
AT_TREND_OUT = AT_SEASON_OUT + NL * L0 // 2
TREND_STEP = 176
AT_FFN_IN = AT_TREND_OUT + NL * TREND_STEP
AT_FFN_OUT = AT_FFN_IN + NL * 2 * LANES
USED_ROWS = AT_FFN_OUT + NL * 2 * LANES
PIECES = 4
FIRST_STEPS = 3


def dot(a, b):
    return jnp.dot(a, b, preferred_element_type=F32)


def dot_nt(a, b):
    return lax.dot_general(a, b, (((1,), (1,)), ((), ())), preferred_element_type=F32)


def dot_tn(a, b):
    return lax.dot_general(a, b, (((0,), (0,)), ((), ())), preferred_element_type=F32)


def gelu_parts(v):
    cumulative = 0.5 * (1.0 + lax.erf(v * 0.7071067811865476))
    density = jnp.exp(-0.5 * (v * v)) * 0.3989422804014327
    return v * cumulative, cumulative + v * density


def iota(shape, dim):
    return lax.broadcasted_iota(jnp.int32, shape, dim)


def selection(rows, columns, count, length, base, turned=False, stride=1):
    shape = (columns, rows) if turned else (rows, columns)
    r = iota(shape, 1 if turned else 0)
    c = iota(shape, 0 if turned else 1)
    found = jnp.zeros(shape, jnp.bool_)
    for k in range(count):
        near = c == (r - k * length) * stride + base
        found = found | (near & (r >= k * length) & (r < (k + 1) * length))
    return found.astype(F32)


def block_mask(count, height, width, turned=False):
    shape = (count * width, count * height) if turned else (count * height, count * width)
    r = iota(shape, 1 if turned else 0)
    c = iota(shape, 0 if turned else 1)
    found = jnp.zeros(shape, jnp.bool_)
    for k in range(count):
        found = found | (
            (r >= k * height) & (r < (k + 1) * height) & (c >= k * width) & (c < (k + 1) * width)
        )
    return found.astype(F32)


def moving_counts(count, length, turned):
    size = count * length
    t = iota((size, size), 1 if turned else 0)
    u = iota((size, size), 0 if turned else 1)
    total = jnp.zeros((size, size), F32)
    half = (KERNEL - 1) // 2
    for k in range(count):
        low, high = k * length, (k + 1) * length - 1
        inside = (t >= low) & (t <= high) & (u >= low) & (u <= high)
        near = (jnp.abs(t - u) <= half).astype(F32)
        first = jnp.where(u == low, jnp.maximum(half - (t - low), 0), 0).astype(F32)
        last = jnp.where(u == high, jnp.maximum(half - (high - t), 0), 0).astype(F32)
        total = total + jnp.where(inside, near + first + last, 0.0)
    return total


def beside(value, height):
    return jnp.concatenate([value[k : k + height] for k in range(0, value.shape[0], height)], 1)


def drive(threads):
    active = list(threads)
    while active:
        rest = []
        for thread in active:
            if next(thread, None) is not None:
                rest.append(thread)
        active = rest


def fold_rows(value):
    return jnp.sum(value.reshape(-1, 8, value.shape[-1]), 0)


def group_of(groups, scale, slot, position):
    bounds = [0, groups // 2, 3 * groups // 4, 7 * groups // 8]
    offsets = [0, groups // 4, groups // 8, 3 * groups // 8]
    return position - bounds[scale] + offsets[slot]


def home_of(groups, scale, group):
    if scale == 0:
        return group, 0
    if scale == 1:
        return groups // 2 + lax.rem(group, groups // 4), lax.div(group, groups // 4)
    part = lax.div(group, groups // 8)
    slot = jnp.where(part == 1, 2, jnp.where(part == 2, 1, part))
    first = 3 * groups // 4 if scale == 2 else 7 * groups // 8
    return first + lax.rem(group, groups // 8), slot


def chunk_counts(per_device):
    total = per_device // ITEMS
    return total - total // 3, total // 3


def due_results(per_device):
    lower_chunks, upper_chunks = chunk_counts(per_device)

    def at_once(count):
        return {("forward", c): [(0, c)] for c in range(count)} | {("backward", c): [(1, c)] for c in range(count)}

    last, top = lower_chunks - 1, upper_chunks - 1
    return {
        (True, False): {("forward", c + 1): [(0, c)] for c in range(last)}
        | {("backward", c): [(1, c)] for c in range(last)}
        | {("forward", last): [(0, last - 1), (0, last)], ("gathered", 0): [(1, last)]},
        (False, False): at_once(lower_chunks) | {("backward", last): [], ("paired", 0): [(1, last)]},
        (False, True): at_once(upper_chunks) | {("forward", top): [], ("backward", top): [], ("paired", 0): [(0, top), (1, top)]},
        (True, True): {
            ("crossed", 0): [(kind, c) for c in range(upper_chunks) for kind in range(2)][:-1],
            ("gathered", 0): [(1, top)],
        },
    }


def kernel_body(
    groups,
    n_scale,
    per_device,
    pack_rows,
    tokens,
    cotangent,
    item_mask_hbm,
    ln_gain_hbm,
    ln_bias_hbm,
    season_in,
    season_out_hbm,
    trend_in_hbm,
    trend_out_hbm,
    ffn_in_hbm,
    ffn_bias_hbm,
    ffn_out_hbm,
    mixed_out,
    input_grad,
    packed_out,
    item_mask,
    ln_gain,
    ln_bias,
    season_out,
    trend_in,
    trend_out,
    ffn_in,
    ffn_bias,
    ffn_out,
    param_sem,
    tok_buf,
    cot_buf,
    out_buf,
    grad_buf,
    live,
    field,
    grad,
    df_keep,
    da_keep,
    unit_all,
    inverse_all,
    z_keep_all,
    hidden_all,
    slope_all,
    season_src_all,
    trend_src_all,
    season_hid_all,
    season_slope_all,
    trend_hid_all,
    trend_slope_all,
    sa,
    sb,
    ta,
    tb,
    sa_t,
    sb_t,
    ta_t,
    tb_t,
    moving,
    moving_t,
    win_t,
    wout_t,
    d_sa,
    d_sb,
    d_ta,
    d_tb,
    d_win,
    d_wout,
    d_bias,
    d_gain,
    d_off,
    pack,
    half_in,
    half_bf,
    plane_in,
    plane_bf,
    pair_in,
    across_out,
    across_in,
    pad_sem,
    come_down,
    relay_buf,
    relay_send,
    relay_recv,
    in_send,
    in_recv,
    out_send,
    out_recv,
    ar_send,
    ar_recv,
    *pack_refs,
):
    scale_index = lax.axis_index("scale")
    position = lax.axis_index("dp")
    worker_group = lax.rem(position, groups // 2)
    worker_half = lax.div(position, groups // 2)
    upper = position >= groups // 2
    lower_chunks, upper_chunks = chunk_counts(per_device)
    chunks = jnp.where(upper, upper_chunks, lower_chunks)
    bounds = [0, groups // 2, 3 * groups // 4, 7 * groups // 8, groups]

    masks, places, lays = pack_refs[0:4], pack_refs[4:8], pack_refs[8:12]
    params = [
        pltpu.make_async_copy(source, target, param_sem.at[k])
        for k, (source, target) in enumerate(
            (
                (item_mask_hbm, item_mask),
                (ln_gain_hbm, ln_gain),
                (ln_bias_hbm, ln_bias),
                (season_out_hbm, season_out),
                (trend_in_hbm, trend_in),
                (trend_out_hbm, trend_out),
                (ffn_in_hbm, ffn_in),
                (ffn_bias_hbm, ffn_bias),
                (ffn_out_hbm, ffn_out),
            )
        )
    ]

    barrier = pltpu.get_barrier_semaphore()

    plane_dp = groups // 8
    plane_size = plane_dp * n_scale
    core = lax.rem(position, 2)
    place_dp = lax.rem(lax.div(position, 2), plane_dp)
    depth_index = lax.div(position, 2 * plane_dp)

    def greet(device):
        pl.semaphore_signal(barrier, inc=1, device_id=device, device_id_type=MESH)

    def greet_row(k, carry):
        greet((scale_index, lax.rem(position + k, groups)))
        return carry

    def greet_plane(k, carry):
        other = lax.rem(scale_index + 1 + lax.div(k, plane_dp), n_scale)
        greet((other, (depth_index * plane_dp + lax.rem(k, plane_dp)) * 2 + core))
        return carry

    lax.fori_loop(1, groups, greet_row, 0)
    lax.fori_loop(0, (n_scale - 1) * plane_dp, greet_plane, 0)
    pl.semaphore_wait(barrier, groups - 1 + (n_scale - 1) * plane_dp)

    def relayed(scale, slot, half):
        return half == 0 and ((scale == 2 and slot >= 2) or (scale == 3 and slot < 2))

    def inbound(kind, scale, slot, half, chunk):
        source = (tokens, cotangent)[kind]
        target = (tok_buf, cot_buf)[kind]
        length, size = LENGTHS[scale], SIZES[scale]
        first = (slot * per_device + (half * lower_chunks + chunk) * ITEMS) * length
        src = source.at[pl.ds(pl.multiple_of(first, 16), size)]
        dst = target.at[chunk, pl.ds(STARTS[scale], size)]
        recv = in_recv.at[kind, chunk, scale]
        if (slot, half) == SELF[scale]:
            return pltpu.make_async_copy(src, dst, recv), False
        owner = half * (groups // 2) + group_of(groups, scale, slot, position)
        if relayed(scale, slot, half):
            owner = position + (groups // 8 if scale == 2 else -(groups // 8))
            dst = relay_buf.at[kind, chunk, slot % 2, pl.ds(0, size)]
            recv = relay_recv.at[kind, chunk, slot % 2]
        return (
            pltpu.make_async_remote_copy(
                src_ref=src,
                dst_ref=dst,
                send_sem=in_send.at[kind, chunk, slot * 2 + half],
                recv_sem=recv,
                device_id=(scale_index, owner),
                device_id_type=MESH,
            ),
            True,
        )

    def relay(kind, scale, slot, chunk):
        length, size = LENGTHS[scale], SIZES[scale]
        src = relay_buf.at[kind, chunk, slot % 2, pl.ds(0, size)]
        target = (tok_buf, cot_buf)[kind]
        partner = position + (groups // 8 if scale == 3 else -(groups // 8))
        return pltpu.make_async_remote_copy(
            src_ref=src,
            dst_ref=target.at[chunk, pl.ds(STARTS[scale], size)],
            send_sem=relay_send.at[kind, chunk, slot % 2],
            recv_sem=in_recv.at[kind, chunk, scale],
            device_id=(scale_index, group_of(groups, scale, slot, partner)),
            device_id_type=MESH,
        )

    def order(scale):
        moves = [(kind, slot, half) for kind in range(2) for slot in range(SLOTS[scale]) for half in (1, 0)]
        return sorted(moves, key=lambda move: (move[0], not relayed(scale, move[1], move[2])))

    def each_inbound(act, act_relay, low, high):
        for scale in range(4):

            @pl.when((position >= bounds[scale]) & (position < bounds[scale + 1]))
            def _():
                def one_step(step, carry):
                    for kind, slot, half in order(scale):
                        chunk = step - kind

                        @pl.when((chunk >= 0) & (chunk < (upper_chunks if half else lower_chunks)))
                        def _():
                            act(*inbound(kind, scale, slot, half, chunk))

                    if scale >= 2:
                        other = 5 - scale
                        for kind in range(2):
                            chunk = step - kind

                            @pl.when((chunk >= 0) & (chunk < lower_chunks))
                            def _():
                                for slot in range(4):
                                    if relayed(other, slot, 0):
                                        act_relay(relay(kind, other, slot, chunk), kind, slot, chunk)

                    return carry

                lax.fori_loop(low, high, one_step, 0)

    def pass_on(copy, kind, slot, chunk):
        size = SIZES[2 if slot >= 2 else 3]
        ref = relay_buf.at[kind, chunk, slot % 2, pl.ds(0, size)]
        pltpu.make_async_copy(ref, ref, relay_recv.at[kind, chunk, slot % 2]).wait()
        copy.start()

    def inbound_start(low, high):
        each_inbound(lambda copy, remote: copy.start(), pass_on, low, high)

    far = (position < groups // 4) | (position >= bounds[2])
    inbound_start(0, jnp.where(far, FIRST_STEPS, lower_chunks + 1))
    for copy in params:
        copy.start()
    for copy in params:
        copy.wait()

    def inbound_wait(kind, chunk):
        target = (tok_buf, cot_buf)[kind]
        for scale in range(4):
            ref = target.at[chunk, pl.ds(STARTS[scale], SIZES[scale])]
            pltpu.make_async_copy(ref, ref, in_recv.at[kind, chunk, scale]).wait()

    pad_rows = SLOTS[3] * per_device * LENGTHS[3]

    def padding():
        rows = pl.ds(pad_rows, tokens.shape[0] - pad_rows)
        return [
            pltpu.make_async_copy(tokens.at[rows], mixed_out.at[rows], pad_sem.at[0]),
            pltpu.make_async_copy(cotangent.at[rows], input_grad.at[rows], pad_sem.at[1]),
        ]

    @pl.when(position >= bounds[3])
    def _():
        for copy in padding():
            copy.start()

    def outbound(kind, scale, chunk):
        source = (out_buf, grad_buf)[kind]
        target = (mixed_out, input_grad)[kind]
        home, slot = home_of(groups, scale, worker_group)
        length, size = LENGTHS[scale], SIZES[scale]
        first = (slot * per_device + (worker_half * lower_chunks + chunk) * ITEMS) * length
        src = source.at[chunk, pl.ds(STARTS[scale], size)]
        dst = target.at[pl.ds(pl.multiple_of(first, 16), size)]
        recv = out_recv.at[kind, chunk, slot * 2 + worker_half]
        local = pltpu.make_async_copy(src, dst, recv)
        remote = pltpu.make_async_remote_copy(
            src_ref=src,
            dst_ref=dst,
            send_sem=out_send.at[kind, chunk, scale],
            recv_sem=recv,
            device_id=(scale_index, home),
            device_id_type=MESH,
        )
        return home, local, remote

    def outbound_start(kind, chunk):
        for scale in range(4):
            home, local, remote = outbound(kind, scale, chunk)

            @pl.when(home == position)
            def _():
                local.start()

            @pl.when(home != position)
            def _():
                remote.start()

    def results_out(event, chunk):
        for (is_far, is_upper), due in due_results(per_device).items():
            for at, sends in due.items():
                if at[0] == event and sends:

                    @pl.when((far == is_far) & (upper == is_upper) & (chunk == at[1]))
                    def _():
                        for kind, done in sends:
                            outbound_start(kind, done)

    for layer in range(NL):
        for c in (1, 2, 3):
            count = WEIGHT_COUNT[c]
            fine, coarse = LENGTHS[c - 1], LENGTHS[c]
            at_season = L0 - fine
            at_trend = 2 * L0 - 2 * fine
            for whole, normal, turned, height, width, row, column, stride in (
                (season_in[...], sa, sa_t, coarse, fine, NL * at_season + layer, 0, NL),
                (season_out[layer], sb_t, sb, coarse, coarse, 0, at_season, 1),
                (trend_in[layer], ta_t, ta, coarse, fine, 0, at_trend, 1),
                (trend_out[...], tb, tb_t, fine, fine, TREND_ROWS * layer + at_trend, 0, 1),
            ):
                rows = selection(count * height, whole.shape[0], count, height, row, stride=stride)
                columns = selection(count * width, whole.shape[1], count, width, column).astype(BF16)
                tall = dot(rows.astype(BF16), whole).astype(BF16)
                normal[layer, c - 1, : count * height, : count * width] = (
                    dot_nt(tall, columns) * block_mask(count, height, width)
                ).astype(BF16)
                turned[layer, c - 1, : count * width, : count * height] = (
                    dot_nt(columns, tall) * block_mask(count, height, width, True)
                ).astype(BF16)
        eye_in = selection(ffn_in.shape[2], ffn_in.shape[2], 1, ffn_in.shape[2], 0).astype(BF16)
        eye_out = selection(LANES, LANES, 1, LANES, 0).astype(BF16)
        win_t[layer] = dot_nt(eye_in, ffn_in[layer]).astype(BF16)
        wout_t[layer] = dot_nt(eye_out, ffn_out[layer]).astype(BF16)
    for c in (1, 2, 3):
        count = GRAD_COUNT[c]
        fine, coarse = LENGTHS[c - 1], LENGTHS[c]
        at_season = L0 - fine
        at_trend = 2 * L0 - 2 * fine
        for k, (height, width, row, lane, stride) in enumerate(
            (
                (coarse, fine, NL * at_season, 0, NL),
                (coarse, coarse, 0, at_season, 1),
                (coarse, fine, 0, at_trend, 1),
                (fine, fine, at_trend, 0, 1),
            )
        ):
            masks[k][c - 1] = block_mask(count, height, width)
            rows, lanes = places[k].shape[2], lays[k].shape[2]
            for layer in range(NL):
                start = row + layer if stride > 1 else row
                place = selection(count * height, rows, count, height, start, True, stride)
                places[k][layer, c - 1] = place.astype(BF16)
            lays[k][c - 1] = selection(count * width, lanes, count, width, lane).astype(BF16)
    for scale, height, number in SLABS:
        for ref, is_turned in ((moving, False), (moving_t, True)):
            counts = moving_counts(height // LENGTHS[scale], LENGTHS[scale], is_turned)
            ref[scale, :height, :height] = counts.astype(BF16)
    mean_lanes = jnp.full((LANES, LANES), 1.0 / LANES, BF16)

    mask_rows = jnp.broadcast_to(item_mask[...].astype(F32), (LANES, item_mask.shape[1])).astype(BF16)
    first_item = worker_group * per_device + worker_half * lower_chunks * ITEMS
    chosen = iota((32, item_mask.shape[1]), 1) == iota((32, item_mask.shape[1]), 0) + first_item
    item_live = dot_nt(chosen.astype(F32).astype(BF16), mask_rows).astype(BF16)
    for chunk in range(lower_chunks):
        for i in range(4):
            place = (iota((SIZES[i], 32), 0).astype(F32) + 0.5) * (1.0 / LENGTHS[i])
            column = iota((SIZES[i], 32), 1).astype(F32) - float(chunk * ITEMS)
            one = ((place >= column) & (place < column + 1.0)).astype(F32).astype(BF16)
            live[chunk, STARTS[i] : STARTS[i] + SIZES[i], :] = dot(one, item_live)

    for total in (d_sa, d_sb, d_ta, d_tb, d_win, d_wout, d_bias, d_gain, d_off, pack):
        total[...] = jnp.zeros(total.shape, F32)

    taps = 1.0 / KERNEL

    def matrix(ref, layer, c, rows, columns):
        return ref[layer, c - 1, :rows, :columns]

    def sides(scale, height, j):
        half = SIZES[scale] // 2
        return [STARTS[scale] + side * half + j * height for side in range(2)]

    def kept_of(chunk):
        return [
            ref.at[lax.rem(chunk, 2)]
            for ref in (
                unit_all,
                inverse_all,
                z_keep_all,
                hidden_all,
                slope_all,
                season_src_all,
                trend_src_all,
                season_hid_all,
                season_slope_all,
                trend_hid_all,
                trend_slope_all,
            )
        ]

    def forward(layer, chunk, found):
        (
            unit,
            inverse,
            z_keep,
            hidden,
            slope,
            season_src,
            trend_src,
            season_hid,
            season_slope,
            trend_hid,
            trend_slope,
        ) = kept_of(chunk)
        gain = ln_gain[layer : layer + 1, :]
        offset = ln_bias[layer : layer + 1, :]
        offset_pair = jnp.concatenate([offset, offset], 1)
        bias = ffn_bias[layer : layer + 1, :]

        def rows_of(start, height):
            if layer == 0:
                return tok_buf[chunk, start : start + height, :].astype(F32)
            return field[start : start + height, :]

        def norm(scale, height, j):
            while layer > 0 and ("y", layer - 1, scale, j) not in found:
                yield 1
            parts = []
            for start in sides(scale, height, j):
                x = rows_of(start, height)
                centered = x - jnp.mean(x, -1, keepdims=True)
                yield 1
                inv = lax.rsqrt(dot((centered * centered).astype(BF16), mean_lanes) + EPS)
                n = centered * inv
                unit[layer, start : start + height, :] = n
                inverse[layer, start : start + height, :] = inv
                parts.append(n * gain)
                yield 1
            both = jnp.concatenate(parts, 1)
            average = dot(moving[scale, :height, :height], both.astype(BF16)) * taps
            found["n", layer, scale, j] = both + offset_pair
            found["s", layer, scale, j] = both - average
            found["t", layer, scale, j] = average + offset_pair

        def mixed(source, first, second, kept, hid, slp, u, layer_at, c, fine_to_coarse):
            a = source.astype(BF16)
            rows_in = a.shape[0]
            rows_out = rows_in // 2 if fine_to_coarse else rows_in * 2
            kept[layer_at, u, :rows_in, :] = a
            p = dot(matrix(first, layer_at, c, rows_out, rows_in), a)
            yield None
            h, slope_value = gelu_parts(p)
            h = h.astype(BF16)
            hid[layer_at, u, :rows_out, :] = h
            slp[layer_at, u, :rows_out, :] = slope_value.astype(BF16)
            yield None
            yield dot(matrix(second, layer_at, c, rows_out, rows_out), h)

        def season(c):
            results = []
            for j, u in enumerate(UNITS[c]):
                while ("S", layer, c - 1, j) not in found and not (
                    c == 1 and ("s", layer, 0, j) in found
                ):
                    yield 1
                source = found["s", layer, 0, j] if c == 1 else found["S", layer, c - 1, j]
                for value in mixed(
                    source, sa, sb, season_src, season_hid, season_slope, u, layer, c, True
                ):
                    if value is None:
                        yield 1
                    else:
                        results.append(value)
            mix = results[0] if len(results) == 1 else jnp.concatenate(results, 0)
            found["sm", layer, c, 0] = mix
            while ("s", layer, c, 0) not in found:
                yield 1
            found["S", layer, c, 0] = found["s", layer, c, 0] + mix

        def trend(c):
            while ("t" if c == 3 else "T", layer, c, 0) not in found:
                yield 1
            source = found["t" if c == 3 else "T", layer, c, 0]
            for j, u in enumerate(UNITS[c]):
                part = source[96 * j : 96 * (j + 1)] if c == 1 else source
                for value in mixed(part, ta, tb, trend_src, trend_hid, trend_slope, u, layer, c, False):
                    if value is None:
                        yield 1
                    else:
                        found["tm", layer, c - 1, j] = value
            if c > 1:
                while ("t", layer, c - 1, 0) not in found:
                    yield 1
                found["T", layer, c - 1, 0] = found["t", layer, c - 1, 0] + found["tm", layer, c - 1, 0]

        def ffn(scale, height, j):
            needed = [("n", layer, scale, j)]
            if scale > 0:
                needed.append(("sm", layer, scale, j))
            if scale < 3:
                needed.append(("tm", layer, scale, j))
            while not all(key in found for key in needed):
                yield 1
            value = found[needed[0]]
            for key in needed[1:]:
                value = value + found[key]
            value = value.astype(BF16)
            starts = sides(scale, height, j)
            halves = [value[:, :LANES], value[:, LANES:]]
            for start, z in zip(starts, halves):
                z_keep[layer, start : start + height, :] = z
            a = dot(jnp.concatenate(halves, 0), ffn_in[layer]) + bias
            yield 1
            h, slope_value = gelu_parts(a)
            h = h.astype(BF16)
            slope_value = slope_value.astype(BF16)
            for k, start in enumerate(starts):
                hidden[layer, start : start + height, :] = h[k * height : (k + 1) * height]
                slope[layer, start : start + height, :] = slope_value[k * height : (k + 1) * height]
            yield 1
            f = dot(h, ffn_out[layer])
            yield 1
            for k, start in enumerate(starts):
                y = rows_of(start, height) + live[chunk, start : start + height, :] * f[
                    k * height : (k + 1) * height
                ]
                if layer == NL - 1:
                    out_buf[chunk, start : start + height, :] = y.astype(BF16)
                else:
                    field[start : start + height, :] = y
            found["y", layer, scale, j] = True

        for scale, height, number in reversed(SLABS):
            for j in range(number):
                yield norm(scale, height, j)
        for c in (3, 2, 1):
            yield trend(c)
        for c in (1, 2, 3):
            yield season(c)
        for scale, height, number in (SLABS[1], SLABS[2], SLABS[0], SLABS[3]):
            for j in range(number):
                yield ffn(scale, height, j)

    def backward(layer, chunk, found):
        (
            unit,
            inverse,
            z_keep,
            hidden,
            slope,
            season_src,
            trend_src,
            season_hid,
            season_slope,
            trend_hid,
            trend_slope,
        ) = kept_of(chunk)
        gain = ln_gain[layer : layer + 1, :]

        def rows_of(start, height):
            if layer == NL - 1:
                return cot_buf[chunk, start : start + height, :].astype(F32)
            return grad[start : start + height, :]

        def ffn(scale, height, j):
            while layer < NL - 1 and ("x", layer + 1, scale, j) not in found:
                yield 1
            starts = sides(scale, height, j)
            parts = []
            for start in starts:
                df = (live[chunk, start : start + height, :] * rows_of(start, height)).astype(BF16)
                df_keep[start : start + height, :] = df
                parts.append(df)
            dh = dot(jnp.concatenate(parts, 0), wout_t[layer])
            yield 1
            parts = []
            for k, start in enumerate(starts):
                da = dh[k * height : (k + 1) * height] * slope[layer, start : start + height, :].astype(F32)
                d_bias[layer] += fold_rows(da)
                da = da.astype(BF16)
                da_keep[start : start + height, :] = da
                parts.append(da)
            yield 1
            dz = dot(jnp.concatenate(parts, 0), win_t[layer])
            found["dz", layer, scale, j] = jnp.concatenate([dz[:height], dz[height:]], 1)

        def weight_grads():
            while not all(("dz", layer, scale, j) in found for scale, _, number in SLABS for j in range(number)):
                yield 1
            for t in range(0, CHUNK, TILE):
                d_win[layer] += dot_tn(z_keep[layer, t : t + TILE, :], da_keep[t : t + TILE, :])
                yield 1
                d_wout[layer] += dot_tn(df_keep[t : t + TILE, :], hidden[layer, t : t + TILE, :])
                yield 1

        def mixed(g, first_t, second_t, slp, u, c, fine_to_coarse):
            rows = g.shape[0]
            rows_out = rows * 2 if fine_to_coarse else rows // 2
            dh = dot(matrix(second_t, layer, c, rows, rows), g)
            yield None
            dp = (dh * slp[layer, u, :rows, :].astype(F32)).astype(BF16)
            yield dp
            yield dot(matrix(first_t, layer, c, rows_out, rows), dp)

        def trend(c):
            results, gs, dps = [], [], []
            for j, u in enumerate(UNITS[c]):
                key = ("dz", layer, 0, j) if c == 1 else ("dT", layer, c - 1, 0)
                while key not in found:
                    yield 1
                g = found[key].astype(BF16)
                gs.append(beside(g, 96))
                steps = []
                for value in mixed(g, ta_t, tb_t, trend_slope, u, c, False):
                    if value is not None:
                        steps.append(value)
                    yield 1
                dps.append(beside(steps[0], 96))
                results.append(steps[1])
            total = results[0] if len(results) == 1 else jnp.concatenate(results, 0)
            found["gT", layer, c, 0] = total
            while ("dz", layer, c, 0) not in found:
                yield 1
            found["dT", layer, c, 0] = found["dz", layer, c, 0] + total
            rows = 48 if c == 3 else 96
            kept = [beside(trend_hid[layer, u, : 2 * rows, :], 96) for u in UNITS[c]]
            d_tb[layer, c - 1] += dot_nt(jnp.concatenate(gs, 1), jnp.concatenate(kept, 1))
            yield 1
            kept = [beside(trend_src[layer, u, :rows, :], 48) for u in UNITS[c]]
            d_ta[layer, c - 1] += dot_nt(jnp.concatenate(kept, 1), jnp.concatenate(dps, 1))

        def season(c):
            key = ("dz", layer, 3, 0) if c == 3 else ("dS", layer, c, 0)
            while key not in found:
                yield 1
            gs, dps = [], []
            for j, u in enumerate(UNITS[c]):
                g = found[key].astype(BF16)
                if c == 1:
                    g = g[96 * j : 96 * (j + 1)]
                gs.append(beside(g, 48))
                steps = []
                for value in mixed(g, sa_t, sb_t, season_slope, u, c, True):
                    if value is not None:
                        steps.append(value)
                    yield 1
                dps.append(beside(steps[0], 48))
                found["gS", layer, c - 1, j] = steps[1]
            if c > 1:
                while ("dz", layer, c - 1, 0) not in found:
                    yield 1
                found["dS", layer, c - 1, 0] = found["dz", layer, c - 1, 0] + found["gS", layer, c - 1, 0]
            rows = 48 if c == 3 else 96
            kept = [beside(season_hid[layer, u, :rows, :], 48) for u in UNITS[c]]
            d_sb[layer, c - 1] += dot_nt(jnp.concatenate(kept, 1), jnp.concatenate(gs, 1))
            yield 1
            kept = [beside(season_src[layer, u, : 2 * rows, :], 96) for u in UNITS[c]]
            d_sa[layer, c - 1] += dot_nt(jnp.concatenate(dps, 1), jnp.concatenate(kept, 1))

        def norm(scale, height, j):
            needed = [("dz", layer, scale, j)]
            if scale < 3:
                needed.append(("gS", layer, scale, j))
            if scale > 0:
                needed.append(("gT", layer, scale, j))
            while not all(key in found for key in needed):
                yield 1
            value = found[needed[0]]
            if scale == 0:
                moved = -found[needed[1]]
                value = value + found[needed[1]]
            elif scale == 3:
                moved = found[needed[1]]
            else:
                moved = found[needed[2]] - found[needed[1]]
                value = value + found[needed[1]]
            value = value + dot(moving_t[scale, :height, :height], moved.astype(BF16)) * taps
            yield 1
            for side, start in enumerate(sides(scale, height, j)):
                d = value[:, side * LANES : (side + 1) * LANES]
                n = unit[layer, start : start + height, :]
                dn = d * n
                d_gain[layer] += fold_rows(dn)
                d_off[layer] += fold_rows(d)
                q = d * gain
                qn = dn * gain
                mean_q = dot(q.astype(BF16), mean_lanes)
                mean_qn = dot(qn.astype(BF16), mean_lanes)
                yield 1
                x = rows_of(start, height) + inverse[layer, start : start + height, :] * (
                    q - mean_q - n * mean_qn
                )
                if layer == 0:
                    grad_buf[chunk, start : start + height, :] = x.astype(BF16)
                else:
                    grad[start : start + height, :] = x
                yield 1
            found["x", layer, scale, j] = True

        for scale, height, number in (SLABS[0], SLABS[3], SLABS[1], SLABS[2]):
            for j in range(number):
                yield ffn(scale, height, j)
        for c in (1, 2, 3):
            yield trend(c)
        for c in (3, 2, 1):
            yield season(c)
        for scale, height, number in reversed(SLABS):
            for j in range(number):
                yield norm(scale, height, j)
        yield weight_grads()

    def one_step(step, carry):
        @pl.when(step < chunks)
        def _():
            inbound_wait(0, step)
            found = {}
            drive([thread for layer in range(NL) for thread in forward(layer, step, found)])
            later = step + FIRST_STEPS
            inbound_start(later, jnp.where(far & (later <= lower_chunks), later + 1, later))
            results_out("forward", step)

        @pl.when(step > 0)
        def _():
            chunk = step - 1
            inbound_wait(1, chunk)

            @pl.when(jnp.logical_not(upper | far) & (chunk == lower_chunks - 1))
            def _():
                pl.semaphore_signal(
                    come_down,
                    inc=1,
                    device_id=(scale_index, position + groups // 2),
                    device_id_type=MESH,
                )

            found = {}
            drive([thread for layer in reversed(range(NL)) for thread in backward(layer, chunk, found)])
            results_out("backward", chunk)

        return carry

    lax.fori_loop(0, chunks + 1, one_step, 0)
    rest = chunks + FIRST_STEPS
    inbound_start(rest, jnp.where(far & upper, lower_chunks + 1, rest))

    for layer in range(NL):
        parts = [None] * 4
        for c in (1, 2, 3):
            for k, value in enumerate((d_sa, d_sb, d_ta, d_tb)):
                masked = (value[layer, c - 1] * masks[k][c - 1]).astype(BF16)
                found = dot(dot(places[k][layer, c - 1], masked).astype(BF16), lays[k][c - 1])
                parts[k] = found if parts[k] is None else parts[k] + found
        pack[layer : layer + 1, :] = jnp.sum(d_gain[layer], 0, keepdims=True)
        pack[NL + layer : NL + layer + 1, :] = jnp.sum(d_off[layer], 0, keepdims=True)
        bias_sum = jnp.sum(d_bias[layer], 0, keepdims=True)
        pack[AT_SEASON_IN : AT_SEASON_IN + NL * SEASON_ROWS, :] += parts[0]
        row = AT_SEASON_OUT + layer * L0 // 2
        pack[row : row + L0 // 2, :] = parts[1]
        row = AT_TREND_OUT + layer * TREND_STEP
        pack[row : row + TREND_ROWS, :] = parts[3]
        for side in range(2):
            lanes = slice(side * LANES, (side + 1) * LANES)
            row = 2 * NL + 2 * layer + side
            pack[row : row + 1, :] = bias_sum[:, lanes]
            row = AT_TREND_IN + layer * L0 + side * L0 // 2
            pack[row : row + L0 // 2, :] = parts[2][:, lanes]
            row = AT_FFN_IN + (2 * layer + side) * LANES
            pack[row : row + LANES, :] = d_win[layer, :, lanes]
            row = AT_FFN_OUT + (2 * layer + side) * LANES
            pack[row : row + LANES, :] = d_wout[layer, :, lanes].T

    plane_index = scale_index * plane_dp + place_dp
    half_rows = pack_rows // 2
    plane_rows = half_rows // plane_size

    def core_id():
        return (scale_index, position + 1 - 2 * core)

    def plane_id(index):
        return (
            lax.div(index, plane_dp),
            depth_index * (2 * plane_dp) + lax.rem(index, plane_dp) * 2 + core,
        )

    def depth_id(index):
        return (scale_index, index * (2 * plane_dp) + place_dp * 2 + core)

    def remote(src, dst, stage, slot_out, slot_in, device):
        return pltpu.make_async_remote_copy(
            src_ref=src,
            dst_ref=dst,
            send_sem=ar_send.at[stage, slot_out],
            recv_sem=ar_recv.at[stage, slot_in],
            device_id=device,
            device_id_type=MESH,
        )

    def arrived(ref, stage, slot):
        pltpu.make_async_copy(ref, ref, ar_recv.at[stage, slot]).wait()

    mine = pl.multiple_of(core * half_rows, 16)
    theirs = pl.multiple_of((1 - core) * half_rows, 16)
    first_copy = remote(pack.at[pl.ds(theirs, half_rows)], half_in, 0, 0, 0, core_id())
    first_copy.start()
    results_out("packed", 0)
    first_copy.wait_send()
    arrived(half_in, 0, 0)
    half_bf[pl.ds(mine, half_rows)] = (pack[pl.ds(mine, half_rows)] + half_in[...]).astype(BF16)

    def plane_piece(index):
        return pl.ds(pl.multiple_of(mine + index * plane_rows, 16), plane_rows)

    def plane_round(act):
        def one(k, carry):
            other = lax.rem(plane_index + k, plane_size)
            back = lax.rem(plane_index + plane_size - k, plane_size)
            act(other, back, k)
            return carry

        lax.fori_loop(1, plane_size, one, 0)

    def plane_scatter(other, back, k):
        remote(half_bf.at[plane_piece(other)], plane_in.at[k], 1, k, k, plane_id(other)).start()

    plane_round(plane_scatter)
    results_out("planed", 0)
    plane_sum = pack[plane_piece(plane_index)] + half_in[
        pl.ds(pl.multiple_of(plane_index * plane_rows, 16), plane_rows)
    ]

    def plane_wait(k, carry):
        remote(half_bf.at[plane_piece(0)], plane_in.at[k], 1, k, k, core_id()).wait_send()
        arrived(plane_in.at[k], 1, k)
        return carry

    lax.fori_loop(1, plane_size, plane_wait, 0)
    for k in range(1, plane_size):
        plane_sum = plane_sum + plane_in[k].astype(F32)
    plane_bf[...] = plane_sum.astype(BF16)

    outer = jnp.where(depth_index < 2, 0, 3)
    inner = jnp.where(depth_index < 2, 1, 2)
    own_plane = plane_piece(plane_index)
    give = remote(plane_bf, pair_in, 2, 0, 0, depth_id(outer))
    across = remote(across_out, across_in, 3, 0, 0, depth_id(3 - outer))
    back = remote(packed_out.at[own_plane], packed_out.at[own_plane], 4, 0, 0, depth_id(inner))

    @pl.when(depth_index == inner)
    def _():
        give.start()

    results_out("paired", 0)

    @pl.when(depth_index == inner)
    def _():
        give.wait_send()
        arrived(packed_out.at[own_plane], 4, 0)

    @pl.when(depth_index == outer)
    def _():
        arrived(pair_in, 2, 0)
        across_out[...] = (plane_bf[...].astype(F32) + pair_in[...].astype(F32)).astype(BF16)
        across.start()

    @pl.when(far & upper)
    def _():
        pl.semaphore_wait(come_down, 1)

    results_out("crossed", 0)

    @pl.when(depth_index == outer)
    def _():
        across.wait_send()
        arrived(across_in, 3, 0)
        packed_out[own_plane] = (across_out[...].astype(F32) + across_in[...].astype(F32)).astype(BF16)
        back.start()

    results_out("gathered", 0)

    @pl.when(depth_index == outer)
    def _():
        back.wait_send()


    def plane_gather(other, back, k):
        remote(packed_out.at[own_plane], packed_out.at[own_plane], 5, k, k, plane_id(other)).start()

    plane_round(plane_gather)

    def plane_gathered(other, back, k):
        remote(packed_out.at[own_plane], packed_out.at[own_plane], 5, k, k, core_id()).wait_send()
        arrived(packed_out.at[plane_piece(back)], 5, k)

    plane_round(plane_gathered)
    own_half = pl.ds(mine, half_rows)
    last_copy = remote(packed_out.at[own_half], packed_out.at[own_half], 6, 0, 0, core_id())
    last_copy.start()
    last_copy.wait_send()
    arrived(packed_out.at[pl.ds(theirs, half_rows)], 6, 0)

    @pl.when(position >= bounds[3])
    def _():
        for copy in padding():
            copy.wait()

    def sent(copy, remote_copy):
        if remote_copy:
            copy.wait_send()

    each_inbound(sent, lambda copy, kind, slot, chunk: copy.wait_send(), 0, lower_chunks + 1)

    def finish(chunk, carry):
        for kind in range(2):
            for scale in range(4):
                home, local, remote_copy = outbound(kind, scale, chunk)

                @pl.when((home != position) & (chunk < chunks))
                def _():
                    remote_copy.wait_send()

            for scale in range(4):

                @pl.when((position >= bounds[scale]) & (position < bounds[scale + 1]))
                def _():
                    for slot in range(SLOTS[scale]):
                        for half in range(2):

                            @pl.when(chunk < (upper_chunks if half else lower_chunks))
                            def _():
                                place = half * lower_chunks + chunk
                                first = (slot * per_device + place * ITEMS) * LENGTHS[scale]
                                ref = (mixed_out, input_grad)[kind].at[
                                    pl.ds(pl.multiple_of(first, 16), SIZES[scale])
                                ]
                                sem = out_recv.at[kind, chunk, slot * 2 + half]
                                pltpu.make_async_copy(ref, ref, sem).wait()

        return carry

    lax.fori_loop(0, lower_chunks, finish, 0)


def unpack_body(mixed, grad, packed, mixed_out, input_grad, *refs):
    finals, small_sem, big_sem = refs[:9], refs[18], refs[19]
    (
        gain_grad,
        bias_grad,
        season_in_grad,
        season_out_grad,
        trend_in_grad,
        trend_out_grad,
        ffn_in_grad,
        ffn_bias_grad,
        ffn_out_grad,
    ) = refs[9:18]
    size = mixed.shape[0] // PIECES
    big = []
    for kind, (source, target) in enumerate(((mixed, mixed_out), (grad, input_grad))):
        for k in range(PIECES):
            rows = pl.ds(k * size, size)
            big.append(pltpu.make_async_copy(source.at[rows], target.at[rows], big_sem.at[kind, k]))
    for copy in big:
        copy.start()
    top = packed[0:16, :].astype(F32)
    gain_grad[...] = top[0:NL]
    bias_grad[...] = top[NL : 2 * NL]
    for layer in range(NL):
        for side in range(2):
            lanes = slice(side * LANES, (side + 1) * LANES)
            row = 2 * NL + 2 * layer + side
            ffn_bias_grad[layer : layer + 1, lanes] = top[row : row + 1]
            row = AT_FFN_IN + (2 * layer + side) * LANES
            ffn_in_grad[layer, :, lanes] = packed[row : row + LANES, :].astype(F32)
            row = AT_FFN_OUT + (2 * layer + side) * LANES
            ffn_out_grad[layer, side * LANES : (side + 1) * LANES, :] = packed[row : row + LANES, :].astype(F32)
        row = AT_SEASON_OUT + layer * L0 // 2
        season_out_grad[layer] = packed[row : row + L0 // 2, :SEASON_ROWS].astype(F32)
        row = AT_TREND_IN + layer * L0
        trend_in_grad[layer, :, :LANES] = packed[row : row + L0 // 2, :].astype(F32)
        trend_in_grad[layer, :, LANES:] = packed[
            row + L0 // 2 : row + L0, : TREND_ROWS - LANES
        ].astype(F32)
        row = AT_TREND_OUT + layer * TREND_STEP
        trend_out_grad[layer] = packed[row : row + TREND_ROWS, :L0].astype(F32)
    season_in_grad[...] = packed[AT_SEASON_IN : AT_SEASON_IN + NL * SEASON_ROWS, :L0].astype(F32)
    small = [
        pltpu.make_async_copy(source, target, small_sem.at[k])
        for k, (source, target) in enumerate(zip(refs[9:18], finals))
    ]
    for copy in small:
        copy.start()
    for copy in small + big:
        copy.wait()


def body(groups, n_scale, *args):
    tokens = args[0]
    hidden = args[9].shape[2]
    per_device = tokens.shape[0] // L0
    chunks = max(chunk_counts(per_device))
    unit_rows = 16 * 2 * (groups // 8) * n_scale
    pack_rows = -(-USED_ROWS // unit_rows) * unit_rows
    plane_size = groups // 8 * n_scale
    plane_rows = pack_rows // 2 // plane_size
    anywhere = pl.BlockSpec(memory_space=pl.ANY)
    vmem = pl.BlockSpec(memory_space=pltpu.VMEM)
    dma = pltpu.SemaphoreType.DMA
    turned = (
        args[:5]
        + (jnp.swapaxes(args[5], 0, 1).reshape(NL * SEASON_ROWS, L0),)
        + tuple(jnp.swapaxes(member, 1, 2) for member in args[6:8])
        + (args[8].reshape(NL * TREND_ROWS, L0),)
        + args[9:]
    )
    scratch = [pltpu.VMEM(member.shape, member.dtype) for k, member in enumerate(turned) if k not in (0, 1, 5)]
    scratch += [
        dma((len(turned) - 3,)),
        pltpu.VMEM((chunks, CHUNK, LANES), BF16),
        pltpu.VMEM((chunks, CHUNK, LANES), BF16),
        pltpu.VMEM((chunks, CHUNK, LANES), BF16),
        pltpu.VMEM((chunks, CHUNK, LANES), BF16),
        pltpu.VMEM((chunks, CHUNK, LANES), F32),
        pltpu.VMEM((CHUNK, LANES), F32),
        pltpu.VMEM((CHUNK, LANES), F32),
        pltpu.VMEM((CHUNK, LANES), BF16),
        pltpu.VMEM((CHUNK, hidden), BF16),
        pltpu.VMEM((2, NL, CHUNK, LANES), F32),
        pltpu.VMEM((2, NL, CHUNK, LANES), F32),
        pltpu.VMEM((2, NL, CHUNK, LANES), BF16),
        pltpu.VMEM((2, NL, CHUNK, hidden), BF16),
        pltpu.VMEM((2, NL, CHUNK, hidden), BF16),
        pltpu.VMEM((2, NL, 4, 192, 2 * LANES), BF16),
        pltpu.VMEM((2, NL, 4, 96, 2 * LANES), BF16),
        pltpu.VMEM((2, NL, 4, 96, 2 * LANES), BF16),
        pltpu.VMEM((2, NL, 4, 96, 2 * LANES), BF16),
        pltpu.VMEM((2, NL, 4, 192, 2 * LANES), BF16),
        pltpu.VMEM((2, NL, 4, 192, 2 * LANES), BF16),
        pltpu.VMEM((NL, 3, 96, 192), BF16),
        pltpu.VMEM((NL, 3, 96, 96), BF16),
        pltpu.VMEM((NL, 3, 192, 96), BF16),
        pltpu.VMEM((NL, 3, 192, 192), BF16),
        pltpu.VMEM((NL, 3, 192, 96), BF16),
        pltpu.VMEM((NL, 3, 96, 96), BF16),
        pltpu.VMEM((NL, 3, 96, 192), BF16),
        pltpu.VMEM((NL, 3, 192, 192), BF16),
        pltpu.VMEM((4, 192, 192), BF16),
        pltpu.VMEM((4, 192, 192), BF16),
        pltpu.VMEM((NL, hidden, LANES), BF16),
        pltpu.VMEM((NL, LANES, hidden), BF16),
        pltpu.VMEM((NL, 3, 48, 96), F32),
        pltpu.VMEM((NL, 3, 48, 48), F32),
        pltpu.VMEM((NL, 3, 48, 96), F32),
        pltpu.VMEM((NL, 3, 96, 96), F32),
        pltpu.VMEM((NL, LANES, hidden), F32),
        pltpu.VMEM((NL, LANES, hidden), F32),
        pltpu.VMEM((NL, 8, hidden), F32),
        pltpu.VMEM((NL, 8, LANES), F32),
        pltpu.VMEM((NL, 8, LANES), F32),
        pltpu.VMEM((pack_rows, LANES), F32),
        pltpu.VMEM((pack_rows // 2, LANES), F32),
        pltpu.VMEM((pack_rows, LANES), BF16),
        pltpu.VMEM((plane_size, plane_rows, LANES), BF16),
        pltpu.VMEM((plane_rows, LANES), BF16),
        pltpu.VMEM((plane_rows, LANES), BF16),
        pltpu.VMEM((plane_rows, LANES), BF16),
        pltpu.VMEM((plane_rows, LANES), BF16),
        dma((2,)),
        pltpu.SemaphoreType.REGULAR,
        pltpu.VMEM((2, chunks, 2, SIZES[2], LANES), BF16),
        dma((2, chunks, 2)),
        dma((2, chunks, 2)),
        dma((2, chunks, 8)),
        dma((2, chunks, 4)),
        dma((2, chunks, 4)),
        dma((2, chunks, 8)),
        dma((7, plane_size)),
        dma((7, plane_size)),
        pltpu.VMEM((3, 48, 96), F32),
        pltpu.VMEM((3, 48, 48), F32),
        pltpu.VMEM((3, 48, 96), F32),
        pltpu.VMEM((3, 96, 96), F32),
        pltpu.VMEM((NL, 3, NL * SEASON_ROWS, 48), BF16),
        pltpu.VMEM((NL, 3, L0 // 2, 48), BF16),
        pltpu.VMEM((NL, 3, L0 // 2, 48), BF16),
        pltpu.VMEM((NL, 3, TREND_ROWS, 96), BF16),
        pltpu.VMEM((3, 96, LANES), BF16),
        pltpu.VMEM((3, 48, LANES), BF16),
        pltpu.VMEM((3, 96, 2 * LANES), BF16),
        pltpu.VMEM((3, 96, LANES), BF16),
    ]
    mixed_out, input_grad, packed = pl.pallas_call(
        functools.partial(kernel_body, groups, n_scale, per_device, pack_rows),
        out_shape=[
            pltpu.VMEM(tokens.shape, BF16),
            pltpu.VMEM(tokens.shape, BF16),
            pltpu.VMEM((pack_rows, LANES), BF16),
        ],
        in_specs=[vmem if k == 5 else anywhere for k in range(len(turned))],
        out_specs=[vmem, vmem, vmem],
        scratch_shapes=scratch,
        compiler_params=pltpu.CompilerParams(
            collective_id=0, has_side_effects=True, vmem_limit_bytes=58 << 20
        ),
    )(*turned)
    finals = [
        jax.ShapeDtypeStruct(shape, F32)
        for shape in (
            (NL, LANES),
            (NL, LANES),
            (NL * SEASON_ROWS, L0),
            (NL, L0 // 2, SEASON_ROWS),
            (NL, L0 // 2, TREND_ROWS),
            (NL, TREND_ROWS, L0),
            (NL, LANES, hidden),
            (NL, hidden),
            (NL, hidden, LANES),
        )
    ]
    outs = pl.pallas_call(
        unpack_body,
        out_shape=[
            jax.ShapeDtypeStruct(tokens.shape, BF16),
            jax.ShapeDtypeStruct(tokens.shape, BF16),
            *finals,
        ],
        in_specs=[vmem] * 3,
        out_specs=[anywhere] * 11,
        scratch_shapes=[pltpu.VMEM(member.shape, F32) for member in finals]
        + [dma((len(finals),)), dma((2, PIECES))],
        compiler_params=pltpu.CompilerParams(vmem_limit_bytes=16 << 20),
    )(*(pltpu.with_memory_space_constraint(member, pltpu.VMEM) for member in (mixed_out, input_grad, packed)))
    return (
        *outs[:4],
        jnp.swapaxes(outs[4].reshape(SEASON_ROWS, NL, L0), 0, 1),
        jnp.swapaxes(outs[5], 1, 2),
        jnp.swapaxes(outs[6], 1, 2),
        *outs[7:],
    )


def solution(mesh):
    rows = P(("scale", "dp"), None)
    return jax.shard_map(
        functools.partial(body, mesh.shape["dp"], mesh.shape["scale"]),
        mesh=mesh,
        in_specs=(rows, rows, P("scale", None)) + (P(),) * 9,
        out_specs=(rows, rows) + (P(),) * 9,
        check_vma=False,
    )
```
